32 devices in a mesh: rep: 4 (over y, x), shard: 8 (over z, core).
Axes of the slice: x: 2, y: 2, z: 4, core: 2. Of those that a mesh axis runs over, the one named last changes fastest.
Arguments:
- tokens: bfloat16 [16384, 1024], P(('rep', 'shard')), may hold values from -6 to 6
- cotangent: float32 [16384, 1024], P(('rep', 'shard')), may hold values from -6 to 6
- positions: int32 [16384], P(('rep', 'shard')), may hold values from -1 to 511, as said below
- qkv_master: float32 [1024, 3072], P('shard'), may hold values from -0.1875 to 0.1875
- qkv_first: float32 [1024, 3072], P('shard'), may hold values from -64 to 64
- qkv_second: float32 [1024, 3072], P('shard'), may hold values from 647.168 to 2588.672
- out_master: float32 [1024, 1024], P('shard'), may hold values from -1 to 1
- out_first: float32 [1024, 1024], P('shard'), may hold values from -7 to 7
- out_second: float32 [1024, 1024], P('shard'), may hold values from 6.47168 to 25.88672
- fc1_master: float32 [1024, 4096], P('shard'), may hold values from -0.1875 to 0.1875
- fc1_first: float32 [1024, 4096], P('shard'), may hold values from -20 to 20
- fc1_second: float32 [1024, 4096], P('shard'), may hold values from 58.1632 to 232.6528
- fc2_master: float32 [4096, 1024], P('shard'), may hold values from -0.09375 to 0.09375
- fc2_first: float32 [4096, 1024], P('shard'), may hold values from -48 to 48
- fc2_second: float32 [4096, 1024], P('shard'), may hold values from 232.6528 to 930.6112
- vec_master: float32 [13312], P('shard'), may hold values from -0.7 to 1.35
- vec_first: float32 [13312], P('shard'), may hold values from -64 to 64
- vec_second: float32 [13312], P('shard'), may hold values from 647.168 to 2588.672
Outputs:
- output: float32 [16384, 1024], P(('rep', 'shard'))
- input_grad: float32 [16384, 1024], P(('rep', 'shard'))
- qkv_first_new: float32 [1024, 3072], P('shard')
- qkv_second_new: float32 [1024, 3072], P('shard')
- qkv_new: float32 [1024, 3072], P('shard')
- out_first_new: float32 [1024, 1024], P('shard')
- out_second_new: float32 [1024, 1024], P('shard')
- out_new: float32 [1024, 1024], P('shard')
- fc1_first_new: float32 [1024, 4096], P('shard')
- fc1_second_new: float32 [1024, 4096], P('shard')
- fc1_new: float32 [1024, 4096], P('shard')
- fc2_first_new: float32 [4096, 1024], P('shard')
- fc2_second_new: float32 [4096, 1024], P('shard')
- fc2_new: float32 [4096, 1024], P('shard')
- vec_first_new: float32 [13312], P('shard')
- vec_second_new: float32 [13312], P('shard')
- vec_new: float32 [13312], P('shard')
The draws below stay inside these ranges and needn't reach their ends.
Inputs may be any that keep to these rules, and one draw needn't show every extreme that they name: `positions`: each device's 512 slots hold one or two whole sequences from the first slot on, each value counting up from 0 within its sequence; -1 marks the unused slots at the end. Each device uses 512 // 2 slots or more, and some device holds one sequence of all 512 slots.
All inputs are finite; a program needn't handle non-finite values.
Results may differ from the reference program's by a relative error of at most 0.0025.
The reference program's roundings to bfloat16 on the way count: a program that leaves them out, or rounds other values in their place, can miss the bound.
Values may be sent and summed in bfloat16 or wider, within the bound.
A program may use at most 320 MiB of HBM per device.

```python
import math
import jax
import jax.numpy as jnp
from jax import lax

D = 1024
H = 16
HD = 64
FF = 4096
ROT = 16
STEP = 10
TOK_DEV = 512
TOKENS = 16384
VEC = 13312
DEVICES = 32


def draw_positions(key, part):
    key = jax.random.fold_in(key, 11)
    devices_all = TOKENS // TOK_DEV
    key_used, key_full, key_cut = jax.random.split(key, 3)
    used = jax.random.randint(key_used, (devices_all,), TOK_DEV // 2, TOK_DEV + 1)
    fullest = jax.random.randint(key_full, (), 0, devices_all)
    cut_bits = jax.random.randint(key_cut, (devices_all,), 0, 1 << 20)
    cut = 1 + cut_bits % (used - 1)
    is_full = jnp.arange(devices_all) == fullest
    used = jnp.where(is_full, TOK_DEV, used)
    cut = jnp.where(is_full, TOK_DEV, cut)
    slots = jnp.arange(TOK_DEV)[None, :]
    place = jnp.where(slots < cut[:, None], slots, slots - cut[:, None])
    place = jnp.where(slots < used[:, None], place, -1)
    return place.reshape(TOKENS).astype(jnp.int32)


def draw_vec_master(key, part):
    key = jax.random.fold_in(key, 5)
    index = jnp.arange(VEC)
    is_gain = (index < D) | (index >= 2 * D) & (index < 3 * D)
    noise = jnp.clip(jax.random.normal(key, (VEC,), jnp.float32) * 0.25, -0.7, 0.7)
    return jnp.where(is_gain, 1.0 + 0.5 * noise, noise).astype(jnp.float32)


def levels(rng, extent, cuts, low, high):
    loudness, own = 1.0, jax.random.fold_in(rng, 6)
    for axis_at, blocks in cuts:
        draws = jnp.exp(jax.random.uniform(jax.random.fold_in(own, axis_at), (blocks,), jnp.float32, low / len(cuts), high / len(cuts)))
        loudness = loudness * jnp.repeat(draws, extent[axis_at] // blocks).reshape([-1 if axis == axis_at else 1 for axis in range(len(extent))])
    return loudness


def bell_draw(rng, shape, spread, reach, shards=(), dtype=jnp.bfloat16):
    array = jax.random.normal(rng, shape, jnp.float32) * spread
    if len(shards) > 0:
        array = levels(rng, shape, shards, -0.22, 0.18) * array
    return jnp.clip(array, min=-reach, max=reach).astype(dtype)


def setup_inputs(seed: int = 0) -> dict:
    key_list = jax.random.split(jax.random.key(seed), 19)
    return {
        "tokens": bell_draw(key_list[0], (TOKENS, D), 1.0, 6.0, ((0, 32),)),
        "cotangent": bell_draw(key_list[1], (TOKENS, D), 1.0, 6.0, ((0, 32),), jnp.float32),
        "positions": draw_positions(jax.random.fold_in(key_list[18], 71), 0),
        "qkv_master": bell_draw(key_list[3], (D, 3 * D), D ** -0.5, 0.1875, ((0, 8),), jnp.float32),
        "qkv_first": bell_draw(key_list[4], (D, 3 * D), (0.111 * (0.75 * TOK_DEV * DEVICES) ** 0.5), 64.0, ((0, 8),), jnp.float32),
        "qkv_second": jnp.clip(jnp.exp(math.log(2588.672) - 1.3862944 * jax.random.uniform(key_list[5], (D, 3 * D), jnp.float32) ** levels(key_list[5], (D, 3 * D), ((0, 8),), -0.2, 0.2)), 647.168, 2588.672),
        "out_master": bell_draw(key_list[6], (D, D), (D // 32) ** -0.5, 1.0, ((0, 8),), jnp.float32),
        "out_first": bell_draw(key_list[7], (D, D), (0.0111 * (0.75 * TOK_DEV * DEVICES) ** 0.5), 7.0, ((0, 8),), jnp.float32),
        "out_second": jnp.clip(jnp.exp(math.log(25.88672) - 1.3862944 * jax.random.uniform(key_list[8], (D, D), jnp.float32) ** levels(key_list[8], (D, D), ((0, 8),), -0.2, 0.2)), 6.47168, 25.88672),
        "fc1_master": bell_draw(key_list[9], (D, FF), D ** -0.5, 0.1875, ((0, 8),), jnp.float32),
        "fc1_first": bell_draw(key_list[10], (D, FF), (0.0333 * (0.75 * TOK_DEV * DEVICES) ** 0.5), 20.0, ((0, 8),), jnp.float32),
        "fc1_second": jnp.clip(jnp.exp(math.log(232.6528) - 1.3862944 * jax.random.uniform(key_list[11], (D, FF), jnp.float32) ** levels(key_list[11], (D, FF), ((0, 8),), -0.2, 0.2)), 58.1632, 232.6528),
        "fc2_master": bell_draw(key_list[12], (FF, D), FF ** -0.5, 0.09375, ((0, 8),), jnp.float32),
        "fc2_first": bell_draw(key_list[13], (FF, D), (0.0667 * (0.75 * TOK_DEV * DEVICES) ** 0.5), 48.0, ((0, 8),), jnp.float32),
        "fc2_second": jnp.clip(jnp.exp(math.log(930.6112) - 1.3862944 * jax.random.uniform(key_list[14], (FF, D), jnp.float32) ** levels(key_list[14], (FF, D), ((0, 8),), -0.2, 0.2)), 232.6528, 930.6112),
        "vec_master": draw_vec_master(jax.random.fold_in(key_list[18], 71), 0),
        "vec_first": bell_draw(key_list[16], (VEC,), (0.111 * (0.75 * TOK_DEV * DEVICES) ** 0.5), 64.0, ((0, 8),), jnp.float32),
        "vec_second": jnp.clip(jnp.exp(math.log(2588.672) - 1.3862944 * jax.random.uniform(key_list[17], (VEC,), jnp.float32) ** levels(key_list[17], (VEC,), ((0, 8),), -0.2, 0.2)), 647.168, 2588.672),
    }


@jax.custom_vjp
def low(v):
    return lax.optimization_barrier(v.astype(jnp.bfloat16)).astype(jnp.float32)

@jax.custom_vjp
def low_back(v):
    return v

def low_keep(v):
    return (low(v), None)

def low_pass(kept, grad):
    return (grad,)

def back_keep(v):
    return (v, None)

def back_low(kept, grad):
    return (low(grad),)
low.defvjp(low_keep, low_pass)
low_back.defvjp(back_keep, back_low)
beta_one = 0.9
beta_two = 0.95
epsilon = 1e-08
weight_decay = 0.1
norm_eps = 1e-05
vector_rate = 0.1

def split_vector(vec):
    bounds = [D, D, D, D, 3 * D, D, FF, D]
    pieces = []
    start = 0
    for width in bounds:
        pieces.append(vec[start:start + width])
        start = start + width
    return pieces

def layer_norm(x, gain, bias):
    mean = lax.optimization_barrier(jnp.mean(x, axis=-1, keepdims=True))
    centred = x - mean
    var = lax.optimization_barrier(jnp.mean(centred * centred, axis=-1, keepdims=True))
    return centred * lax.rsqrt(var + norm_eps) * gain + bias

def rotary_tables(positions):
    half = ROT // 2
    freqs = 10000.0 ** (-jnp.arange(half).astype(jnp.float32) * 2.0 / ROT)
    angle = jnp.maximum(positions, 0).astype(jnp.float32)[:, None] * freqs[None, :]
    return (jnp.cos(angle), jnp.sin(angle))

def rotate(heads_in, cosine, sine):
    half = ROT // 2
    first = heads_in[..., :half]
    second = heads_in[..., half:ROT]
    cos_b = cosine[:, None, :]
    sin_b = sine[:, None, :]
    return jnp.concatenate([first * cos_b - second * sin_b, second * cos_b + first * sin_b, heads_in[..., ROT:]], axis=-1)

def block(x, qkv_w, out_w, fc1_w, fc2_w, vec, positions):
    high = lax.Precision.HIGHEST
    gain_one, bias_one, gain_two, bias_two, bias_qkv, bias_out, bias_fc1, bias_fc2 = split_vector(vec)
    rows = x.shape[0]
    normed_one = low(layer_norm(x, gain_one, bias_one))
    normed_two = low(layer_norm(x, gain_two, bias_two))
    qkv = low_back(jnp.dot(normed_one, qkv_w, precision=high) + bias_qkv).reshape(rows, 3, H, HD)
    cosine, sine = rotary_tables(positions)
    query = low(rotate(qkv[:, 0], cosine, sine))
    keys = low(rotate(qkv[:, 1], cosine, sine))
    values = low(qkv[:, 2])
    scores = low_back(jnp.einsum('qhd,khd->hqk', query, keys, precision=high) * HD ** (-0.5))
    query_idx = jnp.arange(rows)[:, None]
    key_idx = jnp.arange(rows)[None, :]
    allowed = (key_idx <= query_idx) & (key_idx >= query_idx - jnp.maximum(positions, 0)[:, None])
    scores = jnp.where(allowed[None], scores, -1e+30)
    top = lax.optimization_barrier(jnp.max(scores, axis=-1, keepdims=True))
    expo = jnp.exp(scores - top)
    probs = low(expo / lax.optimization_barrier(jnp.sum(expo, axis=-1, keepdims=True)))
    mixed = low(low_back(jnp.einsum('hqk,khd->qhd', probs, values, precision=high))).reshape(rows, D)
    attn = low_back(jnp.dot(mixed, out_w, precision=high) + bias_out)
    hidden = low_back(jnp.dot(normed_two, fc1_w, precision=high) + bias_fc1)
    act = low(jax.nn.gelu(hidden, approximate=False))
    mlp = low_back(jnp.dot(act, fc2_w, precision=high) + bias_fc2)
    return x + attn + mlp

def adam(master, first, second, grad, rate, decay_on):
    first_new = beta_one * first + (1.0 - beta_one) * grad
    second_new = beta_two * second + (1.0 - beta_two) * grad * grad
    mhat = first_new / (1.0 - beta_one ** STEP)
    vhat = second_new / (1.0 - beta_two ** STEP)
    new = master - rate * (mhat / (jnp.sqrt(vhat) + epsilon) + decay_on * master)
    return (first_new, second_new, new)

def reference(tokens, cotangent, positions, qkv_master, qkv_first, qkv_second, out_master, out_first, out_second, fc1_master, fc1_first, fc1_second, fc2_master, fc2_first, fc2_second, vec_master, vec_first, vec_second):
    weights = (low(qkv_master), low(out_master), low(fc1_master), low(fc2_master), low(vec_master))
    blocks = TOKENS // TOK_DEV
    x_all = tokens.astype(jnp.float32).reshape(blocks, TOK_DEV, D)
    dy_all = cotangent.reshape(blocks, TOK_DEV, D)
    pos_all = positions.reshape(blocks, TOK_DEV)

    def one(carry, items):
        x_blk, dy_blk, pos_blk = items
        valid = (pos_blk >= 0).astype(jnp.float32)[:, None]

        def run(xx, w_qkv, w_out, w_fc1, w_fc2, w_vec):
            return block(xx, w_qkv, w_out, w_fc1, w_fc2, w_vec, pos_blk)
        result, pull = jax.vjp(run, x_blk, *weights)
        grads = pull(dy_blk * valid)
        carry = tuple((c + g for c, g in zip(carry, grads[1:])))
        return (carry, (result, grads[0]))
    zeros = tuple((jnp.zeros(w.shape, jnp.float32) for w in weights))
    totals, (outs, dxs) = lax.scan(one, zeros, (x_all, dy_all, pos_all))
    g_qkv, g_out, g_fc1, g_fc2, g_vec = totals
    qf, qs, qn = adam(qkv_master, qkv_first, qkv_second, g_qkv, 0.5 * D ** (-0.5), weight_decay)
    of, os_, on = adam(out_master, out_first, out_second, g_out, 0.5 * (32.0 / D) ** 0.5, weight_decay)
    f1f, f1s, f1n = adam(fc1_master, fc1_first, fc1_second, g_fc1, 0.5 * D ** (-0.5), weight_decay)
    f2f, f2s, f2n = adam(fc2_master, fc2_first, fc2_second, g_fc2, 0.5 * FF ** (-0.5), weight_decay)
    vf, vs, vn = adam(vec_master, vec_first, vec_second, g_vec, vector_rate, 0.0)
    return (outs.reshape(TOKENS, D), dxs.reshape(TOKENS, D), qf, qs, qn, of, os_, on, f1f, f1s, f1n, f2f, f2s, f2n, vf, vs, vn)
```

```python
import functools
import math

import jax
import jax.numpy as jnp
from jax import lax
from jax.experimental import pallas as pl
from jax.experimental.pallas import tpu as pltpu
from jax.sharding import PartitionSpec as P

D = 1024
H = 16
HD = 64
FF = 4096
ROT = 16
STEP = 10

beta_one = 0.9
beta_two = 0.95
epsilon = 1e-08
weight_decay = 0.1
norm_eps = 1e-05
vector_rate = 0.1

MESH = pl.DeviceIdType.MESH
LANES = 128
UNITS = 12
WIDE = 1024
TILE = 256
RING = 4
VEC_ROWS = 13
f32 = jnp.float32
bf16 = jnp.bfloat16


def dot(a, b):
    return jnp.dot(a, b, preferred_element_type=f32)


def dot_nt(a, b):
    return lax.dot_general(a, b, (((1,), (1,)), ((), ())), preferred_element_type=f32)


def dot_tn(a, b):
    return lax.dot_general(a, b, (((0,), (0,)), ((), ())), preferred_element_type=f32)


def run(first, count, width):
    return pl.ds(pl.multiple_of(first * width, LANES), count * width)


class Place:
    def __init__(self, n_rep, n_shard):
        self.n_rep, self.n_shard = n_rep, n_shard
        self.line = n_shard // 2
        self.bits = n_rep.bit_length() - 1
        self.rep = lax.axis_index("rep")
        self.shard = lax.axis_index("shard")
        self.core = lax.rem(self.shard, 2)
        self.spot = lax.div(self.shard, 2)
        digits = [lax.rem(lax.div(self.rep, 1 << p), 2) for p in range(self.bits)]
        turned = sum(digits[p] * (1 << (self.bits - 1 - p)) for p in range(self.bits))
        self.block = (1 - self.core) * self.rep + self.core * turned
        self.twins = []
        for p in range(self.bits):
            q = self.bits - 1 - p
            step_even = (1 - 2 * digits[p]) * (1 << p)
            step_odd = (1 - 2 * digits[q]) * (1 << q)
            self.twins.append(self.rep + (1 - self.core) * step_even + self.core * step_odd)

    def hold(self, p):
        return lax.div(self.block, 1 << p) * (1 << p)

    def other(self, p):
        mine = lax.div(self.block, 1 << p)
        return (mine + 1 - 2 * lax.rem(mine, 2)) * (1 << p)

    def ahead(self, d):
        return lax.rem(self.spot + d, self.line)

    def behind(self, d):
        return lax.rem(self.spot + self.line - d, self.line)

    def along(self, d):
        return (self.rep, 2 * self.ahead(d) + self.core)

    def sibling(self):
        return (self.rep, self.shard + 1 - 2 * self.core)

    def twin(self, p):
        return (self.twins[p], self.shard)

    def group(self, d):
        return (self.rep, lax.rem(self.shard + d, self.n_shard))

    def replica(self, d):
        return (lax.rem(self.rep + d, self.n_rep), self.shard)

    def greet(self):
        barrier = pltpu.get_barrier_semaphore()
        peers = [self.group(d) for d in range(1, self.n_shard)]
        peers += [self.replica(d) for d in range(1, self.n_rep)]
        for peer in peers:
            pl.semaphore_signal(barrier, inc=1, device_id=peer, device_id_type=MESH)
        pl.semaphore_wait(barrier, len(peers))


class Copies:
    def __init__(self, send, recv):
        self.send, self.recv, self.used, self.sent = send, recv, 0, []

    def take(self, count):
        self.used += count
        return self.used - count

    def make(self, slot, src, dst, peer):
        return pltpu.make_async_remote_copy(
            src_ref=src,
            dst_ref=dst,
            send_sem=self.send.at[slot],
            recv_sem=self.recv.at[slot],
            device_id=peer,
            device_id_type=MESH,
        )

    def start(self, slot, src, dst, peer):
        copy = self.make(slot, src, dst, peer)
        copy.start()
        self.sent.append(copy)

    def arrived(self, slot, dst, peer):
        self.make(slot, dst, dst, peer).wait_recv()

    def drain(self):
        for copy in self.sent:
            copy.wait_send()


class Gather:
    def __init__(self, at, copies, own, full):
        self.at, self.copies, self.own, self.full = at, copies, own, full
        self.width = WIDE // at.n_rep
        self.per_unit = (at.line - 1) * (at.bits + 1) + at.line
        self.base = copies.take(self.per_unit * UNITS)

    def slot(self, u, p):
        return self.base + u * self.per_unit + p * (self.at.line - 1)

    def line_sends(self, u):
        at, mine = self.at, run(self.at.hold(0), 1, self.width)
        return [
            self.copies.make(
                self.slot(u, 0) + d - 1,
                self.own.at[u, :, mine],
                self.full.at[u, at.spot, at.core, :, mine],
                at.along(d),
            )
            for d in range(1, at.line)
        ]

    def twin_send(self, u, p, d):
        at = self.at
        piece = self.full.at[u, at.behind(d), at.core, :, run(at.hold(p), 1 << p, self.width)]
        return self.copies.make(self.slot(u, p + 1) + d - 1, piece, piece, at.twin(p))

    def sibling_send(self, u, d):
        at = self.at
        piece = self.full.at[u, at.behind(d), at.core]
        return self.copies.make(
            self.slot(u, at.bits + 1) + d, self.own.at[u] if d == 0 else piece, piece, at.sibling()
        )

    def stage(self, u, p):
        at = self.at
        if p == at.bits + 1:
            for d in range(at.line):
                self.copies.arrived(
                    self.slot(u, p) + d, self.full.at[u, at.behind(d), 1 - at.core], at.sibling()
                )
            return
        if p == at.bits:
            self.sibling_send(u, 0).start()
        for d in range(1, at.line):
            got = run(at.other(p - 1), 1 << (p - 1), self.width) if p > 0 else run(at.hold(0), 1, self.width)
            self.copies.arrived(
                self.slot(u, p) + d - 1,
                self.full.at[u, at.behind(d), at.core, :, got],
                at.twin(p - 1) if p > 0 else at.along(d),
            )
            if p < at.bits:
                self.twin_send(u, p, d).start()
            else:
                self.sibling_send(u, d).start()

    def drain(self, u):
        at = self.at
        for copy in self.line_sends(u):
            copy.wait_send()
        for p in range(at.bits):
            for d in range(1, at.line):
                self.twin_send(u, p, d).wait_send()
        for d in range(at.line):
            self.sibling_send(u, d).wait_send()


def vector_places(n_shard, lane):
    places = []
    for row in range(VEC_ROWS):
        for q in range(WIDE // lane):
            if 8 <= row < 12:
                start = 8 * WIDE + q * (FF // n_shard) + (row - 8) * lane
            else:
                start = row * WIDE + q * lane
            places.append((row, q * lane, start // lane // VEC_ROWS, start // lane % VEC_ROWS))
    return places


def mlp_kernel(
    n_rep, n_shard, own, vec_own, tokens, cot, valid,
    late, grads, rows_out, part, d_two, act_one, grad_low, grad_vec,
    full, vec_full, act_two, act_two_t, act, d_hidden, stage_grads, send, recv, local,
):
    at = Place(n_rep, n_shard)
    line, bits = at.line, at.bits
    shard_rows = own.shape[1]
    tall = TILE // (2 * shard_rows)
    tokens_here = tokens.shape[0]
    lane = vec_own.shape[1]
    at.greet()
    copies = Copies(send, recv)
    gather = Gather(at, copies, own, full)
    vec_slot = copies.take(n_shard)
    for d in range(1, n_shard):
        copies.start(vec_slot + d, vec_own, vec_full.at[at.shard], at.group(d))

    def begin(u, _):
        for copy in gather.line_sends(u):
            copy.start()
        pltpu.make_async_copy(own.at[u], full.at[u, at.spot, at.core], local.at[u]).start()
        return 0

    lax.fori_loop(0, UNITS, begin, 0)
    vec_full[at.shard] = vec_own[...]

    sums = jnp.zeros((1, WIDE), f32)
    step = 64

    def lower(i, sums):
        rows = pl.ds(pl.multiple_of(i * step, step), step)
        low = (cot[rows] * valid[rows]).astype(bf16)
        grad_low[rows] = low
        d_two[rows] = jnp.zeros((step, WIDE), f32)
        return sums + jnp.sum(low.astype(f32), axis=0, keepdims=True)

    grad_vec[4:5] = lax.fori_loop(0, tokens_here // step, lower, sums)

    for d in range(1, n_shard):
        copies.arrived(vec_slot + d, vec_full.at[lax.rem(at.shard + n_shard - d, n_shard)], at.group(d))
    for row, first, device, place in vector_places(n_shard, lane):
        rows_out[row : row + 1, first : first + lane] = vec_full[device, place : place + 1, :]

    def norm(i, _):
        rows = pl.ds(pl.multiple_of(i * step, step), step)
        x = tokens[rows].astype(f32)
        centred = x - jnp.mean(x, axis=-1, keepdims=True)
        var = jnp.mean(centred * centred, axis=-1, keepdims=True)
        unit = centred * lax.rsqrt(var + norm_eps)
        act_one[rows] = (unit * rows_out[0:1] + rows_out[1:2]).astype(bf16)
        act_two[rows] = (unit * rows_out[2:3] + rows_out[3:4]).astype(bf16)
        part[rows] = x + rows_out[12:13]
        return 0

    lax.fori_loop(0, tokens_here // step, norm, 0)
    act_two_t[...] = act_two[...].T

    stages = bits + 2

    def steps_of(t):
        return [(t - p, p) for p in range(stages)]

    def guarded(u, p):
        if isinstance(u, int):
            if 0 <= u < UNITS:
                gather.stage(u, p)
        else:
            pl.when(u < UNITS)(lambda: gather.stage(u, p))

    def here(u):
        return pltpu.make_async_copy(own.at[u], full.at[u, at.spot, at.core], local.at[u])

    for t in range(stages + 1):
        for u, p in steps_of(t):
            guarded(u, p)

    def out_copy(k, u):
        return pltpu.make_async_copy(stage_grads.at[k], grads.at[u], local.at[UNITS + k])

    def tile(j, _):
        u1, u2 = 2 * j, 2 * j + 1
        here(u1).wait()
        here(u2).wait()
        jobs = steps_of(stages + 1 + 2 * j) + steps_of(stages + 2 + 2 * j)

        def comm(q):
            for u, p in jobs[q * len(jobs) // 8 : (q + 1) * len(jobs) // 8]:
                guarded(u, p)

        for q in range(4):
            comm(q)
            cols = slice(q * TILE, (q + 1) * TILE)
            spots = slice(q * tall, (q + 1) * tall)
            w1 = full[u1, :, :, :, cols].reshape(D, TILE)
            h = dot(act_two[...], w1) + rows_out[pl.ds(8 + j, 1), cols]
            below = 0.5 + 0.5 * lax.erf(h * (0.5**0.5))
            act[:, cols] = (h * below).astype(bf16)
            slope = below + h * (jnp.exp(-0.5 * h * h) * (1.0 / math.sqrt(2.0 * math.pi)))
            w2 = full[u2, spots].reshape(TILE, D)
            dh = (dot_nt(grad_low[...], w2) * slope).astype(bf16)
            d_hidden[:, cols] = dh
            grad_vec[pl.ds(j, 1), cols] = jnp.sum(dh.astype(f32), axis=0, keepdims=True)
        for q in range(4):
            comm(4 + q)
            cols = slice(q * TILE, (q + 1) * TILE)
            spots = slice(q * tall, (q + 1) * tall)
            if q == 0:

                @pl.when(j > 0)
                def _():
                    out_copy(0, 0).wait()
                    out_copy(1, 0).wait()

            part[:, cols] += dot(act[...], full[u2, :, :, :, cols].reshape(D, TILE))
            d_two[:, cols] += dot_nt(d_hidden[...], full[u1, spots].reshape(TILE, WIDE))
            stage_grads[1, spots] = dot_tn(act[:, cols], grad_low[...]).reshape(tall, 2, shard_rows, WIDE)
            stage_grads[0, spots] = dot(act_two_t[cols], d_hidden[...]).reshape(tall, 2, shard_rows, WIDE)
        out_copy(0, u1).start()
        out_copy(1, u2).start()
        return 0

    lax.fori_loop(0, 4, tile, 0)
    for t in range(stages + 9, UNITS + stages - 1):
        for u, p in steps_of(t):
            guarded(u, p)
    for u in range(8, UNITS):
        here(u).wait()
        pltpu.make_async_copy(full.at[u], late.at[u - 8], local.at[u]).start()
    out_copy(0, 0).wait()
    out_copy(1, 0).wait()
    for u in range(8, UNITS):
        pltpu.make_async_copy(full.at[u], late.at[u - 8], local.at[u]).wait()

    def finish(u, _):
        gather.drain(u)
        return 0

    lax.fori_loop(0, UNITS, finish, 0)
    copies.drain()


def mlp(own, vec_own, tokens, cot, valid, n_rep, n_shard):
    shard_rows, line, bits = own.shape[1], n_shard // 2, n_rep.bit_length() - 1
    slots = UNITS * ((line - 1) * (bits + 1) + line) + n_shard
    count = tokens.shape[0]
    anywhere = pl.BlockSpec(memory_space=pl.ANY)
    vmem = pl.BlockSpec(memory_space=pltpu.VMEM)
    unit = (line, 2, shard_rows, WIDE)
    return pl.pallas_call(
        functools.partial(mlp_kernel, n_rep, n_shard),
        out_shape=(
            jax.ShapeDtypeStruct((4,) + unit, bf16),
            jax.ShapeDtypeStruct((8,) + unit, f32),
            jax.ShapeDtypeStruct((16, WIDE), f32),
            jax.ShapeDtypeStruct((count, WIDE), f32),
            jax.ShapeDtypeStruct((count, WIDE), f32),
            jax.ShapeDtypeStruct((count, WIDE), bf16),
            jax.ShapeDtypeStruct((count, WIDE), bf16),
            jax.ShapeDtypeStruct((8, WIDE), f32),
        ),
        in_specs=[anywhere, vmem, vmem, vmem, vmem],
        out_specs=(anywhere, anywhere, vmem, vmem, vmem, vmem, vmem, vmem),
        scratch_shapes=[
            pltpu.VMEM((UNITS,) + unit, bf16),
            pltpu.VMEM((n_shard,) + vec_own.shape, f32),
            pltpu.VMEM((count, WIDE), bf16),
            pltpu.VMEM((WIDE, count), bf16),
            pltpu.VMEM((count, WIDE), bf16),
            pltpu.VMEM((count, WIDE), bf16),
            pltpu.VMEM((2,) + unit, f32),
            pltpu.SemaphoreType.DMA((slots,)),
            pltpu.SemaphoreType.DMA((slots,)),
            pltpu.SemaphoreType.DMA((UNITS + 2,)),
        ],
        compiler_params=pltpu.CompilerParams(
            collective_id=0, has_side_effects=True, vmem_limit_bytes=60 * 2**20
        ),
        name="gather_and_mlp",
    )(own, vec_own, tokens, cot, valid)


def turn(u, tables, sign):
    cosine, up, down = tables
    return u * cosine + sign * (pltpu.roll(u, LANES - ROT // 2, 1) * up + pltpu.roll(u, ROT // 2, 1) * down)


def attention_kernel(
    late, rows, act_one, grad_low, tokens, cot, valid, part, d_two, positions, cosine, up, down,
    output, input_grad, grads, grad_vec,
    query, keys, values, d_mixed, mixed, d_qkv, act_one_t, bias, d_one, stage_grads, local,
):
    count = tokens.shape[0]
    line, shard_rows = late.shape[1], late.shape[3]
    tall = TILE // (2 * shard_rows)
    step = 64
    scale = HD**-0.5
    tables = (cosine[...], up[...], down[...])

    def weight(j, cols):
        return late[j, :, :, :, cols].reshape(D, cols.stop - cols.start)

    key_idx = lax.broadcasted_iota(jnp.int32, (count, count), 0)
    query_idx = lax.broadcasted_iota(jnp.int32, (count, count), 1)
    allowed = (key_idx <= query_idx) & (key_idx >= query_idx - jnp.maximum(positions[...], 0))
    bias[...] = jnp.where(allowed, 0.0, -1e30)
    act_one_t[...] = act_one[...].T

    for q in range(4):
        cols = slice(q * TILE, (q + 1) * TILE)
        spots = slice(q * tall, (q + 1) * tall)
        for j, target in enumerate((query, keys, values)):
            value = dot(act_one[...], weight(j, cols)) + rows[4 + j : 5 + j, cols]
            for half in range(TILE // LANES):
                piece = value[:, half * LANES : (half + 1) * LANES]
                if j < 2:
                    piece = turn(piece, tables, 1.0)
                piece = piece.astype(bf16)
                if j == 0:
                    piece = piece * jnp.asarray(scale, bf16)
                target[:, q * TILE + half * LANES : q * TILE + (half + 1) * LANES] = piece
        d_mixed[:, cols] = dot_nt(grad_low[...], late[3, spots].reshape(TILE, WIDE)).astype(bf16)

    first_head = lax.broadcasted_iota(jnp.int32, (1, LANES), 1) < HD

    def pair(i, _):
        cols = pl.ds(pl.multiple_of(i * LANES, LANES), LANES)
        q2, k2, v2, o2 = query[:, cols], keys[:, cols], values[:, cols], d_mixed[:, cols]
        nothing = jnp.zeros((), bf16)
        mixed_parts, dq_parts = [0.0, 0.0], [0.0, 0.0]
        dk_parts, dv_parts = [0.0, 0.0], [0.0, 0.0]
        for head in range(2):
            keep = first_head if head == 0 else jnp.logical_not(first_head)
            qm, km, vm, om = (jnp.where(keep, w, nothing) for w in (q2, k2, v2, o2))
            for b in range(count // TILE):
                span = slice(0, (b + 1) * TILE)
                mine = slice(b * TILE, (b + 1) * TILE)
                scores = dot_nt(k2[span], qm[mine]) + bias[span, mine]
                top = jnp.max(scores, axis=0, keepdims=True)
                expo = jnp.exp(scores - top)
                probs = expo * (1.0 / jnp.sum(expo, axis=0, keepdims=True))
                low = probs.astype(bf16)
                d_probs = dot_nt(v2[span], om[mine])
                inner = jnp.sum(probs * d_probs, axis=0, keepdims=True)
                d_scores = (probs * (d_probs - inner)).astype(bf16)
                mixed_parts[b] += dot_tn(low, vm[span])
                dq_parts[b] += dot_tn(d_scores, km[span])
                dv = dot(low, om[mine])
                dk = dot(d_scores, qm[mine])
                for c in range(b + 1):
                    dk_parts[c] += dk[c * TILE : (c + 1) * TILE]
                    dv_parts[c] += dv[c * TILE : (c + 1) * TILE]
        for b in range(count // TILE):
            mine = slice(b * TILE, (b + 1) * TILE)
            local_tables = tuple(w[mine] for w in tables)
            mixed[mine, cols] = mixed_parts[b].astype(bf16)
            d_qkv[0, mine, cols] = turn(dq_parts[b] * scale, local_tables, -1.0).astype(bf16)
            d_qkv[1, mine, cols] = turn(dk_parts[b], local_tables, -1.0).astype(bf16)
            d_qkv[2, mine, cols] = dv_parts[b].astype(bf16)
        return 0

    lax.fori_loop(0, H // 2, pair, 0)

    def out_copy(j):
        return pltpu.make_async_copy(stage_grads.at[j % 2], grads.at[j], local.at[j % 2])

    for j in range(4):
        if j >= 2:
            out_copy(j - 2).wait()
        for q in range(4):
            cols = slice(q * TILE, (q + 1) * TILE)
            spots = slice(q * tall, (q + 1) * tall)
            if j < 3:
                value = dot(act_one_t[cols], d_qkv[j])
            else:
                value = dot_tn(mixed[:, cols], grad_low[...])
            stage_grads[j % 2, spots] = value.reshape(tall, 2, shard_rows, WIDE)
        out_copy(j).start()
    for q in range(4):
        cols = slice(q * TILE, (q + 1) * TILE)
        spots = slice(q * tall, (q + 1) * tall)
        output[:, cols] = part[:, cols] + (dot(mixed[...], weight(3, cols)) + rows[7:8, cols])
        value = dot_nt(d_qkv[0], late[0, spots].reshape(TILE, WIDE))
        value += dot_nt(d_qkv[1], late[1, spots].reshape(TILE, WIDE))
        value += dot_nt(d_qkv[2], late[2, spots].reshape(TILE, WIDE))
        d_one[:, cols] = value
    for j in range(3):
        grad_vec[4 + j : 5 + j] = jnp.sum(d_qkv[j].astype(f32), axis=0, keepdims=True)

    def norm_back(i, sums):
        mine = pl.ds(pl.multiple_of(i * step, step), step)
        x = tokens[mine].astype(f32)
        centred = x - jnp.mean(x, axis=-1, keepdims=True)
        var = jnp.mean(centred * centred, axis=-1, keepdims=True)
        spread = lax.rsqrt(var + norm_eps)
        unit = centred * spread
        one, two = d_one[mine], d_two[mine]
        d_unit = one * rows[0:1] + two * rows[2:3]
        flat = jnp.mean(d_unit, axis=-1, keepdims=True)
        tilt = jnp.mean(d_unit * unit, axis=-1, keepdims=True)
        input_grad[mine] = cot[mine] * valid[mine] + spread * (d_unit - flat - unit * tilt)
        return tuple(
            s + jnp.sum(w, axis=0, keepdims=True) for s, w in zip(sums, (one * unit, one, two * unit, two))
        )

    sums = lax.fori_loop(0, count // step, norm_back, (jnp.zeros((1, WIDE), f32),) * 4)
    for k in range(4):
        grad_vec[k : k + 1] = sums[k]
    out_copy(2).wait()
    out_copy(3).wait()


def attention(late, rows, act_one, grad_low, tokens, cot, valid, part, d_two, positions, tables):
    count = tokens.shape[0]
    unit = late.shape[1:]
    anywhere = pl.BlockSpec(memory_space=pl.ANY)
    vmem = pl.BlockSpec(memory_space=pltpu.VMEM)
    return pl.pallas_call(
        attention_kernel,
        out_shape=(
            jax.ShapeDtypeStruct((count, WIDE), f32),
            jax.ShapeDtypeStruct((count, WIDE), f32),
            jax.ShapeDtypeStruct((4,) + unit, f32),
            jax.ShapeDtypeStruct((8, WIDE), f32),
        ),
        in_specs=[vmem] * 13,
        out_specs=(vmem, vmem, anywhere, vmem),
        scratch_shapes=[
            pltpu.VMEM((count, WIDE), bf16),
            pltpu.VMEM((count, WIDE), bf16),
            pltpu.VMEM((count, WIDE), bf16),
            pltpu.VMEM((count, WIDE), bf16),
            pltpu.VMEM((count, WIDE), bf16),
            pltpu.VMEM((3, count, WIDE), bf16),
            pltpu.VMEM((WIDE, count), bf16),
            pltpu.VMEM((count, count), f32),
            pltpu.VMEM((count, WIDE), f32),
            pltpu.VMEM((2,) + unit, f32),
            pltpu.SemaphoreType.DMA((2,)),
        ],
        compiler_params=pltpu.CompilerParams(vmem_limit_bytes=60 * 2**20),
        name="attention",
    )(late, rows, act_one, grad_low, tokens, cot, valid, part, d_two, positions, *tables)


def reduce_kernel(
    n_rep, n_shard, early, late, vec_part, total, vec_sum, sib, vec_got, vec_all,
    mine_buf, sib_buf, keep, halves_out, halves_in, line_out, line_in, final, send, recv, local,
):
    at = Place(n_rep, n_shard)
    line, bits, width = at.line, at.bits, WIDE // n_rep
    at.greet()
    copies = Copies(send, recv)
    per_unit = 1 + bits + (line - 1) + bits
    base = copies.take(per_unit * UNITS)
    vec_slot = copies.take(n_shard)
    vec_slot_rep = copies.take(n_rep)

    def part(u, core):
        return early.at[u, :, core] if u < 8 else late.at[u - 8, :, core]

    for d in range(1, n_shard):
        to = lax.rem(at.shard + d, n_shard)
        copies.start(vec_slot + d, vec_part.at[to], vec_got.at[d], at.group(d))
    for u in range(UNITS):
        copies.start(base + u * per_unit, part(u, 1 - at.core), sib.at[u], at.sibling())

    def load(u):
        return (
            pltpu.make_async_copy(part(u, at.core), mine_buf.at[u % 2], local.at[u % 2, 0]),
            pltpu.make_async_copy(sib.at[u], sib_buf.at[u % 2], local.at[u % 2, 1]),
        )

    def fetch(u):
        copies.arrived(base + u * per_unit, sib.at[u], at.sibling())
        for copy in load(u):
            copy.start()

    def first(u):
        for copy in load(u):
            copy.wait()
        p = bits - 1
        to, stay = run(at.other(p), 1 << p, width), run(at.hold(p), 1 << p, width)

        def body(spot, _):
            a = mine_buf.at[u % 2, spot]
            b = sib_buf.at[u % 2, spot]
            halves_out[p][u, spot] = (a[:, to] + b[:, to]).astype(bf16)
            keep[p][u % RING, spot] = a[:, stay] + b[:, stay]
            return 0

        lax.fori_loop(0, line, body, 0)
        copies.start(base + u * per_unit + 1, halves_out[p].at[u], halves_in[p].at[u], at.twin(p))

    def later(u, j):
        p = bits - 1 - j
        copies.arrived(base + u * per_unit + 1 + j, halves_in[p].at[u], at.twin(p))
        if p > 0:
            half = width << (p - 1)
            side = lax.rem(lax.div(at.block, 1 << (p - 1)), 2)
            to, stay = run(1 - side, 1, half), run(side, 1, half)

            def body(spot, _):
                a = keep[p].at[u % RING, spot]
                b = halves_in[p].at[u, spot]
                halves_out[p - 1][u, spot] = (a[:, to] + b[:, to].astype(f32)).astype(bf16)
                keep[p - 1][u % RING, spot] = a[:, stay] + b[:, stay].astype(f32)
                return 0

            lax.fori_loop(0, line, body, 0)
            copies.start(
                base + u * per_unit + 2 + j, halves_out[p - 1].at[u], halves_in[p - 1].at[u], at.twin(p - 1)
            )
            return
        for d in range(1, line):
            spot = at.ahead(d)
            line_out[u, d - 1] = keep[0][u % RING, spot] + halves_in[0][u, spot].astype(f32)
            copies.start(base + u * per_unit + bits + d, line_out.at[u, d - 1], line_in.at[u, d - 1], at.along(d))
        final[u % RING] = keep[0][u % RING, at.spot] + halves_in[0][u, at.spot].astype(f32)

    def spread(u, p):
        slot = base + u * per_unit + bits + line
        if p == 0:
            value = final[u % RING]
            for d in range(1, line):
                copies.arrived(slot - line + d, line_in.at[u, d - 1], at.along(d))
                value = value + line_in[u, d - 1]
            total[u, :, run(at.hold(0), 1, width)] = value
        else:
            got = run(at.other(p - 1), 1 << (p - 1), width)
            copies.arrived(slot + p - 1, total.at[u, :, got], at.twin(p - 1))
        if p < bits:
            piece = total.at[u, :, run(at.hold(p), 1 << p, width)]
            copies.start(slot + p, piece, piece, at.twin(p))

    def vec_first():
        value = vec_part[at.shard]
        for d in range(1, n_shard):
            copies.arrived(vec_slot + d, vec_got.at[d], at.group(d))
            value = value + vec_got[d]
        vec_all[at.rep] = value
        for d in range(1, n_rep):
            copies.start(vec_slot_rep + d, vec_all.at[at.rep], vec_all.at[at.rep], at.replica(d))

    def vec_last():
        for d in range(1, n_rep):
            copies.arrived(vec_slot_rep + d, vec_all.at[lax.rem(at.rep + n_rep - d, n_rep)], at.replica(d))
        value = vec_all[0]
        for i in range(1, n_rep):
            value = value + vec_all[i]
        vec_sum[...] = value

    stages = [fetch, first]
    stages += [functools.partial(later, j=j) for j in range(bits)]
    stages += [functools.partial(spread, p=p) for p in range(bits + 1)]
    for t in range(UNITS + len(stages) - 1):
        for i, do in enumerate(stages):
            if 0 <= t - i < UNITS:
                do(t - i)
        if t == 2:
            vec_first()
    vec_last()
    copies.drain()


def reduce(early, late, vec_part, n_rep, n_shard):
    rows, line, bits = early.shape[3], n_shard // 2, n_rep.bit_length() - 1
    slots = UNITS * (1 + bits + line - 1 + bits) + n_shard + n_rep
    width = WIDE // n_rep
    anywhere = pl.BlockSpec(memory_space=pl.ANY)
    vmem = pl.BlockSpec(memory_space=pltpu.VMEM)
    vec_shape = vec_part.shape[1:]
    total, vec_sum, _ = pl.pallas_call(
        functools.partial(reduce_kernel, n_rep, n_shard),
        out_shape=(
            jax.ShapeDtypeStruct((UNITS, rows, WIDE), f32),
            jax.ShapeDtypeStruct(vec_shape, f32),
            jax.ShapeDtypeStruct((UNITS, line, rows, WIDE), f32),
        ),
        in_specs=[anywhere, anywhere, vmem],
        out_specs=(vmem, vmem, anywhere),
        scratch_shapes=[
            pltpu.VMEM((n_shard,) + vec_shape, f32),
            pltpu.VMEM((n_rep,) + vec_shape, f32),
            pltpu.VMEM((2, line, rows, WIDE), f32),
            pltpu.VMEM((2, line, rows, WIDE), f32),
            [pltpu.VMEM((RING, line, rows, width << p), f32) for p in range(bits)],
            [pltpu.VMEM((UNITS, line, rows, width << p), bf16) for p in range(bits)],
            [pltpu.VMEM((UNITS, line, rows, width << p), bf16) for p in range(bits)],
            pltpu.VMEM((UNITS, line - 1, rows, width), f32),
            pltpu.VMEM((UNITS, line - 1, rows, width), f32),
            pltpu.VMEM((RING, rows, width), f32),
            pltpu.SemaphoreType.DMA((slots,)),
            pltpu.SemaphoreType.DMA((slots,)),
            pltpu.SemaphoreType.DMA((2, 2)),
        ],
        compiler_params=pltpu.CompilerParams(
            collective_id=1, has_side_effects=True, vmem_limit_bytes=60 * 2**20
        ),
        name="reduce_gradients",
    )(early, late, vec_part)
    return total, vec_sum


def lanes(vec, parts):
    return jnp.pad(vec.reshape(parts, VEC_ROWS, -1), ((0, 0), (0, 16 - VEC_ROWS), (0, 0)))


def unshuffle(cols, n_shard):
    return cols.reshape(cols.shape[0], 4, n_shard, -1).transpose(0, 2, 1, 3).reshape(cols.shape[0], FF)


def to_units(qkv, out, fc1, fc2, n_shard):
    rows = out.shape[0]
    up = fc1.reshape(rows, n_shard, 4, -1).transpose(2, 0, 1, 3).reshape(4, 1, rows, WIDE)
    down = fc2.reshape(4, 1, rows, WIDE)
    pairs = jnp.concatenate([up, down], axis=1).reshape(8, rows, WIDE)
    return jnp.concatenate([pairs, qkv.reshape(rows, 3, WIDE).transpose(1, 0, 2), out[None]])


def from_units(units, n_shard):
    rows = units.shape[1]
    up = unshuffle(units[0:8:2].transpose(1, 0, 2).reshape(rows, FF), n_shard)
    return units[8:11].transpose(1, 0, 2).reshape(rows, 3 * D), units[11], up, units[1:8:2].reshape(4 * rows, WIDE)


def rotary_tables(positions):
    half = ROT // 2
    freqs = 10000.0 ** (-jnp.arange(half).astype(f32) * 2.0 / ROT)
    angle = jnp.maximum(positions, 0).astype(f32)[:, None] * freqs[None, :]
    cosine, sine = jnp.cos(angle), jnp.sin(angle)
    one, none = jnp.ones_like(cosine), jnp.zeros_like(cosine)
    rest = HD // half - 2
    return (
        jnp.concatenate(([cosine, cosine] + [one] * rest) * 2, axis=1),
        jnp.concatenate(([-sine, none] + [none] * rest) * 2, axis=1),
        jnp.concatenate(([none, sine] + [none] * rest) * 2, axis=1),
    )


def adam(master, first, second, grad, rate, decay_on):
    first_new = beta_one * first + (1.0 - beta_one) * grad
    second_new = beta_two * second + (1.0 - beta_two) * grad * grad
    mhat = first_new / (1.0 - beta_one**STEP)
    vhat = second_new / (1.0 - beta_two**STEP)
    new = master - rate * (mhat / (jnp.sqrt(vhat) + epsilon) + decay_on * master)
    return (first_new, second_new, new)


def shards(
    tokens,
    cotangent,
    positions,
    qkv_master,
    qkv_first,
    qkv_second,
    out_master,
    out_first,
    out_second,
    fc1_master,
    fc1_first,
    fc1_second,
    fc2_master,
    fc2_first,
    fc2_second,
    vec_master,
    vec_first,
    vec_second,
):
    n_rep, n_shard = lax.axis_size("rep"), lax.axis_size("shard")
    own = to_units(
        qkv_master.astype(bf16), out_master.astype(bf16), fc1_master.astype(bf16), fc2_master.astype(bf16), n_shard
    )
    valid = (positions >= 0).astype(f32)[:, None]
    vec_own = lanes(vec_master.astype(bf16).astype(f32), 1)[0]
    late, early_grads, rows, part, d_two, act_one, grad_low, vec_early = mlp(
        own, vec_own, tokens, cotangent, valid, n_rep, n_shard
    )
    output, input_grad, late_grads, vec_late = attention(
        late, rows, act_one, grad_low, tokens, cotangent, valid, part, d_two, positions[None], rotary_tables(positions)
    )
    grad_sum = vec_early[4]
    grad_vec = jnp.concatenate(
        [vec_late[:7].reshape(-1), grad_sum, unshuffle(vec_early[:4].reshape(1, FF), n_shard)[0], grad_sum]
    )
    total, vec_sum = reduce(early_grads, late_grads, lanes(grad_vec, n_shard), n_rep, n_shard)
    owned_qkv, owned_out, owned_fc1, owned_fc2 = from_units(total, n_shard)
    owned_vec = vec_sum[:VEC_ROWS].reshape(-1)
    qf, qs, qn = adam(qkv_master, qkv_first, qkv_second, owned_qkv, 0.5 * D ** (-0.5), weight_decay)
    of, osec, on = adam(
        out_master, out_first, out_second, owned_out, 0.5 * (32.0 / D) ** 0.5, weight_decay
    )
    f1f, f1s, f1n = adam(
        fc1_master, fc1_first, fc1_second, owned_fc1, 0.5 * D ** (-0.5), weight_decay
    )
    f2f, f2s, f2n = adam(
        fc2_master, fc2_first, fc2_second, owned_fc2, 0.5 * FF ** (-0.5), weight_decay
    )
    vf, vs, vn = adam(vec_master, vec_first, vec_second, owned_vec, vector_rate, 0.0)
    return (output, input_grad, qf, qs, qn, of, osec, on, f1f, f1s, f1n, f2f, f2s, f2n, vf, vs, vn)


def solution(mesh):
    rows, owned, slots = P(("rep", "shard"), None), P("shard", None), P(("rep", "shard"))
    vector = P("shard")
    return jax.shard_map(
        shards,
        mesh=mesh,
        in_specs=(rows, rows, slots) + (owned,) * 12 + (vector,) * 3,
        out_specs=(rows, rows) + (owned,) * 12 + (vector,) * 3,
        check_vma=False,
    )
```

```python
import functools
import math

import jax
import jax.numpy as jnp
from jax import lax
from jax.experimental import pallas as pl
from jax.experimental.pallas import tpu as pltpu
from jax.sharding import PartitionSpec as P

D = 1024
H = 16
HD = 64
FF = 4096
ROT = 16
STEP = 10

beta_one = 0.9
beta_two = 0.95
epsilon = 1e-08
weight_decay = 0.1
norm_eps = 1e-05
vector_rate = 0.1

MESH = pl.DeviceIdType.MESH
LANES = 128
UNITS = 12
WIDE = 1024
TILE = 256
EARLY = 8
PIECES = 24
STAGES = 4
SLOTS = 4
RING = 4
VEC_ROWS = 13
f32 = jnp.float32
bf16 = jnp.bfloat16


def dot(a, b):
    return jnp.dot(a, b, preferred_element_type=f32)


def dot_nt(a, b):
    return lax.dot_general(a, b, (((1,), (1,)), ((), ())), preferred_element_type=f32)


def dot_tn(a, b):
    return lax.dot_general(a, b, (((0,), (0,)), ((), ())), preferred_element_type=f32)


def run(first, count, width):
    return pl.ds(pl.multiple_of(first * width, LANES), count * width)


class Place:
    def __init__(self, n_rep, n_shard):
        self.n_rep, self.n_shard = n_rep, n_shard
        self.line = n_shard // 2
        self.bits = n_rep.bit_length() - 1
        self.rep = lax.axis_index("rep")
        self.shard = lax.axis_index("shard")
        self.core = lax.rem(self.shard, 2)
        self.spot = lax.div(self.shard, 2)
        digits = [lax.rem(lax.div(self.rep, 1 << p), 2) for p in range(self.bits)]
        turned = sum(digits[p] * (1 << (self.bits - 1 - p)) for p in range(self.bits))
        self.block = (1 - self.core) * self.rep + self.core * turned
        self.twins = []
        for p in range(self.bits):
            q = self.bits - 1 - p
            step_even = (1 - 2 * digits[p]) * (1 << p)
            step_odd = (1 - 2 * digits[q]) * (1 << q)
            self.twins.append(self.rep + (1 - self.core) * step_even + self.core * step_odd)

    def hold(self, p):
        return lax.div(self.block, 1 << p) * (1 << p)

    def other(self, p):
        mine = lax.div(self.block, 1 << p)
        return (mine + 1 - 2 * lax.rem(mine, 2)) * (1 << p)

    def ahead(self, d):
        return lax.rem(self.spot + d, self.line)

    def behind(self, d):
        return lax.rem(self.spot + self.line - d, self.line)

    def along(self, d):
        return (self.rep, 2 * self.ahead(d) + self.core)

    def sibling(self):
        return (self.rep, self.shard + 1 - 2 * self.core)

    def twin(self, p):
        return (self.twins[p], self.shard)

    def group(self, d):
        return (self.rep, lax.rem(self.shard + d, self.n_shard))

    def replica(self, d):
        return (lax.rem(self.rep + d, self.n_rep), self.shard)

    def greet(self):
        barrier = pltpu.get_barrier_semaphore()
        peers = [self.group(d) for d in range(1, self.n_shard)]
        peers += [self.replica(d) for d in range(1, self.n_rep)]
        for peer in peers:
            pl.semaphore_signal(barrier, inc=1, device_id=peer, device_id_type=MESH)
        pl.semaphore_wait(barrier, len(peers))


class Copies:
    def __init__(self, send, recv):
        self.send, self.recv, self.used, self.sent = send, recv, 0, []

    def take(self, count):
        self.used += count
        return self.used - count

    def make(self, slot, src, dst, peer):
        return pltpu.make_async_remote_copy(
            src_ref=src,
            dst_ref=dst,
            send_sem=self.send.at[slot],
            recv_sem=self.recv.at[slot],
            device_id=peer,
            device_id_type=MESH,
        )

    def start(self, slot, src, dst, peer):
        copy = self.make(slot, src, dst, peer)
        copy.start()
        self.sent.append(copy)

    def arrived(self, slot, dst, peer):
        self.make(slot, dst, dst, peer).wait_recv()

    def drain(self):
        for copy in self.sent:
            copy.wait_send()


class Gather:
    def __init__(self, at, copies, own, full):
        self.at, self.copies, self.own, self.full = at, copies, own, full
        self.width = WIDE // at.n_rep
        self.per_unit = (at.line - 1) * (at.bits + 1) + at.line
        self.base = copies.take(self.per_unit * UNITS)

    def slot(self, u, p):
        return self.base + u * self.per_unit + p * (self.at.line - 1)

    def line_sends(self, u):
        at, mine = self.at, run(self.at.hold(0), 1, self.width)
        return [
            self.copies.make(
                self.slot(u, 0) + d - 1,
                self.own.at[u, :, mine],
                self.full.at[u, at.spot, at.core, :, mine],
                at.along(d),
            )
            for d in range(1, at.line)
        ]

    def twin_send(self, u, p, d):
        at = self.at
        piece = self.full.at[u, at.behind(d), at.core, :, run(at.hold(p), 1 << p, self.width)]
        return self.copies.make(self.slot(u, p + 1) + d - 1, piece, piece, at.twin(p))

    def sibling_send(self, u, d):
        at = self.at
        piece = self.full.at[u, at.behind(d), at.core]
        return self.copies.make(
            self.slot(u, at.bits + 1) + d, self.own.at[u] if d == 0 else piece, piece, at.sibling()
        )

    def stage(self, u, p):
        at = self.at
        if p == at.bits + 1:
            for d in range(at.line):
                self.copies.arrived(
                    self.slot(u, p) + d, self.full.at[u, at.behind(d), 1 - at.core], at.sibling()
                )
            return
        if p == at.bits:
            self.sibling_send(u, 0).start()
        for d in range(1, at.line):
            got = run(at.other(p - 1), 1 << (p - 1), self.width) if p > 0 else run(at.hold(0), 1, self.width)
            self.copies.arrived(
                self.slot(u, p) + d - 1,
                self.full.at[u, at.behind(d), at.core, :, got],
                at.twin(p - 1) if p > 0 else at.along(d),
            )
            if p < at.bits:
                self.twin_send(u, p, d).start()
            else:
                self.sibling_send(u, d).start()

    def drain(self, u):
        at = self.at
        for copy in self.line_sends(u):
            copy.wait_send()
        for p in range(at.bits):
            for d in range(1, at.line):
                self.twin_send(u, p, d).wait_send()
        for d in range(at.line):
            self.sibling_send(u, d).wait_send()


def vector_places(n_shard, lane):
    places = []
    for row in range(VEC_ROWS):
        for q in range(WIDE // lane):
            if 8 <= row < 12:
                start = 8 * WIDE + q * (FF // n_shard) + (row - 8) * lane
            else:
                start = row * WIDE + q * lane
            places.append((row, q * lane, start // lane // VEC_ROWS, start // lane % VEC_ROWS))
    return places


def mlp_kernel(
    n_rep, n_shard, own, vec_own, tokens, cot, valid,
    late, grads, rows_out, part, d_two, act_one, grad_low, grad_vec,
    full, vec_full, act_two, act_two_t, act, d_hidden, stage_grads, send, recv, local,
):
    at = Place(n_rep, n_shard)
    line, bits = at.line, at.bits
    shard_rows = own.shape[1]
    tall = TILE // (2 * shard_rows)
    tokens_here = tokens.shape[0]
    lane = vec_own.shape[1]
    at.greet()
    copies = Copies(send, recv)
    gather = Gather(at, copies, own, full)
    vec_slot = copies.take(n_shard)
    for d in range(1, n_shard):
        copies.start(vec_slot + d, vec_own, vec_full.at[at.shard], at.group(d))

    def begin(u, _):
        for copy in gather.line_sends(u):
            copy.start()
        pltpu.make_async_copy(own.at[u], full.at[u, at.spot, at.core], local.at[u]).start()
        return 0

    lax.fori_loop(0, UNITS, begin, 0)
    vec_full[at.shard] = vec_own[...]

    sums = jnp.zeros((1, WIDE), f32)
    step = 64

    def lower(i, sums):
        rows = pl.ds(pl.multiple_of(i * step, step), step)
        low = (cot[rows] * valid[rows]).astype(bf16)
        grad_low[rows] = low
        d_two[rows] = jnp.zeros((step, WIDE), f32)
        return sums + jnp.sum(low.astype(f32), axis=0, keepdims=True)

    grad_vec[4:5] = lax.fori_loop(0, tokens_here // step, lower, sums)

    for d in range(1, n_shard):
        copies.arrived(vec_slot + d, vec_full.at[lax.rem(at.shard + n_shard - d, n_shard)], at.group(d))
    for row, first, device, place in vector_places(n_shard, lane):
        rows_out[row : row + 1, first : first + lane] = vec_full[device, place : place + 1, :]

    def norm(i, _):
        rows = pl.ds(pl.multiple_of(i * step, step), step)
        x = tokens[rows].astype(f32)
        centred = x - jnp.mean(x, axis=-1, keepdims=True)
        var = jnp.mean(centred * centred, axis=-1, keepdims=True)
        unit = centred * lax.rsqrt(var + norm_eps)
        act_one[rows] = (unit * rows_out[0:1] + rows_out[1:2]).astype(bf16)
        act_two[rows] = (unit * rows_out[2:3] + rows_out[3:4]).astype(bf16)
        part[rows] = x + rows_out[12:13]
        return 0

    lax.fori_loop(0, tokens_here // step, norm, 0)
    act_two_t[...] = act_two[...].T

    stages = bits + 2

    def steps_of(t):
        return [(t - p, p) for p in range(stages)]

    def guarded(u, p):
        if isinstance(u, int):
            if 0 <= u < UNITS:
                gather.stage(u, p)
        else:
            pl.when(u < UNITS)(lambda: gather.stage(u, p))

    def here(u):
        return pltpu.make_async_copy(own.at[u], full.at[u, at.spot, at.core], local.at[u])

    for t in range(stages + 1):
        for u, p in steps_of(t):
            guarded(u, p)

    def out_copy(k, u):
        return pltpu.make_async_copy(stage_grads.at[k], grads.at[u], local.at[UNITS + k])

    def tile(j, _):
        u1, u2 = 2 * j, 2 * j + 1
        here(u1).wait()
        here(u2).wait()
        jobs = steps_of(stages + 1 + 2 * j) + steps_of(stages + 2 + 2 * j)

        def comm(q):
            for u, p in jobs[q * len(jobs) // 8 : (q + 1) * len(jobs) // 8]:
                guarded(u, p)

        for q in range(4):
            comm(q)
            cols = slice(q * TILE, (q + 1) * TILE)
            spots = slice(q * tall, (q + 1) * tall)
            w1 = full[u1, :, :, :, cols].reshape(D, TILE)
            h = dot(act_two[...], w1) + rows_out[pl.ds(8 + j, 1), cols]
            below = 0.5 + 0.5 * lax.erf(h * (0.5**0.5))
            act[:, cols] = (h * below).astype(bf16)
            slope = below + h * (jnp.exp(-0.5 * h * h) * (1.0 / math.sqrt(2.0 * math.pi)))
            w2 = full[u2, spots].reshape(TILE, D)
            dh = (dot_nt(grad_low[...], w2) * slope).astype(bf16)
            d_hidden[:, cols] = dh
            grad_vec[pl.ds(j, 1), cols] = jnp.sum(dh.astype(f32), axis=0, keepdims=True)
        for q in range(4):
            comm(4 + q)
            cols = slice(q * TILE, (q + 1) * TILE)
            spots = slice(q * tall, (q + 1) * tall)
            if q == 0:

                @pl.when(j > 0)
                def _():
                    out_copy(0, 0).wait()
                    out_copy(1, 0).wait()

            part[:, cols] += dot(act[...], full[u2, :, :, :, cols].reshape(D, TILE))
            d_two[:, cols] += dot_nt(d_hidden[...], full[u1, spots].reshape(TILE, WIDE))
            stage_grads[1, spots] = dot_tn(act[:, cols], grad_low[...]).reshape(tall, 2, shard_rows, WIDE)
            stage_grads[0, spots] = dot(act_two_t[cols], d_hidden[...]).reshape(tall, 2, shard_rows, WIDE)
        out_copy(0, u1).start()
        out_copy(1, u2).start()
        return 0

    lax.fori_loop(0, 4, tile, 0)
    for t in range(stages + 9, UNITS + stages - 1):
        for u, p in steps_of(t):
            guarded(u, p)
    for u in range(8, UNITS):
        here(u).wait()
        pltpu.make_async_copy(full.at[u], late.at[u - 8], local.at[u]).start()
    out_copy(0, 0).wait()
    out_copy(1, 0).wait()
    for u in range(8, UNITS):
        pltpu.make_async_copy(full.at[u], late.at[u - 8], local.at[u]).wait()

    def finish(u, _):
        gather.drain(u)
        return 0

    lax.fori_loop(0, UNITS, finish, 0)
    copies.drain()


def mlp(own, vec_own, tokens, cot, valid, n_rep, n_shard):
    shard_rows, line, bits = own.shape[1], n_shard // 2, n_rep.bit_length() - 1
    slots = UNITS * ((line - 1) * (bits + 1) + line) + n_shard
    count = tokens.shape[0]
    anywhere = pl.BlockSpec(memory_space=pl.ANY)
    vmem = pl.BlockSpec(memory_space=pltpu.VMEM)
    unit = (line, 2, shard_rows, WIDE)
    return pl.pallas_call(
        functools.partial(mlp_kernel, n_rep, n_shard),
        out_shape=(
            jax.ShapeDtypeStruct((4,) + unit, bf16),
            jax.ShapeDtypeStruct((8,) + unit, f32),
            jax.ShapeDtypeStruct((16, WIDE), f32),
            jax.ShapeDtypeStruct((count, WIDE), f32),
            jax.ShapeDtypeStruct((count, WIDE), f32),
            jax.ShapeDtypeStruct((count, WIDE), bf16),
            jax.ShapeDtypeStruct((count, WIDE), bf16),
            jax.ShapeDtypeStruct((8, WIDE), f32),
        ),
        in_specs=[anywhere, vmem, vmem, vmem, vmem],
        out_specs=(anywhere, anywhere, vmem, vmem, vmem, vmem, vmem, vmem),
        scratch_shapes=[
            pltpu.VMEM((UNITS,) + unit, bf16),
            pltpu.VMEM((n_shard,) + vec_own.shape, f32),
            pltpu.VMEM((count, WIDE), bf16),
            pltpu.VMEM((WIDE, count), bf16),
            pltpu.VMEM((count, WIDE), bf16),
            pltpu.VMEM((count, WIDE), bf16),
            pltpu.VMEM((2,) + unit, f32),
            pltpu.SemaphoreType.DMA((slots,)),
            pltpu.SemaphoreType.DMA((slots,)),
            pltpu.SemaphoreType.DMA((UNITS + 2,)),
        ],
        compiler_params=pltpu.CompilerParams(
            collective_id=0, has_side_effects=True, vmem_limit_bytes=60 * 2**20
        ),
        name="gather_and_mlp",
    )(own, vec_own, tokens, cot, valid)


def turn(u, tables, sign):
    cosine, up, down = tables
    return u * cosine + sign * (pltpu.roll(u, LANES - ROT // 2, 1) * up + pltpu.roll(u, ROT // 2, 1) * down)


class Reduce:
    def __init__(self, at, copies, early, late, sib, bufs, local):
        self.at, self.copies, self.early, self.late, self.sib, self.local = at, copies, early, late, sib, local
        (self.mine_buf, self.sib_buf, self.keep, self.halves_out, self.halves_in,
         self.line_out, self.line_in, self.final, self.total) = bufs
        self.width = WIDE // at.n_rep
        self.half = early.shape[3] // 2
        self.per_piece = 1 + at.bits + (at.line - 1) + at.bits
        self.base = copies.take(self.per_piece * PIECES)
        self.stages = [self.fetch, self.first]
        self.stages += [functools.partial(self.later, j=j) for j in range(at.bits)]
        self.stages += [functools.partial(self.spread, p=p) for p in range(at.bits + 1)]
        self.lags = [0, 1] + [1 + 2 * (i + 1) for i in range(len(self.stages) - 2)]
        self.depth = self.lags[-1] + 1

    def slot(self, v, k):
        return self.base + v * self.per_piece + k

    def rows(self, v):
        return pl.ds(pl.multiple_of(lax.rem(v, 2) * self.half, self.half), self.half)

    def source(self, v, core):
        if isinstance(v, int) and v >= 2 * EARLY:
            return self.late.at[v // 2 - EARLY, :, core, pl.ds((v % 2) * self.half, self.half)]
        return self.early.at[lax.div(v, 2), :, core, self.rows(v)]

    def sums(self, v, first, count):
        return self.total.at[lax.div(v, 2), self.rows(v), run(first, count, self.width)]

    def sibling_copy(self, v):
        return self.copies.make(self.slot(v, 0), self.source(v, 1 - self.at.core), self.sib.at[v], self.at.sibling())

    def twin_copy(self, v, p):
        ring = lax.rem(v, RING)
        return self.copies.make(
            self.slot(v, self.at.bits - p), self.halves_out[p].at[ring], self.halves_in[p].at[ring], self.at.twin(p)
        )

    def line_copy(self, v, d):
        ring = lax.rem(v, RING)
        return self.copies.make(
            self.slot(v, self.at.bits + d),
            self.line_out.at[ring, d - 1],
            self.line_in.at[ring, d - 1],
            self.at.along(d),
        )

    def spread_copy(self, v, p):
        piece = self.sums(v, self.at.hold(p), 1 << p)
        return self.copies.make(self.slot(v, self.at.bits + self.at.line + p), piece, piece, self.at.twin(p))

    def loads(self, v):
        return (
            pltpu.make_async_copy(self.source(v, self.at.core), self.mine_buf, self.local.at[0]),
            pltpu.make_async_copy(self.sib.at[v], self.sib_buf, self.local.at[1]),
        )

    def reuse(self, v, copies):
        def wait():
            for copy in copies(v - RING):
                copy.wait_send()

        if isinstance(v, int):
            if v >= RING:
                wait()
        else:
            pl.when(v >= RING)(wait)

    def fetch(self, v):
        self.sibling_copy(v).wait_recv()
        for copy in self.loads(v):
            copy.start()

    def first(self, v):
        at, width = self.at, self.width
        for copy in self.loads(v):
            copy.wait()
        p = at.bits - 1
        self.reuse(v, lambda w: [self.twin_copy(w, p)])
        to, stay = run(at.other(p), 1 << p, width), run(at.hold(p), 1 << p, width)
        ring = lax.rem(v, RING)

        def body(spot, _):
            a, b = self.mine_buf.at[spot], self.sib_buf.at[spot]
            self.halves_out[p][ring, spot] = (a[:, to] + b[:, to]).astype(bf16)
            self.keep[p][ring, spot] = a[:, stay] + b[:, stay]
            return 0

        lax.fori_loop(0, at.line, body, 0)
        self.twin_copy(v, p).start()

    def later(self, v, j):
        at = self.at
        p = at.bits - 1 - j
        ring = lax.rem(v, RING)
        self.twin_copy(v, p).wait_recv()
        if p > 0:
            self.reuse(v, lambda w: [self.twin_copy(w, p - 1)])
            half = self.width << (p - 1)
            side = lax.rem(lax.div(at.block, 1 << (p - 1)), 2)
            to, stay = run(1 - side, 1, half), run(side, 1, half)

            def body(spot, _):
                a, b = self.keep[p].at[ring, spot], self.halves_in[p].at[ring, spot]
                self.halves_out[p - 1][ring, spot] = (a[:, to] + b[:, to].astype(f32)).astype(bf16)
                self.keep[p - 1][ring, spot] = a[:, stay] + b[:, stay].astype(f32)
                return 0

            lax.fori_loop(0, at.line, body, 0)
            self.twin_copy(v, p - 1).start()
            return
        self.reuse(v, lambda w: [self.line_copy(w, d) for d in range(1, at.line)])
        for d in range(1, at.line):
            spot = at.ahead(d)
            self.line_out[ring, d - 1] = self.keep[0][ring, spot] + self.halves_in[0][ring, spot].astype(f32)
            self.line_copy(v, d).start()
        self.final[ring] = self.keep[0][ring, at.spot] + self.halves_in[0][ring, at.spot].astype(f32)

    def spread(self, v, p):
        at = self.at
        if p == 0:
            ring = lax.rem(v, RING)
            value = self.final[ring]
            for d in range(1, at.line):
                self.line_copy(v, d).wait_recv()
                value = value + self.line_in[ring, d - 1]
            self.total[lax.div(v, 2), self.rows(v), run(at.hold(0), 1, self.width)] = value
        else:
            got = self.sums(v, at.other(p - 1), 1 << (p - 1))
            self.copies.make(self.slot(v, at.bits + at.line + p - 1), got, got, at.twin(p - 1)).wait_recv()
        if p < at.bits:
            self.spread_copy(v, p).start()

    def jobs(self, t):
        out = []
        for i in reversed(range(len(self.stages))):
            v = t - self.lags[i]
            if isinstance(t, int):
                if 0 <= v < PIECES:
                    out.append(functools.partial(self.stages[i], v))
            else:
                out.append(functools.partial(lambda i, v: pl.when(v >= 0)(lambda: self.stages[i](v)), i, v))
        return out

    def drain(self):
        at = self.at
        for v in range(PIECES - RING, PIECES):
            for p in range(at.bits):
                self.twin_copy(v, p).wait_send()
            for d in range(1, at.line):
                self.line_copy(v, d).wait_send()

        def body(v, _):
            for p in range(at.bits):
                self.spread_copy(v, p).wait_send()
            return 0

        lax.fori_loop(0, PIECES, body, 0)

        def siblings(v, _):
            self.sibling_copy(v).wait_send()
            return 0

        lax.fori_loop(0, 2 * EARLY, siblings, 0)
        for v in range(2 * EARLY, PIECES):
            self.sibling_copy(v).wait_send()


def attention_kernel(
    n_rep, n_shard, early, late, rows_in, act_one, grad_low, tokens, cot, valid, part_in, d_two_in, positions,
    cosine, up, down, vec_early,
    output, input_grad, sums_out, vec_sum, late_grads, sib,
    weights, part, d_two, query, keys, values, d_mixed, mixed, d_qkv, act_one_t, bias, d_one, stage_grads,
    grad_vec, vec_part, vec_got, vec_all, reduce_bufs, send, recv, local,
):
    at = Place(n_rep, n_shard)
    count = tokens.shape[0]
    line, shard_rows = late.shape[1], late.shape[3]
    tall = TILE // (2 * shard_rows)
    step = 64
    scale = HD**-0.5

    def bring(k, src, dst):
        return pltpu.make_async_copy(src, dst, local.at[2 + k])

    inputs = [(late.at[j], weights.at[j]) for j in range(4)] + [(part_in, part), (d_two_in, d_two)]
    for k, (src, dst) in enumerate(inputs):
        bring(k, src, dst).start()
    at.greet()
    copies = Copies(send, recv)
    reduce = Reduce(at, copies, early, late_grads, sib, reduce_bufs, local)
    vec_slot = copies.take(n_shard)
    vec_slot_rep = copies.take(n_rep)

    def begin(v, _):
        reduce.sibling_copy(v).start()
        return 0

    lax.fori_loop(0, 2 * EARLY, begin, 0)
    total = reduce_bufs[-1]

    tables = (cosine[...], up[...], down[...])

    def weight(j, cols):
        return weights[j, :, :, :, cols].reshape(D, cols.stop - cols.start)

    key_idx = lax.broadcasted_iota(jnp.int32, (count, count), 0)
    query_idx = lax.broadcasted_iota(jnp.int32, (count, count), 1)
    allowed = (key_idx <= query_idx) & (key_idx >= query_idx - jnp.maximum(positions[...], 0))
    bias[...] = jnp.where(allowed, 0.0, -1e30)
    act_one_t[...] = act_one[...].T
    for k in range(4):
        bring(k, *inputs[k]).wait()

    queue = []
    clock = [0]

    def tick(number):
        for _ in range(number):
            while not queue:
                queue.extend(reduce.jobs(clock[0]))
                clock[0] += 1
            queue.pop(0)()

    def flush():
        while queue:
            queue.pop(0)()

    for q in range(4):
        if q % 2 == 0:
            queue.extend(reduce.jobs(clock[0]))
            clock[0] += 1
        flush()
        cols = slice(q * TILE, (q + 1) * TILE)
        spots = slice(q * tall, (q + 1) * tall)
        for j, target in enumerate((query, keys, values)):
            value = dot(act_one[...], weight(j, cols)) + rows_in[4 + j : 5 + j, cols]
            for half in range(TILE // LANES):
                piece = value[:, half * LANES : (half + 1) * LANES]
                if j < 2:
                    piece = turn(piece, tables, 1.0)
                piece = piece.astype(bf16)
                if j == 0:
                    piece = piece * jnp.asarray(scale, bf16)
                target[:, q * TILE + half * LANES : q * TILE + (half + 1) * LANES] = piece
        d_mixed[:, cols] = dot_nt(grad_low[...], weights[3, spots].reshape(TILE, WIDE)).astype(bf16)

    first_head = lax.broadcasted_iota(jnp.int32, (1, LANES), 1) < HD

    def pair(i):
        cols = pl.ds(pl.multiple_of(i * LANES, LANES), LANES)
        q2, k2, v2, o2 = query[:, cols], keys[:, cols], values[:, cols], d_mixed[:, cols]
        nothing = jnp.zeros((), bf16)
        blocks = count // TILE
        mixed_parts, dq_parts = [0.0] * blocks, [0.0] * blocks
        dk_parts, dv_parts = [0.0] * blocks, [0.0] * blocks
        for head in range(2):
            keep = first_head if head == 0 else jnp.logical_not(first_head)
            qm, km, vm, om = (jnp.where(keep, w, nothing) for w in (q2, k2, v2, o2))
            for b in range(blocks):
                span = slice(0, (b + 1) * TILE)
                mine = slice(b * TILE, (b + 1) * TILE)
                scores = dot_nt(k2[span], qm[mine]) + bias[span, mine]
                top = jnp.max(scores, axis=0, keepdims=True)
                expo = jnp.exp(scores - top)
                probs = expo * (1.0 / jnp.sum(expo, axis=0, keepdims=True))
                low = probs.astype(bf16)
                d_probs = dot_nt(v2[span], om[mine])
                inner = jnp.sum(probs * d_probs, axis=0, keepdims=True)
                d_scores = (probs * (d_probs - inner)).astype(bf16)
                mixed_parts[b] += dot_tn(low, vm[span])
                dq_parts[b] += dot_tn(d_scores, km[span])
                dv = dot(low, om[mine])
                dk = dot(d_scores, qm[mine])
                for c in range(b + 1):
                    dk_parts[c] += dk[c * TILE : (c + 1) * TILE]
                    dv_parts[c] += dv[c * TILE : (c + 1) * TILE]
        for b in range(blocks):
            mine = slice(b * TILE, (b + 1) * TILE)
            local_tables = (cosine[mine], up[mine], down[mine])
            mixed[mine, cols] = mixed_parts[b].astype(bf16)
            d_qkv[0, mine, cols] = turn(dq_parts[b] * scale, local_tables, -1.0).astype(bf16)
            d_qkv[1, mine, cols] = turn(dk_parts[b], local_tables, -1.0).astype(bf16)
            d_qkv[2, mine, cols] = dv_parts[b].astype(bf16)

    clock_here = clock[0]

    def two_pairs(i, _):
        jobs = reduce.jobs(clock_here + i)
        pair(2 * i)
        for job in jobs[: len(jobs) // 2]:
            job()
        pair(2 * i + 1)
        for job in jobs[len(jobs) // 2 :]:
            job()
        return 0

    lax.fori_loop(0, H // 4, two_pairs, 0)
    clock[0] += H // 4

    def out_copy(k):
        j, q = k // 4, k % 4
        spots = pl.ds(q * tall, tall)
        return pltpu.make_async_copy(
            stage_grads.at[k % STAGES], late_grads.at[j, spots], local.at[2 + len(inputs) + k % STAGES]
        )

    for k in range(16):
        j, q = k // 4, k % 4
        if k >= STAGES:
            out_copy(k - STAGES).wait()
        cols = slice(q * TILE, (q + 1) * TILE)
        if j < 3:
            value = dot(act_one_t[cols], d_qkv[j])
        else:
            value = dot_tn(mixed[:, cols], grad_low[...])
        stage_grads[k % STAGES] = value.reshape(tall, 2, shard_rows, WIDE)
        out_copy(k).start()
        if k % 2 == 1:
            tick(1)
    for k in range(16 - STAGES, 16):
        out_copy(k).wait()
    for v in range(2 * EARLY, PIECES):
        reduce.sibling_copy(v).start()
    bring(4, *inputs[4]).wait()
    bring(5, *inputs[5]).wait()
    for q in range(4):
        cols = slice(q * TILE, (q + 1) * TILE)
        spots = slice(q * tall, (q + 1) * tall)
        part[:, cols] += dot(mixed[...], weight(3, cols)) + rows_in[7:8, cols]
        value = dot_nt(d_qkv[0], weights[0, spots].reshape(TILE, WIDE))
        value += dot_nt(d_qkv[1], weights[1, spots].reshape(TILE, WIDE))
        value += dot_nt(d_qkv[2], weights[2, spots].reshape(TILE, WIDE))
        d_one[:, cols] = value
        tick(2)
    pltpu.make_async_copy(part, output, local.at[2]).start()
    for j in range(3):
        grad_vec[4 + j : 5 + j] = jnp.sum(d_qkv[j].astype(f32), axis=0, keepdims=True)

    def norm_back(i, sums):
        mine = pl.ds(pl.multiple_of(i * step, step), step)
        x = tokens[mine].astype(f32)
        centred = x - jnp.mean(x, axis=-1, keepdims=True)
        var = jnp.mean(centred * centred, axis=-1, keepdims=True)
        spread = lax.rsqrt(var + norm_eps)
        unit = centred * spread
        one, two = d_one[mine], d_two[mine]
        d_unit = one * rows_in[0:1] + two * rows_in[2:3]
        flat = jnp.mean(d_unit, axis=-1, keepdims=True)
        tilt = jnp.mean(d_unit * unit, axis=-1, keepdims=True)
        d_two[mine] = cot[mine] * valid[mine] + spread * (d_unit - flat - unit * tilt)
        return tuple(
            s + jnp.sum(w, axis=0, keepdims=True) for s, w in zip(sums, (one * unit, one, two * unit, two))
        )

    sums = lax.fori_loop(0, count // step, norm_back, (jnp.zeros((1, WIDE), f32),) * 4)
    for k in range(4):
        grad_vec[k : k + 1] = sums[k]
    pltpu.make_async_copy(d_two, input_grad, local.at[3]).start()
    grad_vec[7:8] = vec_early[4:5]
    grad_vec[8:12] = vec_early[0:4]
    grad_vec[12:13] = vec_early[4:5]
    lane = vec_sum.shape[1]
    for row, start, device, place in vector_places(n_shard, lane):
        vec_part[device, place : place + 1, :] = grad_vec[row : row + 1, start : start + lane]
    for d in range(1, n_shard):
        to = lax.rem(at.shard + d, n_shard)
        copies.start(vec_slot + d, vec_part.at[to], vec_got.at[d], at.group(d))

    def vec_first():
        value = vec_part[at.shard]
        for d in range(1, n_shard):
            copies.arrived(vec_slot + d, vec_got.at[d], at.group(d))
            value = value + vec_got[d]
        vec_all[at.rep] = value
        for d in range(1, n_rep):
            copies.start(vec_slot_rep + d, vec_all.at[at.rep], vec_all.at[at.rep], at.replica(d))

    def vec_last():
        for d in range(1, n_rep):
            copies.arrived(vec_slot_rep + d, vec_all.at[lax.rem(at.rep + n_rep - d, n_rep)], at.replica(d))
        value = vec_all[0]
        for i in range(1, n_rep):
            value = value + vec_all[i]
        vec_sum[...] = value

    def result(u):
        return pltpu.make_async_copy(total.at[u], sums_out.at[u], local.at[2 + len(inputs) + STAGES + u])

    done = 0
    while queue or clock[0] < PIECES + reduce.depth - 1:
        tick(len(queue) or 1)
        flush()
        if clock[0] == 2 * EARLY:
            vec_first()
        if clock[0] == 2 * EARLY + 4:
            vec_last()
        while done < min(UNITS, (clock[0] - reduce.depth + 1) // 2):
            result(done).start()
            done += 1
    for u in range(UNITS):
        result(u).wait()
    reduce.drain()
    copies.drain()
    pltpu.make_async_copy(part, output, local.at[2]).wait()
    pltpu.make_async_copy(d_two, input_grad, local.at[3]).wait()


def attention(
    early, late, rows, act_one, grad_low, tokens, cot, valid, part, d_two, positions, tables, vec_early, lane,
    n_rep, n_shard,
):
    count = tokens.shape[0]
    unit = late.shape[1:]
    line, _, shard_rows, _ = unit
    bits, width, half = n_rep.bit_length() - 1, WIDE // n_rep, shard_rows // 2
    slots = PIECES * (1 + bits + line - 1 + bits) + n_shard + n_rep
    anywhere = pl.BlockSpec(memory_space=pl.ANY)
    vmem = pl.BlockSpec(memory_space=pltpu.VMEM)
    flat = lambda: pltpu.VMEM((count, WIDE), bf16)
    outs = pl.pallas_call(
        functools.partial(attention_kernel, n_rep, n_shard),
        out_shape=(
            jax.ShapeDtypeStruct((count, WIDE), f32),
            jax.ShapeDtypeStruct((count, WIDE), f32),
            jax.ShapeDtypeStruct((UNITS, shard_rows, WIDE), f32),
            jax.ShapeDtypeStruct((16, lane), f32),
            jax.ShapeDtypeStruct((4,) + unit, f32),
            jax.ShapeDtypeStruct((PIECES, line, half, WIDE), f32),
        ),
        in_specs=[anywhere, anywhere] + [vmem] * 6 + [anywhere, anywhere] + [vmem] * 5,
        out_specs=(anywhere, anywhere, anywhere, vmem, anywhere, anywhere),
        scratch_shapes=[
            pltpu.VMEM((4,) + unit, bf16),
            pltpu.VMEM((count, WIDE), f32),
            pltpu.VMEM((count, WIDE), f32),
            flat(), flat(), flat(), flat(), flat(),
            pltpu.VMEM((3, count, WIDE), bf16),
            pltpu.VMEM((WIDE, count), bf16),
            pltpu.VMEM((count, count), f32),
            pltpu.VMEM((count, WIDE), f32),
            pltpu.VMEM((STAGES, TILE // (2 * shard_rows)) + unit[1:], f32),
            pltpu.VMEM((16, WIDE), f32),
            pltpu.VMEM((n_shard, 16, lane), f32),
            pltpu.VMEM((n_shard, 16, lane), f32),
            pltpu.VMEM((n_rep, 16, lane), f32),
            [
                pltpu.VMEM((line, half, WIDE), f32),
                pltpu.VMEM((line, half, WIDE), f32),
                [pltpu.VMEM((RING, line, half, width << p), f32) for p in range(bits)],
                [pltpu.VMEM((RING, line, half, width << p), bf16) for p in range(bits)],
                [pltpu.VMEM((RING, line, half, width << p), bf16) for p in range(bits)],
                pltpu.VMEM((RING, line - 1, half, width), f32),
                pltpu.VMEM((RING, line - 1, half, width), f32),
                pltpu.VMEM((RING, half, width), f32),
                pltpu.VMEM((UNITS, shard_rows, WIDE), f32),
            ],
            pltpu.SemaphoreType.DMA((slots,)),
            pltpu.SemaphoreType.DMA((slots,)),
            pltpu.SemaphoreType.DMA((2 + 6 + STAGES + UNITS,)),
        ],
        compiler_params=pltpu.CompilerParams(
            collective_id=1, has_side_effects=True, vmem_limit_bytes=62 * 2**20
        ),
        name="attention_and_sums",
    )(
        early, late, rows, act_one, grad_low, tokens, cot, valid, part, d_two, positions, *tables, vec_early
    )
    return outs[:4]


class Adam:
    def __init__(self, n_shard, states, results, ins, outs, total, sums, sems):
        self.states, self.results, self.ins, self.outs, self.total, self.sems = states, results, ins, outs, total, sems
        self.sums = sums
        self.rows = total.shape[1]
        lane = FF // n_shard // 4
        self.blocks = []
        share = n_shard // 4
        for k in range(4):
            runs = []
            for s in range(k * share, (k + 1) * share):
                for j in range(4):
                    runs.append((2 * j, s * lane, ((s - k * share) * 4 + j) * lane, lane))
            self.blocks.append((2, slice(0, self.rows), slice(k * WIDE, (k + 1) * WIDE), runs, 0.5 * D ** (-0.5)))
        for j in range(4):
            rows = slice(j * self.rows, (j + 1) * self.rows)
            self.blocks.append((3, rows, slice(0, WIDE), [(2 * j + 1, 0, 0, WIDE)], 0.5 * FF ** (-0.5)))
        for j in range(3):
            cols = slice(j * WIDE, (j + 1) * WIDE)
            runs = [(8 + j, 0, 0, WIDE)]
            self.blocks.append((0, slice(0, self.rows), cols, runs, 0.5 * D ** (-0.5)))
        runs = [(11, 0, 0, WIDE)]
        self.blocks.append((1, slice(0, self.rows), slice(0, WIDE), runs, 0.5 * (32.0 / D) ** 0.5))

    def load(self, i, k):
        kind, rows, cols = self.blocks[i][:3]
        return pltpu.make_async_copy(self.states[kind][k].at[rows, cols], self.ins.at[i % SLOTS, k], self.sems.at[0, i % SLOTS, k])

    def store(self, i, k):
        kind, rows, cols = self.blocks[i][:3]
        return pltpu.make_async_copy(self.outs.at[i % SLOTS, k], self.results[kind][k].at[rows, cols], self.sems.at[1, i % SLOTS, k])

    def grad(self, unit):
        return pltpu.make_async_copy(self.sums.at[unit], self.total.at[unit], self.sems.at[2, 0, unit])

    def begin(self, i):
        for k in range(3):
            self.load(i, k).start()

    def work(self, i):
        runs, rate = self.blocks[i][3:5]
        ring = i % SLOTS
        if i == 0:
            for unit in (0, 2, 4, 6):
                self.grad(unit).wait()
        elif i >= 4:
            self.grad(runs[0][0]).wait()
        for k in range(3):
            self.load(i, k).wait()
            if i >= SLOTS:
                self.store(i - SLOTS, k).wait()
        step = 16

        def body(r, _):
            rows = pl.ds(pl.multiple_of(r * step, step), step)
            for unit, start, to, count in runs:
                cols = slice(to, to + count)
                grad = self.total[unit, rows, start : start + count]
                new = adam(
                    self.ins[ring, 0, rows, cols], self.ins[ring, 1, rows, cols], self.ins[ring, 2, rows, cols],
                    grad, rate, weight_decay,
                )
                for k in range(3):
                    self.outs[ring, k, rows, cols] = new[k]
            return 0

        lax.fori_loop(0, self.rows // step, body, 0)
        for k in range(3):
            self.store(i, k).start()
        if i + SLOTS < len(self.blocks):
            self.begin(i + SLOTS)

    def drain(self):
        for i in range(len(self.blocks) - SLOTS, len(self.blocks)):
            for k in range(3):
                self.store(i, k).wait()


def finish_kernel(
    n_shard, sums, vec_sum, vec_state, out_done, in_done, qkv_state, out_state, fc1_state, fc2_state,
    output, input_grad, vec_new, qkv_new, out_new, fc1_new, fc2_new, ins, outs, total, sems, whole,
):
    moves = (
        pltpu.make_async_copy(out_done, output, whole.at[0]),
        pltpu.make_async_copy(in_done, input_grad, whole.at[1]),
    )
    optimizer = Adam(
        n_shard, (qkv_state, out_state, fc1_state, fc2_state), (qkv_new, out_new, fc1_new, fc2_new),
        ins, outs, total, sums, sems,
    )
    for unit in (0, 2, 4, 6):
        optimizer.grad(unit).start()
    for i in range(SLOTS):
        optimizer.begin(i)
    for unit in (1, 3, 5, 7, 8, 9, 10, 11):
        optimizer.grad(unit).start()
    for move in moves:
        move.start()
    new = adam(vec_state[0][...], vec_state[1][...], vec_state[2][...], vec_sum[0:VEC_ROWS], vector_rate, 0.0)
    for k in range(3):
        vec_new[k][...] = new[k]
    for i in range(len(optimizer.blocks)):
        optimizer.work(i)
    optimizer.drain()
    for move in moves:
        move.wait()


def finish(sums, vec_sum, vec_state, output, input_grad, states, n_shard):
    anywhere = pl.BlockSpec(memory_space=pl.ANY)
    vmem = pl.BlockSpec(memory_space=pltpu.VMEM)
    rows = sums.shape[1]
    like = lambda a: jax.ShapeDtypeStruct(a.shape, f32)
    return pl.pallas_call(
        functools.partial(finish_kernel, n_shard),
        out_shape=(
            like(output), like(input_grad), (like(vec_state[0]),) * 3, *((like(group[0]),) * 3 for group in states)
        ),
        in_specs=[anywhere, vmem, (vmem,) * 3, anywhere, anywhere] + [(anywhere,) * 3] * 4,
        out_specs=(anywhere, anywhere, (vmem,) * 3) + ((anywhere,) * 3,) * 4,
        scratch_shapes=[
            pltpu.VMEM((SLOTS, 3, rows, WIDE), f32),
            pltpu.VMEM((SLOTS, 3, rows, WIDE), f32),
            pltpu.VMEM((UNITS, rows, WIDE), f32),
            pltpu.SemaphoreType.DMA((3, SLOTS, UNITS)),
            pltpu.SemaphoreType.DMA((2,)),
        ],
        compiler_params=pltpu.CompilerParams(vmem_limit_bytes=62 * 2**20),
        name="update",
    )(sums, vec_sum, vec_state, output, input_grad, *states)


def lanes(vec, parts):
    return jnp.pad(vec.reshape(parts, VEC_ROWS, -1), ((0, 0), (0, 16 - VEC_ROWS), (0, 0)))


def to_units(qkv, out, fc1, fc2, n_shard):
    rows = out.shape[0]
    up = fc1.reshape(rows, n_shard, 4, -1).transpose(2, 0, 1, 3).reshape(4, 1, rows, WIDE)
    down = fc2.reshape(4, 1, rows, WIDE)
    pairs = jnp.concatenate([up, down], axis=1).reshape(8, rows, WIDE)
    return jnp.concatenate([pairs, qkv.reshape(rows, 3, WIDE).transpose(1, 0, 2), out[None]])


def rotary_tables(positions):
    half = ROT // 2
    freqs = 10000.0 ** (-jnp.arange(half).astype(f32) * 2.0 / ROT)
    angle = jnp.maximum(positions, 0).astype(f32)[:, None] * freqs[None, :]
    cosine, sine = jnp.cos(angle), jnp.sin(angle)
    one, none = jnp.ones_like(cosine), jnp.zeros_like(cosine)
    rest = HD // half - 2
    return (
        jnp.concatenate(([cosine, cosine] + [one] * rest) * 2, axis=1),
        jnp.concatenate(([-sine, none] + [none] * rest) * 2, axis=1),
        jnp.concatenate(([none, sine] + [none] * rest) * 2, axis=1),
    )


def adam(master, first, second, grad, rate, decay_on):
    first_new = beta_one * first + (1.0 - beta_one) * grad
    second_new = beta_two * second + (1.0 - beta_two) * grad * grad
    mhat = first_new / (1.0 - beta_one**STEP)
    vhat = second_new / (1.0 - beta_two**STEP)
    new = master - rate * (mhat / (jnp.sqrt(vhat) + epsilon) + decay_on * master)
    return (first_new, second_new, new)


def shards(
    tokens,
    cotangent,
    positions,
    qkv_master,
    qkv_first,
    qkv_second,
    out_master,
    out_first,
    out_second,
    fc1_master,
    fc1_first,
    fc1_second,
    fc2_master,
    fc2_first,
    fc2_second,
    vec_master,
    vec_first,
    vec_second,
):
    n_rep, n_shard = lax.axis_size("rep"), lax.axis_size("shard")
    own = to_units(
        qkv_master.astype(bf16), out_master.astype(bf16), fc1_master.astype(bf16), fc2_master.astype(bf16), n_shard
    )
    valid = (positions >= 0).astype(f32)[:, None]
    vec_own = lanes(vec_master.astype(bf16).astype(f32), 1)[0]
    late, early_grads, rows, part, d_two, act_one, grad_low, vec_early = mlp(
        own, vec_own, tokens, cotangent, valid, n_rep, n_shard
    )
    states = (
        (qkv_master, qkv_first, qkv_second),
        (out_master, out_first, out_second),
        (fc1_master, fc1_first, fc1_second),
        (fc2_master, fc2_first, fc2_second),
    )
    output, input_grad, sums, vec_sum = attention(
        early_grads, late, rows, act_one, grad_low, tokens, cotangent, valid, part, d_two, positions[None],
        rotary_tables(positions), vec_early, vec_own.shape[1], n_rep, n_shard,
    )
    vec_state = tuple(w.reshape(VEC_ROWS, -1) for w in (vec_master, vec_first, vec_second))
    output, input_grad, vec_new, *news = finish(sums, vec_sum, vec_state, output, input_grad, states, n_shard)
    vec_new = (w.reshape(-1) for w in vec_new)
    return (output, input_grad, *(w for new in news for w in new), *vec_new)


def solution(mesh):
    rows, owned, slots = P(("rep", "shard"), None), P("shard", None), P(("rep", "shard"))
    vector = P("shard")
    return jax.shard_map(
        shards,
        mesh=mesh,
        in_specs=(rows, rows, slots) + (owned,) * 12 + (vector,) * 3,
        out_specs=(rows, rows) + (owned,) * 12 + (vector,) * 3,
        check_vma=False,
    )
```

```python
import functools
import math

import jax
import jax.numpy as jnp
import numpy as np
from jax import lax
from jax.experimental import pallas as pl
from jax.experimental.pallas import tpu as pltpu
from jax.sharding import PartitionSpec as P

D = 1024
H = 16
HD = 64
FF = 4096
ROT = 16
STEP = 10

beta_one = 0.9
beta_two = 0.95
epsilon = 1e-08
weight_decay = 0.1
norm_eps = 1e-05
vector_rate = 0.1

MESH = pl.DeviceIdType.MESH
LANES = 128
UNITS = 12
WIDE = 1024
TILE = 256
EARLY = 8
PIECES = 24
STAGES = 4
SLOTS = 4
RING = 4
VEC_ROWS = 13
f32 = jnp.float32
bf16 = jnp.bfloat16


def dot(a, b):
    return jnp.dot(a, b, preferred_element_type=f32)


def dot_nt(a, b):
    return lax.dot_general(a, b, (((1,), (1,)), ((), ())), preferred_element_type=f32)


def dot_tn(a, b):
    return lax.dot_general(a, b, (((0,), (0,)), ((), ())), preferred_element_type=f32)


def run(first, count, width):
    return pl.ds(pl.multiple_of(first * width, LANES), count * width)


class Place:
    def __init__(self, n_rep, n_shard):
        self.n_rep, self.n_shard = n_rep, n_shard
        self.line = n_shard // 2
        self.bits = n_rep.bit_length() - 1
        self.rep = lax.axis_index("rep")
        self.shard = lax.axis_index("shard")
        self.core = lax.rem(self.shard, 2)
        self.spot = lax.div(self.shard, 2)
        digits = [lax.rem(lax.div(self.rep, 1 << p), 2) for p in range(self.bits)]
        turned = sum(digits[p] * (1 << (self.bits - 1 - p)) for p in range(self.bits))
        self.block = (1 - self.core) * self.rep + self.core * turned
        self.twins = []
        for p in range(self.bits):
            q = self.bits - 1 - p
            step_even = (1 - 2 * digits[p]) * (1 << p)
            step_odd = (1 - 2 * digits[q]) * (1 << q)
            self.twins.append(self.rep + (1 - self.core) * step_even + self.core * step_odd)

    def hold(self, p):
        return lax.div(self.block, 1 << p) * (1 << p)

    def other(self, p):
        mine = lax.div(self.block, 1 << p)
        return (mine + 1 - 2 * lax.rem(mine, 2)) * (1 << p)

    def ahead(self, d):
        return lax.rem(self.spot + d, self.line)

    def behind(self, d):
        return lax.rem(self.spot + self.line - d, self.line)

    def along(self, d):
        return (self.rep, 2 * self.ahead(d) + self.core)

    def sibling(self):
        return (self.rep, self.shard + 1 - 2 * self.core)

    def twin(self, p):
        return (self.twins[p], self.shard)

    def group(self, d):
        return (self.rep, lax.rem(self.shard + d, self.n_shard))

    def replica(self, d):
        return (lax.rem(self.rep + d, self.n_rep), self.shard)

    def greet(self):
        barrier = pltpu.get_barrier_semaphore()
        peers = [self.group(d) for d in range(1, self.n_shard)]
        peers += [self.replica(d) for d in range(1, self.n_rep)]
        for peer in peers:
            pl.semaphore_signal(barrier, inc=1, device_id=peer, device_id_type=MESH)
        pl.semaphore_wait(barrier, len(peers))


class Copies:
    def __init__(self, send, recv):
        self.send, self.recv, self.used, self.sent = send, recv, 0, []

    def take(self, count):
        self.used += count
        return self.used - count

    def make(self, slot, src, dst, peer):
        return pltpu.make_async_remote_copy(
            src_ref=src,
            dst_ref=dst,
            send_sem=self.send.at[slot],
            recv_sem=self.recv.at[slot],
            device_id=peer,
            device_id_type=MESH,
        )

    def start(self, slot, src, dst, peer):
        copy = self.make(slot, src, dst, peer)
        copy.start()
        self.sent.append(copy)

    def arrived(self, slot, dst, peer):
        self.make(slot, dst, dst, peer).wait_recv()

    def drain(self):
        for copy in self.sent:
            copy.wait_send()


class Gather:
    def __init__(self, at, copies, full):
        self.at, self.copies, self.full = at, copies, full
        self.width = WIDE // at.n_rep
        self.half = full.shape[3] // 2
        self.per_piece = (at.line - 1) * (at.bits + 1) + at.line
        self.base = copies.take(self.per_piece * PIECES)

    def slot(self, v, p):
        return self.base + v * self.per_piece + p * (self.at.line - 1)

    def place(self, v, spot, core, cols=slice(None)):
        rows = pl.ds(pl.multiple_of(lax.rem(v, 2) * self.half, self.half), self.half)
        return self.full.at[lax.div(v, 2), spot, core, rows, cols]

    def line_send(self, v, d):
        at = self.at
        piece = self.place(v, at.spot, at.core, run(at.hold(0), 1, self.width))
        return self.copies.make(self.slot(v, 0) + d - 1, piece, piece, at.along(d))

    def twin_send(self, v, p, d):
        at = self.at
        piece = self.place(v, at.behind(d), at.core, run(at.hold(p), 1 << p, self.width))
        return self.copies.make(self.slot(v, p + 1) + d - 1, piece, piece, at.twin(p))

    def sibling_send(self, v, d):
        at = self.at
        piece = self.place(v, at.behind(d), at.core)
        return self.copies.make(self.slot(v, at.bits + 1) + d, piece, piece, at.sibling())

    def begin(self, v):
        for d in range(1, self.at.line):
            self.line_send(v, d).start()

    def stage(self, v, p):
        at = self.at
        if p == at.bits + 1:
            for d in range(at.line):
                self.copies.arrived(self.slot(v, p) + d, self.place(v, at.behind(d), 1 - at.core), at.sibling())
            return
        if p == at.bits:
            self.sibling_send(v, 0).start()
        for d in range(1, at.line):
            got = run(at.other(p - 1), 1 << (p - 1), self.width) if p > 0 else run(at.hold(0), 1, self.width)
            self.copies.arrived(
                self.slot(v, p) + d - 1,
                self.place(v, at.behind(d), at.core, got),
                at.twin(p - 1) if p > 0 else at.along(d),
            )
            if p < at.bits:
                self.twin_send(v, p, d).start()
            else:
                self.sibling_send(v, d).start()

    def step(self, t, first, last):
        for p in range(first, last):
            v = t - p
            if isinstance(t, int):
                if 0 <= v < PIECES:
                    self.stage(v, p)
            else:
                pl.when(v < PIECES)(functools.partial(self.stage, v, p))

    def drain(self, v):
        at = self.at
        for d in range(1, at.line):
            self.line_send(v, d).wait_send()
            for p in range(at.bits):
                self.twin_send(v, p, d).wait_send()
        for d in range(at.line):
            self.sibling_send(v, d).wait_send()


def vector_places(n_shard, lane):
    places = []
    for row in range(VEC_ROWS):
        for q in range(WIDE // lane):
            if 8 <= row < 12:
                start = 8 * WIDE + q * (FF // n_shard) + (row - 8) * lane
            else:
                start = row * WIDE + q * lane
            places.append((row, q * lane, start // lane // VEC_ROWS, start // lane % VEC_ROWS))
    return places


def mlp_kernel(
    n_rep, n_shard, qkv, out, fc1, fc2, vec_in, tokens_in, cot_in, positions, freqs,
    late, grads, rows_out, part_out, d_two_out, act_one_out, grad_low_out, grad_vec, valid, cosine, up, down,
    full, vec_own, vec_full, tokens, cot, part, d_two, act_one, grad_low,
    act_two, act_two_t, act, d_hidden, stage_grads, send, recv, local,
):
    at = Place(n_rep, n_shard)
    line, bits = at.line, at.bits
    shard_rows = full.shape[3]
    tall = TILE // (2 * shard_rows)
    count = tokens.shape[0]
    lane = vec_own.shape[1]

    def stage_block(b):
        return stage_grads.at[b // (2 * line), b % (2 * line) // 2, b % 2]

    sources = [fc1.at[:, k * WIDE : (k + 1) * WIDE] for k in range(4)]
    sources += [fc2.at[k * shard_rows : (k + 1) * shard_rows] for k in range(4)]
    sources += [qkv.at[:, k * WIDE : (k + 1) * WIDE] for k in range(3)] + [out]
    brought = [pltpu.make_async_copy(src, stage_block(b), local.at[b]) for b, src in enumerate(sources)]
    brought += [
        pltpu.make_async_copy(tokens_in, tokens, local.at[UNITS]),
        pltpu.make_async_copy(cot_in, cot, local.at[UNITS + 1]),
    ]
    for copy in brought:
        copy.start()
    vec_own[0:VEC_ROWS] = vec_in[...].astype(bf16).astype(f32)
    vec_own[VEC_ROWS:] = jnp.zeros((16 - VEC_ROWS, lane), f32)
    at.greet()
    copies = Copies(send, recv)
    gather = Gather(at, copies, full)
    vec_slot = copies.take(n_shard)
    for d in range(1, n_shard):
        copies.start(vec_slot + d, vec_own, vec_full.at[at.shard], at.group(d))

    for u in range(UNITS):
        if u == 0:
            for b in range(4):
                brought[b].wait()
        mine = full.at[u, at.spot, at.core]
        if u < 8 and u % 2 == 0:
            for s in range(n_shard):
                from_col = (4 * s + u // 2) * lane
                block = stage_block(from_col // WIDE)
                first = from_col % WIDE
                mine[:, s * lane : (s + 1) * lane] = block[:, first : first + lane].astype(bf16)
        else:
            b = 4 + u // 2 if u < 8 else u
            brought[b].wait()
            mine[...] = stage_block(b)[...].astype(bf16)
        gather.begin(2 * u)
        gather.begin(2 * u + 1)
    vec_full[at.shard] = vec_own[...]

    place = jnp.broadcast_to(positions[...].astype(f32), (LANES, count)).T
    valid[...] = (place >= 0.0).astype(f32)
    angle = jnp.maximum(place, 0.0) * freqs[...]
    in_head = lax.rem(lax.broadcasted_iota(jnp.int32, (1, LANES), 1), HD)
    sine = jnp.sin(angle)
    cosine[...] = jnp.where(in_head < ROT, jnp.cos(angle), 1.0)
    up[...] = jnp.where(in_head < ROT // 2, -sine, 0.0)
    down[...] = jnp.where((in_head >= ROT // 2) & (in_head < ROT), sine, 0.0)

    step = 64
    brought[UNITS].wait()
    brought[UNITS + 1].wait()

    def lower(i, sums):
        rows = pl.ds(pl.multiple_of(i * step, step), step)
        low = (cot[rows] * valid[rows, 0:1]).astype(bf16)
        grad_low[rows] = low
        d_two[rows] = jnp.zeros((step, WIDE), f32)
        return sums + jnp.sum(low.astype(f32), axis=0, keepdims=True)

    grad_vec[4:5] = lax.fori_loop(0, count // step, lower, jnp.zeros((1, WIDE), f32))

    for d in range(1, n_shard):
        copies.arrived(vec_slot + d, vec_full.at[lax.rem(at.shard + n_shard - d, n_shard)], at.group(d))
    for row, first, device, spot in vector_places(n_shard, lane):
        rows_out[row : row + 1, first : first + lane] = vec_full[device, spot : spot + 1, :]

    def norm(i, _):
        rows = pl.ds(pl.multiple_of(i * step, step), step)
        x = tokens[rows].astype(f32)
        centred = x - jnp.mean(x, axis=-1, keepdims=True)
        var = jnp.mean(centred * centred, axis=-1, keepdims=True)
        unit = centred * lax.rsqrt(var + norm_eps)
        act_one[rows] = (unit * rows_out[0:1] + rows_out[1:2]).astype(bf16)
        act_two[rows] = (unit * rows_out[2:3] + rows_out[3:4]).astype(bf16)
        part[rows] = x + rows_out[12:13]
        return 0

    lax.fori_loop(0, count // step, norm, 0)
    act_two_t[...] = act_two[...].T

    def leaving(k):
        src, dst = ((act_one, act_one_out), (grad_low, grad_low_out), (part, part_out), (d_two, d_two_out))[k]
        return pltpu.make_async_copy(src, dst, local.at[UNITS + 2 + k])

    leaving(0).start()
    leaving(1).start()
    ahead = bits + 5
    for t in range(ahead):
        gather.step(t, 0, bits + 2)

    def out_copy(k, u):
        return pltpu.make_async_copy(stage_grads.at[k], grads.at[u], local.at[k])

    def tile(j, _):
        u1, u2 = 2 * j, 2 * j + 1

        def comm(q):
            t = ahead + 4 * j + q // 2
            if q % 2 == 0:
                gather.step(t, 0, bits)
            else:
                gather.step(t, bits, bits + 2)

        for q in range(4):
            comm(q)
            cols = slice(q * TILE, (q + 1) * TILE)
            spots = slice(q * tall, (q + 1) * tall)
            w1 = full[u1, :, :, :, cols].reshape(D, TILE)
            h = dot(act_two[...], w1) + rows_out[pl.ds(8 + j, 1), cols]
            below = 0.5 + 0.5 * lax.erf(h * (0.5**0.5))
            act[:, cols] = (h * below).astype(bf16)
            slope = below + h * (jnp.exp(-0.5 * h * h) * (1.0 / math.sqrt(2.0 * math.pi)))
            w2 = full[u2, spots].reshape(TILE, D)
            dh = (dot_nt(grad_low[...], w2) * slope).astype(bf16)
            d_hidden[:, cols] = dh
            grad_vec[pl.ds(j, 1), cols] = jnp.sum(dh.astype(f32), axis=0, keepdims=True)
        for q in range(4):
            comm(4 + q)
            cols = slice(q * TILE, (q + 1) * TILE)
            spots = slice(q * tall, (q + 1) * tall)
            if q == 0:

                @pl.when(j > 0)
                def _():
                    out_copy(0, 0).wait()
                    out_copy(1, 0).wait()

            part[:, cols] += dot(act[...], full[u2, :, :, :, cols].reshape(D, TILE))
            d_two[:, cols] += dot_nt(d_hidden[...], full[u1, spots].reshape(TILE, WIDE))
            stage_grads[1, spots] = dot_tn(act[:, cols], grad_low[...]).reshape(tall, 2, shard_rows, WIDE)
            stage_grads[0, spots] = dot(act_two_t[cols], d_hidden[...]).reshape(tall, 2, shard_rows, WIDE)
        out_copy(0, u1).start()
        out_copy(1, u2).start()
        return 0

    lax.fori_loop(0, 4, tile, 0)
    leaving(2).start()
    leaving(3).start()

    def late_copy(u):
        return pltpu.make_async_copy(full.at[u], late.at[u - 8], local.at[u])

    late_copy(8).start()
    late_copy(9).start()
    for t in range(ahead + 16, PIECES + bits + 1):
        gather.step(t, 0, bits + 2)
        if (t - bits - 1) % 2 == 1:
            late_copy((t - bits - 1) // 2).start()

    def finish(v, _):
        gather.drain(v)
        return 0

    lax.fori_loop(0, PIECES, finish, 0)
    copies.drain()
    out_copy(0, 0).wait()
    out_copy(1, 0).wait()
    for k in range(4):
        leaving(k).wait()
    for u in range(8, UNITS):
        late_copy(u).wait()


def mlp(masters, vec, tokens, cot, positions, n_rep, n_shard):
    shard_rows, line, bits = masters[1].shape[0], n_shard // 2, n_rep.bit_length() - 1
    slots = PIECES * ((line - 1) * (bits + 1) + line) + n_shard
    count = tokens.shape[0]
    anywhere = pl.BlockSpec(memory_space=pl.ANY)
    vmem = pl.BlockSpec(memory_space=pltpu.VMEM)
    unit = (line, 2, shard_rows, WIDE)
    freqs = 10000.0 ** (-(np.arange(LANES) % (ROT // 2)) * 2.0 / ROT)
    table = jax.ShapeDtypeStruct((count, LANES), f32)
    flat = lambda kind: pltpu.VMEM((count, WIDE), kind)
    return pl.pallas_call(
        functools.partial(mlp_kernel, n_rep, n_shard),
        out_shape=(
            jax.ShapeDtypeStruct((4,) + unit, bf16),
            jax.ShapeDtypeStruct((8,) + unit, f32),
            jax.ShapeDtypeStruct((16, WIDE), f32),
            jax.ShapeDtypeStruct((count, WIDE), f32),
            jax.ShapeDtypeStruct((count, WIDE), f32),
            jax.ShapeDtypeStruct((count, WIDE), bf16),
            jax.ShapeDtypeStruct((count, WIDE), bf16),
            jax.ShapeDtypeStruct((8, WIDE), f32),
            table, table, table, table,
        ),
        in_specs=[anywhere] * 4 + [vmem, anywhere, anywhere, vmem, vmem],
        out_specs=(anywhere, anywhere, vmem) + (anywhere,) * 4 + (vmem,) * 5,
        scratch_shapes=[
            pltpu.VMEM((UNITS,) + unit, bf16),
            pltpu.VMEM((16, vec.shape[1]), f32),
            pltpu.VMEM((n_shard, 16, vec.shape[1]), f32),
            flat(bf16), flat(f32), flat(f32), flat(f32), flat(bf16), flat(bf16),
            flat(bf16),
            pltpu.VMEM((WIDE, count), bf16),
            flat(bf16), flat(bf16),
            pltpu.VMEM((2,) + unit, f32),
            pltpu.SemaphoreType.DMA((slots,)),
            pltpu.SemaphoreType.DMA((slots,)),
            pltpu.SemaphoreType.DMA((UNITS + 6,)),
        ],
        compiler_params=pltpu.CompilerParams(
            collective_id=0, has_side_effects=True, vmem_limit_bytes=60 * 2**20
        ),
        name="gather_and_mlp",
    )(*masters, vec, tokens, cot, positions, jnp.asarray(freqs[None], f32))


def turn(u, tables, sign):
    cosine, up, down = tables
    return u * cosine + sign * (pltpu.roll(u, LANES - ROT // 2, 1) * up + pltpu.roll(u, ROT // 2, 1) * down)


class Reduce:
    def __init__(self, at, copies, early, late, sib, bufs, local):
        self.at, self.copies, self.early, self.late, self.sib, self.local = at, copies, early, late, sib, local
        (self.mine_buf, self.sib_buf, self.keep, self.halves_out, self.halves_in,
         self.line_out, self.line_in, self.final, self.total) = bufs
        self.width = WIDE // at.n_rep
        self.half = early.shape[3] // 2
        self.per_piece = 1 + at.bits + (at.line - 1) + at.bits
        self.base = copies.take(self.per_piece * PIECES)
        self.stages = [self.fetch, self.first]
        self.stages += [functools.partial(self.later, j=j) for j in range(at.bits)]
        self.stages += [functools.partial(self.spread, p=p) for p in range(at.bits + 1)]
        self.lags = [0, 1] + [1 + 2 * (i + 1) for i in range(len(self.stages) - 2)]
        self.depth = self.lags[-1] + 1

    def slot(self, v, k):
        return self.base + v * self.per_piece + k

    def rows(self, v):
        return pl.ds(pl.multiple_of(lax.rem(v, 2) * self.half, self.half), self.half)

    def source(self, v, core):
        if isinstance(v, int) and v >= 2 * EARLY:
            return self.late.at[v // 2 - EARLY, :, core, pl.ds((v % 2) * self.half, self.half)]
        return self.early.at[lax.div(v, 2), :, core, self.rows(v)]

    def sums(self, v, first, count):
        return self.total.at[lax.div(v, 2), self.rows(v), run(first, count, self.width)]

    def sibling_copy(self, v):
        return self.copies.make(self.slot(v, 0), self.source(v, 1 - self.at.core), self.sib.at[v], self.at.sibling())

    def twin_copy(self, v, p):
        ring = lax.rem(v, RING)
        return self.copies.make(
            self.slot(v, self.at.bits - p), self.halves_out[p].at[ring], self.halves_in[p].at[ring], self.at.twin(p)
        )

    def line_copy(self, v, d):
        ring = lax.rem(v, RING)
        return self.copies.make(
            self.slot(v, self.at.bits + d),
            self.line_out.at[ring, d - 1],
            self.line_in.at[ring, d - 1],
            self.at.along(d),
        )

    def spread_copy(self, v, p):
        piece = self.sums(v, self.at.hold(p), 1 << p)
        return self.copies.make(self.slot(v, self.at.bits + self.at.line + p), piece, piece, self.at.twin(p))

    def loads(self, v):
        return (
            pltpu.make_async_copy(self.source(v, self.at.core), self.mine_buf, self.local.at[0]),
            pltpu.make_async_copy(self.sib.at[v], self.sib_buf, self.local.at[1]),
        )

    def reuse(self, v, copies):
        def wait():
            for copy in copies(v - RING):
                copy.wait_send()

        if isinstance(v, int):
            if v >= RING:
                wait()
        else:
            pl.when(v >= RING)(wait)

    def fetch(self, v):
        self.sibling_copy(v).wait_recv()
        for copy in self.loads(v):
            copy.start()

    def first(self, v):
        at, width = self.at, self.width
        for copy in self.loads(v):
            copy.wait()
        p = at.bits - 1
        self.reuse(v, lambda w: [self.twin_copy(w, p)])
        to, stay = run(at.other(p), 1 << p, width), run(at.hold(p), 1 << p, width)
        ring = lax.rem(v, RING)

        def body(spot, _):
            a, b = self.mine_buf.at[spot], self.sib_buf.at[spot]
            self.halves_out[p][ring, spot] = (a[:, to] + b[:, to]).astype(bf16)
            self.keep[p][ring, spot] = a[:, stay] + b[:, stay]
            return 0

        lax.fori_loop(0, at.line, body, 0)
        self.twin_copy(v, p).start()

    def later(self, v, j):
        at = self.at
        p = at.bits - 1 - j
        ring = lax.rem(v, RING)
        self.twin_copy(v, p).wait_recv()
        if p > 0:
            self.reuse(v, lambda w: [self.twin_copy(w, p - 1)])
            half = self.width << (p - 1)
            side = lax.rem(lax.div(at.block, 1 << (p - 1)), 2)
            to, stay = run(1 - side, 1, half), run(side, 1, half)

            def body(spot, _):
                a, b = self.keep[p].at[ring, spot], self.halves_in[p].at[ring, spot]
                self.halves_out[p - 1][ring, spot] = (a[:, to] + b[:, to].astype(f32)).astype(bf16)
                self.keep[p - 1][ring, spot] = a[:, stay] + b[:, stay].astype(f32)
                return 0

            lax.fori_loop(0, at.line, body, 0)
            self.twin_copy(v, p - 1).start()
            return
        self.reuse(v, lambda w: [self.line_copy(w, d) for d in range(1, at.line)])
        for d in range(1, at.line):
            spot = at.ahead(d)
            self.line_out[ring, d - 1] = self.keep[0][ring, spot] + self.halves_in[0][ring, spot].astype(f32)
            self.line_copy(v, d).start()
        self.final[ring] = self.keep[0][ring, at.spot] + self.halves_in[0][ring, at.spot].astype(f32)

    def spread(self, v, p):
        at = self.at
        if p == 0:
            ring = lax.rem(v, RING)
            value = self.final[ring]
            for d in range(1, at.line):
                self.line_copy(v, d).wait_recv()
                value = value + self.line_in[ring, d - 1]
            self.total[lax.div(v, 2), self.rows(v), run(at.hold(0), 1, self.width)] = value
        else:
            got = self.sums(v, at.other(p - 1), 1 << (p - 1))
            self.copies.make(self.slot(v, at.bits + at.line + p - 1), got, got, at.twin(p - 1)).wait_recv()
        if p < at.bits:
            self.spread_copy(v, p).start()

    def jobs(self, t):
        out = []
        for i in reversed(range(len(self.stages))):
            v = t - self.lags[i]
            if isinstance(t, int):
                if 0 <= v < PIECES:
                    out.append(functools.partial(self.stages[i], v))
            else:
                out.append(functools.partial(lambda i, v: pl.when(v >= 0)(lambda: self.stages[i](v)), i, v))
        return out

    def drain(self):
        at = self.at
        for v in range(PIECES - RING, PIECES):
            for p in range(at.bits):
                self.twin_copy(v, p).wait_send()
            for d in range(1, at.line):
                self.line_copy(v, d).wait_send()

        def body(v, _):
            for p in range(at.bits):
                self.spread_copy(v, p).wait_send()
            return 0

        lax.fori_loop(0, PIECES, body, 0)

        def siblings(v, _):
            self.sibling_copy(v).wait_send()
            return 0

        lax.fori_loop(0, 2 * EARLY, siblings, 0)
        for v in range(2 * EARLY, PIECES):
            self.sibling_copy(v).wait_send()


def attention_kernel(
    n_rep, n_shard, early, late, rows_in, act_one, grad_low, tokens, cot, valid, part_in, d_two_in, positions,
    cosine, up, down, vec_early,
    output, input_grad, sums_out, vec_sum, late_grads, sib,
    weights, part, d_two, query, keys, values, d_mixed, mixed, d_qkv, act_one_t, bias, d_one, stage_grads,
    grad_vec, vec_part, vec_got, vec_all, reduce_bufs, send, recv, local,
):
    at = Place(n_rep, n_shard)
    count = tokens.shape[0]
    line, shard_rows = late.shape[1], late.shape[3]
    tall = TILE // (2 * shard_rows)
    step = 64
    scale = HD**-0.5

    def bring(k, src, dst):
        return pltpu.make_async_copy(src, dst, local.at[2 + k])

    inputs = [(late.at[j], weights.at[j]) for j in range(4)] + [(part_in, part), (d_two_in, d_two)]
    for k, (src, dst) in enumerate(inputs):
        bring(k, src, dst).start()
    at.greet()
    copies = Copies(send, recv)
    reduce = Reduce(at, copies, early, late_grads, sib, reduce_bufs, local)
    vec_slot = copies.take(n_shard)
    vec_slot_rep = copies.take(n_rep)

    def begin(v, _):
        reduce.sibling_copy(v).start()
        return 0

    lax.fori_loop(0, 2 * EARLY, begin, 0)
    total = reduce_bufs[-1]

    tables = (cosine[...], up[...], down[...])

    def weight(j, cols):
        return weights[j, :, :, :, cols].reshape(D, cols.stop - cols.start)

    key_idx = lax.broadcasted_iota(jnp.int32, (count, count), 0)
    query_idx = lax.broadcasted_iota(jnp.int32, (count, count), 1)
    allowed = (key_idx <= query_idx) & (key_idx >= query_idx - jnp.maximum(positions[...], 0))
    bias[...] = jnp.where(allowed, 0.0, -1e30)
    act_one_t[...] = act_one[...].T
    for k in range(4):
        bring(k, *inputs[k]).wait()

    queue = []
    clock = [0]

    def tick(number):
        for _ in range(number):
            while not queue:
                queue.extend(reduce.jobs(clock[0]))
                clock[0] += 1
            queue.pop(0)()

    def flush():
        while queue:
            queue.pop(0)()

    for q in range(4):
        if q % 2 == 0:
            queue.extend(reduce.jobs(clock[0]))
            clock[0] += 1
        flush()
        cols = slice(q * TILE, (q + 1) * TILE)
        spots = slice(q * tall, (q + 1) * tall)
        for j, target in enumerate((query, keys, values)):
            value = dot(act_one[...], weight(j, cols)) + rows_in[4 + j : 5 + j, cols]
            for half in range(TILE // LANES):
                piece = value[:, half * LANES : (half + 1) * LANES]
                if j < 2:
                    piece = turn(piece, tables, 1.0)
                piece = piece.astype(bf16)
                if j == 0:
                    piece = piece * jnp.asarray(scale, bf16)
                target[:, q * TILE + half * LANES : q * TILE + (half + 1) * LANES] = piece
        d_mixed[:, cols] = dot_nt(grad_low[...], weights[3, spots].reshape(TILE, WIDE)).astype(bf16)

    first_head = lax.broadcasted_iota(jnp.int32, (1, LANES), 1) < HD

    def pair(i):
        cols = pl.ds(pl.multiple_of(i * LANES, LANES), LANES)
        q2, k2, v2, o2 = query[:, cols], keys[:, cols], values[:, cols], d_mixed[:, cols]
        nothing = jnp.zeros((), bf16)
        blocks = count // TILE
        mixed_parts, dq_parts = [0.0] * blocks, [0.0] * blocks
        dk_parts, dv_parts = [0.0] * blocks, [0.0] * blocks
        for head in range(2):
            keep = first_head if head == 0 else jnp.logical_not(first_head)
            qm, km, vm, om = (jnp.where(keep, w, nothing) for w in (q2, k2, v2, o2))
            for b in range(blocks):
                span = slice(0, (b + 1) * TILE)
                mine = slice(b * TILE, (b + 1) * TILE)
                scores = dot_nt(k2[span], qm[mine]) + bias[span, mine]
                top = jnp.max(scores, axis=0, keepdims=True)
                expo = jnp.exp(scores - top)
                probs = expo * (1.0 / jnp.sum(expo, axis=0, keepdims=True))
                low = probs.astype(bf16)
                d_probs = dot_nt(v2[span], om[mine])
                inner = jnp.sum(probs * d_probs, axis=0, keepdims=True)
                d_scores = (probs * (d_probs - inner)).astype(bf16)
                mixed_parts[b] += dot_tn(low, vm[span])
                dq_parts[b] += dot_tn(d_scores, km[span])
                dv = dot(low, om[mine])
                dk = dot(d_scores, qm[mine])
                for c in range(b + 1):
                    dk_parts[c] += dk[c * TILE : (c + 1) * TILE]
                    dv_parts[c] += dv[c * TILE : (c + 1) * TILE]
        for b in range(blocks):
            mine = slice(b * TILE, (b + 1) * TILE)
            local_tables = (cosine[mine], up[mine], down[mine])
            mixed[mine, cols] = mixed_parts[b].astype(bf16)
            d_qkv[0, mine, cols] = turn(dq_parts[b] * scale, local_tables, -1.0).astype(bf16)
            d_qkv[1, mine, cols] = turn(dk_parts[b], local_tables, -1.0).astype(bf16)
            d_qkv[2, mine, cols] = dv_parts[b].astype(bf16)

    clock_here = clock[0]

    def two_pairs(i, _):
        jobs = reduce.jobs(clock_here + i)
        pair(2 * i)
        for job in jobs[: len(jobs) // 2]:
            job()
        pair(2 * i + 1)
        for job in jobs[len(jobs) // 2 :]:
            job()
        return 0

    lax.fori_loop(0, H // 4, two_pairs, 0)
    clock[0] += H // 4

    def out_copy(k):
        j, q = k // 4, k % 4
        spots = pl.ds(q * tall, tall)
        return pltpu.make_async_copy(
            stage_grads.at[k % STAGES], late_grads.at[j, spots], local.at[2 + len(inputs) + k % STAGES]
        )

    for k in range(16):
        j, q = k // 4, k % 4
        if k >= STAGES:
            out_copy(k - STAGES).wait()
        cols = slice(q * TILE, (q + 1) * TILE)
        if j < 3:
            value = dot(act_one_t[cols], d_qkv[j])
        else:
            value = dot_tn(mixed[:, cols], grad_low[...])
        stage_grads[k % STAGES] = value.reshape(tall, 2, shard_rows, WIDE)
        out_copy(k).start()
        if k % 2 == 1:
            tick(1)
    for k in range(16 - STAGES, 16):
        out_copy(k).wait()
    for v in range(2 * EARLY, PIECES):
        reduce.sibling_copy(v).start()
    bring(4, *inputs[4]).wait()
    bring(5, *inputs[5]).wait()
    for q in range(4):
        cols = slice(q * TILE, (q + 1) * TILE)
        spots = slice(q * tall, (q + 1) * tall)
        part[:, cols] += dot(mixed[...], weight(3, cols)) + rows_in[7:8, cols]
        value = dot_nt(d_qkv[0], weights[0, spots].reshape(TILE, WIDE))
        value += dot_nt(d_qkv[1], weights[1, spots].reshape(TILE, WIDE))
        value += dot_nt(d_qkv[2], weights[2, spots].reshape(TILE, WIDE))
        d_one[:, cols] = value
        tick(2)
    pltpu.make_async_copy(part, output, local.at[2]).start()
    for j in range(3):
        grad_vec[4 + j : 5 + j] = jnp.sum(d_qkv[j].astype(f32), axis=0, keepdims=True)

    def norm_back(i, sums):
        mine = pl.ds(pl.multiple_of(i * step, step), step)
        x = tokens[mine].astype(f32)
        centred = x - jnp.mean(x, axis=-1, keepdims=True)
        var = jnp.mean(centred * centred, axis=-1, keepdims=True)
        spread = lax.rsqrt(var + norm_eps)
        unit = centred * spread
        one, two = d_one[mine], d_two[mine]
        d_unit = one * rows_in[0:1] + two * rows_in[2:3]
        flat = jnp.mean(d_unit, axis=-1, keepdims=True)
        tilt = jnp.mean(d_unit * unit, axis=-1, keepdims=True)
        d_two[mine] = cot[mine] * valid[mine, 0:1] + spread * (d_unit - flat - unit * tilt)
        return tuple(
            s + jnp.sum(w, axis=0, keepdims=True) for s, w in zip(sums, (one * unit, one, two * unit, two))
        )

    sums = lax.fori_loop(0, count // step, norm_back, (jnp.zeros((1, WIDE), f32),) * 4)
    for k in range(4):
        grad_vec[k : k + 1] = sums[k]
    pltpu.make_async_copy(d_two, input_grad, local.at[3]).start()
    grad_vec[7:8] = vec_early[4:5]
    grad_vec[8:12] = vec_early[0:4]
    grad_vec[12:13] = vec_early[4:5]
    lane = vec_sum.shape[1]
    for row, start, device, place in vector_places(n_shard, lane):
        vec_part[device, place : place + 1, :] = grad_vec[row : row + 1, start : start + lane]
    for d in range(1, n_shard):
        to = lax.rem(at.shard + d, n_shard)
        copies.start(vec_slot + d, vec_part.at[to], vec_got.at[d], at.group(d))

    def vec_first():
        value = vec_part[at.shard]
        for d in range(1, n_shard):
            copies.arrived(vec_slot + d, vec_got.at[d], at.group(d))
            value = value + vec_got[d]
        vec_all[at.rep] = value
        for d in range(1, n_rep):
            copies.start(vec_slot_rep + d, vec_all.at[at.rep], vec_all.at[at.rep], at.replica(d))

    def vec_last():
        for d in range(1, n_rep):
            copies.arrived(vec_slot_rep + d, vec_all.at[lax.rem(at.rep + n_rep - d, n_rep)], at.replica(d))
        value = vec_all[0]
        for i in range(1, n_rep):
            value = value + vec_all[i]
        vec_sum[...] = value

    def result(u):
        return pltpu.make_async_copy(total.at[u], sums_out.at[u], local.at[2 + len(inputs) + STAGES + u])

    done = 0
    while queue or clock[0] < PIECES + reduce.depth - 1:
        tick(len(queue) or 1)
        flush()
        if clock[0] == 2 * EARLY:
            vec_first()
        if clock[0] == 2 * EARLY + 4:
            vec_last()
        while done < min(UNITS, (clock[0] - reduce.depth + 1) // 2):
            result(done).start()
            done += 1
    for u in range(UNITS):
        result(u).wait()
    reduce.drain()
    copies.drain()
    pltpu.make_async_copy(part, output, local.at[2]).wait()
    pltpu.make_async_copy(d_two, input_grad, local.at[3]).wait()


def attention(
    early, late, rows, act_one, grad_low, tokens, cot, valid, part, d_two, positions, tables, vec_early, lane,
    n_rep, n_shard,
):
    count = tokens.shape[0]
    unit = late.shape[1:]
    line, _, shard_rows, _ = unit
    bits, width, half = n_rep.bit_length() - 1, WIDE // n_rep, shard_rows // 2
    slots = PIECES * (1 + bits + line - 1 + bits) + n_shard + n_rep
    anywhere = pl.BlockSpec(memory_space=pl.ANY)
    vmem = pl.BlockSpec(memory_space=pltpu.VMEM)
    flat = lambda: pltpu.VMEM((count, WIDE), bf16)
    outs = pl.pallas_call(
        functools.partial(attention_kernel, n_rep, n_shard),
        out_shape=(
            jax.ShapeDtypeStruct((count, WIDE), f32),
            jax.ShapeDtypeStruct((count, WIDE), f32),
            jax.ShapeDtypeStruct((UNITS, shard_rows, WIDE), f32),
            jax.ShapeDtypeStruct((16, lane), f32),
            jax.ShapeDtypeStruct((4,) + unit, f32),
            jax.ShapeDtypeStruct((PIECES, line, half, WIDE), f32),
        ),
        in_specs=[anywhere, anywhere] + [vmem] * 6 + [anywhere, anywhere] + [vmem] * 5,
        out_specs=(anywhere, anywhere, anywhere, vmem, anywhere, anywhere),
        scratch_shapes=[
            pltpu.VMEM((4,) + unit, bf16),
            pltpu.VMEM((count, WIDE), f32),
            pltpu.VMEM((count, WIDE), f32),
            flat(), flat(), flat(), flat(), flat(),
            pltpu.VMEM((3, count, WIDE), bf16),
            pltpu.VMEM((WIDE, count), bf16),
            pltpu.VMEM((count, count), f32),
            pltpu.VMEM((count, WIDE), f32),
            pltpu.VMEM((STAGES, TILE // (2 * shard_rows)) + unit[1:], f32),
            pltpu.VMEM((16, WIDE), f32),
            pltpu.VMEM((n_shard, 16, lane), f32),
            pltpu.VMEM((n_shard, 16, lane), f32),
            pltpu.VMEM((n_rep, 16, lane), f32),
            [
                pltpu.VMEM((line, half, WIDE), f32),
                pltpu.VMEM((line, half, WIDE), f32),
                [pltpu.VMEM((RING, line, half, width << p), f32) for p in range(bits)],
                [pltpu.VMEM((RING, line, half, width << p), bf16) for p in range(bits)],
                [pltpu.VMEM((RING, line, half, width << p), bf16) for p in range(bits)],
                pltpu.VMEM((RING, line - 1, half, width), f32),
                pltpu.VMEM((RING, line - 1, half, width), f32),
                pltpu.VMEM((RING, half, width), f32),
                pltpu.VMEM((UNITS, shard_rows, WIDE), f32),
            ],
            pltpu.SemaphoreType.DMA((slots,)),
            pltpu.SemaphoreType.DMA((slots,)),
            pltpu.SemaphoreType.DMA((2 + 6 + STAGES + UNITS,)),
        ],
        compiler_params=pltpu.CompilerParams(
            collective_id=1, has_side_effects=True, vmem_limit_bytes=62 * 2**20
        ),
        name="attention_and_sums",
    )(
        early, late, rows, act_one, grad_low, tokens, cot, valid, part, d_two, positions, *tables, vec_early
    )
    return outs[:4]


class Adam:
    def __init__(self, n_shard, states, results, ins, outs, total, sums, sems):
        self.states, self.results, self.ins, self.outs, self.total, self.sems = states, results, ins, outs, total, sems
        self.sums = sums
        self.rows = total.shape[1]
        lane = FF // n_shard // 4
        self.blocks = []
        share = n_shard // 4
        for k in range(4):
            runs = []
            for s in range(k * share, (k + 1) * share):
                for j in range(4):
                    runs.append((2 * j, s * lane, ((s - k * share) * 4 + j) * lane, lane))
            self.blocks.append((2, slice(0, self.rows), slice(k * WIDE, (k + 1) * WIDE), runs, 0.5 * D ** (-0.5)))
        for j in range(4):
            rows = slice(j * self.rows, (j + 1) * self.rows)
            self.blocks.append((3, rows, slice(0, WIDE), [(2 * j + 1, 0, 0, WIDE)], 0.5 * FF ** (-0.5)))
        for j in range(3):
            cols = slice(j * WIDE, (j + 1) * WIDE)
            runs = [(8 + j, 0, 0, WIDE)]
            self.blocks.append((0, slice(0, self.rows), cols, runs, 0.5 * D ** (-0.5)))
        runs = [(11, 0, 0, WIDE)]
        self.blocks.append((1, slice(0, self.rows), slice(0, WIDE), runs, 0.5 * (32.0 / D) ** 0.5))

    def load(self, i, k):
        kind, rows, cols = self.blocks[i][:3]
        return pltpu.make_async_copy(self.states[kind][k].at[rows, cols], self.ins.at[i % SLOTS, k], self.sems.at[0, i % SLOTS, k])

    def store(self, i, k):
        kind, rows, cols = self.blocks[i][:3]
        return pltpu.make_async_copy(self.outs.at[i % SLOTS, k], self.results[kind][k].at[rows, cols], self.sems.at[1, i % SLOTS, k])

    def grad(self, unit):
        return pltpu.make_async_copy(self.sums.at[unit], self.total.at[unit], self.sems.at[2, 0, unit])

    def begin(self, i):
        for k in range(3):
            self.load(i, k).start()

    def work(self, i):
        runs, rate = self.blocks[i][3:5]
        ring = i % SLOTS
        if i == 0:
            for unit in (0, 2, 4, 6):
                self.grad(unit).wait()
        elif i >= 4:
            self.grad(runs[0][0]).wait()
        for k in range(3):
            self.load(i, k).wait()
            if i >= SLOTS:
                self.store(i - SLOTS, k).wait()
        step = 16

        def body(r, _):
            rows = pl.ds(pl.multiple_of(r * step, step), step)
            for unit, start, to, count in runs:
                cols = slice(to, to + count)
                grad = self.total[unit, rows, start : start + count]
                new = adam(
                    self.ins[ring, 0, rows, cols], self.ins[ring, 1, rows, cols], self.ins[ring, 2, rows, cols],
                    grad, rate, weight_decay,
                )
                for k in range(3):
                    self.outs[ring, k, rows, cols] = new[k]
            return 0

        lax.fori_loop(0, self.rows // step, body, 0)
        for k in range(3):
            self.store(i, k).start()
        if i + SLOTS < len(self.blocks):
            self.begin(i + SLOTS)

    def drain(self):
        for i in range(len(self.blocks) - SLOTS, len(self.blocks)):
            for k in range(3):
                self.store(i, k).wait()


def finish_kernel(
    n_shard, sums, vec_sum, vec_state, out_done, in_done, qkv_state, out_state, fc1_state, fc2_state,
    output, input_grad, vec_new, qkv_new, out_new, fc1_new, fc2_new, ins, outs, total, passing, sems, whole,
):
    pairs = ((out_done, output), (in_done, input_grad))
    arrive = [pltpu.make_async_copy(src, passing.at[k], whole.at[k]) for k, (src, _) in enumerate(pairs)]
    leave = [pltpu.make_async_copy(passing.at[k], dst, whole.at[k]) for k, (_, dst) in enumerate(pairs)]
    optimizer = Adam(
        n_shard, (qkv_state, out_state, fc1_state, fc2_state), (qkv_new, out_new, fc1_new, fc2_new),
        ins, outs, total, sums, sems,
    )
    for unit in (0, 2, 4, 6):
        optimizer.grad(unit).start()
    for i in range(SLOTS):
        optimizer.begin(i)
    for unit in (1, 3, 5, 7, 8, 9, 10, 11):
        optimizer.grad(unit).start()
    for copy in arrive:
        copy.start()
    new = adam(vec_state[0][...], vec_state[1][...], vec_state[2][...], vec_sum[0:VEC_ROWS], vector_rate, 0.0)
    for k in range(3):
        vec_new[k][...] = new[k]
    for i in range(len(optimizer.blocks)):
        optimizer.work(i)
        if i == 3:
            for k in range(2):
                arrive[k].wait()
                leave[k].start()
    optimizer.drain()
    for copy in leave:
        copy.wait()


def finish(sums, vec_sum, vec_state, output, input_grad, states, n_shard):
    anywhere = pl.BlockSpec(memory_space=pl.ANY)
    vmem = pl.BlockSpec(memory_space=pltpu.VMEM)
    rows = sums.shape[1]
    like = lambda a: jax.ShapeDtypeStruct(a.shape, f32)
    return pl.pallas_call(
        functools.partial(finish_kernel, n_shard),
        out_shape=(
            like(output), like(input_grad), (like(vec_state[0]),) * 3, *((like(group[0]),) * 3 for group in states)
        ),
        in_specs=[anywhere, vmem, (vmem,) * 3, anywhere, anywhere] + [(anywhere,) * 3] * 4,
        out_specs=(anywhere, anywhere, (vmem,) * 3) + ((anywhere,) * 3,) * 4,
        scratch_shapes=[
            pltpu.VMEM((SLOTS, 3, rows, WIDE), f32),
            pltpu.VMEM((SLOTS, 3, rows, WIDE), f32),
            pltpu.VMEM((UNITS, rows, WIDE), f32),
            pltpu.VMEM((2,) + output.shape, f32),
            pltpu.SemaphoreType.DMA((3, SLOTS, UNITS)),
            pltpu.SemaphoreType.DMA((2,)),
        ],
        compiler_params=pltpu.CompilerParams(vmem_limit_bytes=62 * 2**20),
        name="update",
    )(sums, vec_sum, vec_state, output, input_grad, *states)


class Adam:
    def __init__(self, n_shard, states, results, ins, outs, total, sums, sems):
        self.states, self.results, self.ins, self.outs, self.total, self.sems = states, results, ins, outs, total, sems
        self.sums = sums
        self.rows = total.shape[1]
        lane = FF // n_shard // 4
        self.blocks = []
        share = n_shard // 4
        for k in range(4):
            runs = []
            for s in range(k * share, (k + 1) * share):
                for j in range(4):
                    runs.append((2 * j, s * lane, ((s - k * share) * 4 + j) * lane, lane))
            self.blocks.append((2, slice(0, self.rows), slice(k * WIDE, (k + 1) * WIDE), runs, 0.5 * D ** (-0.5)))
        for j in range(4):
            rows = slice(j * self.rows, (j + 1) * self.rows)
            self.blocks.append((3, rows, slice(0, WIDE), [(2 * j + 1, 0, 0, WIDE)], 0.5 * FF ** (-0.5)))
        for j in range(3):
            cols = slice(j * WIDE, (j + 1) * WIDE)
            runs = [(8 + j, 0, 0, WIDE)]
            self.blocks.append((0, slice(0, self.rows), cols, runs, 0.5 * D ** (-0.5)))
        runs = [(11, 0, 0, WIDE)]
        self.blocks.append((1, slice(0, self.rows), slice(0, WIDE), runs, 0.5 * (32.0 / D) ** 0.5))

    def load(self, i, k):
        kind, rows, cols = self.blocks[i][:3]
        return pltpu.make_async_copy(self.states[kind][k].at[rows, cols], self.ins.at[i % SLOTS, k], self.sems.at[0, i % SLOTS, k])

    def store(self, i, k):
        kind, rows, cols = self.blocks[i][:3]
        return pltpu.make_async_copy(self.outs.at[i % SLOTS, k], self.results[kind][k].at[rows, cols], self.sems.at[1, i % SLOTS, k])

    def grad(self, unit):
        return pltpu.make_async_copy(self.sums.at[unit], self.total.at[unit], self.sems.at[2, 0, unit])

    def begin(self, i):
        for k in range(3):
            self.load(i, k).start()

    def work(self, i):
        runs, rate = self.blocks[i][3:5]
        ring = i % SLOTS
        if i == 0:
            for unit in (0, 2, 4, 6):
                self.grad(unit).wait()
        elif i >= 4:
            self.grad(runs[0][0]).wait()
        for k in range(3):
            self.load(i, k).wait()
            if i >= SLOTS:
                self.store(i - SLOTS, k).wait()
        step = 16

        def body(r, _):
            rows = pl.ds(pl.multiple_of(r * step, step), step)
            for unit, start, to, count in runs:
                cols = slice(to, to + count)
                grad = self.total[unit, rows, start : start + count]
                new = adam(
                    self.ins[ring, 0, rows, cols], self.ins[ring, 1, rows, cols], self.ins[ring, 2, rows, cols],
                    grad, rate, weight_decay,
                )
                for k in range(3):
                    self.outs[ring, k, rows, cols] = new[k]
            return 0

        lax.fori_loop(0, self.rows // step, body, 0)
        for k in range(3):
            self.store(i, k).start()
        if i + SLOTS < len(self.blocks):
            self.begin(i + SLOTS)

    def drain(self):
        for i in range(len(self.blocks) - SLOTS, len(self.blocks)):
            for k in range(3):
                self.store(i, k).wait()


def finish_kernel(
    n_shard, sums, vec_sum, vec_state, out_done, in_done, qkv_state, out_state, fc1_state, fc2_state,
    output, input_grad, vec_new, qkv_new, out_new, fc1_new, fc2_new, ins, outs, total, passing, sems, whole,
):
    pairs = ((out_done, output), (in_done, input_grad))
    arrive = [pltpu.make_async_copy(src, passing.at[k], whole.at[k]) for k, (src, _) in enumerate(pairs)]
    leave = [pltpu.make_async_copy(passing.at[k], dst, whole.at[k]) for k, (_, dst) in enumerate(pairs)]
    optimizer = Adam(
        n_shard, (qkv_state, out_state, fc1_state, fc2_state), (qkv_new, out_new, fc1_new, fc2_new),
        ins, outs, total, sums, sems,
    )
    for unit in (0, 2, 4, 6):
        optimizer.grad(unit).start()
    for i in range(SLOTS):
        optimizer.begin(i)
    for unit in (1, 3, 5, 7, 8, 9, 10, 11):
        optimizer.grad(unit).start()
    for copy in arrive:
        copy.start()
    new = adam(vec_state[0][...], vec_state[1][...], vec_state[2][...], vec_sum[0:VEC_ROWS], vector_rate, 0.0)
    for k in range(3):
        vec_new[k][...] = new[k]
    for i in range(len(optimizer.blocks)):
        optimizer.work(i)
        if i == 3:
            for k in range(2):
                arrive[k].wait()
                leave[k].start()
    optimizer.drain()
    for copy in leave:
        copy.wait()


def finish(sums, vec_sum, vec_state, output, input_grad, states, n_shard):
    anywhere = pl.BlockSpec(memory_space=pl.ANY)
    vmem = pl.BlockSpec(memory_space=pltpu.VMEM)
    rows = sums.shape[1]
    like = lambda a: jax.ShapeDtypeStruct(a.shape, f32)
    return pl.pallas_call(
        functools.partial(finish_kernel, n_shard),
        out_shape=(
            like(output), like(input_grad), (like(vec_state[0]),) * 3, *((like(group[0]),) * 3 for group in states)
        ),
        in_specs=[anywhere, vmem, (vmem,) * 3, anywhere, anywhere] + [(anywhere,) * 3] * 4,
        out_specs=(anywhere, anywhere, (vmem,) * 3) + ((anywhere,) * 3,) * 4,
        scratch_shapes=[
            pltpu.VMEM((SLOTS, 3, rows, WIDE), f32),
            pltpu.VMEM((SLOTS, 3, rows, WIDE), f32),
            pltpu.VMEM((UNITS, rows, WIDE), f32),
            pltpu.VMEM((2,) + output.shape, f32),
            pltpu.SemaphoreType.DMA((3, SLOTS, UNITS)),
            pltpu.SemaphoreType.DMA((2,)),
        ],
        compiler_params=pltpu.CompilerParams(vmem_limit_bytes=62 * 2**20),
        name="update",
    )(sums, vec_sum, vec_state, output, input_grad, *states)


def lanes(vec, parts):
    return jnp.pad(vec.reshape(parts, VEC_ROWS, -1), ((0, 0), (0, 16 - VEC_ROWS), (0, 0)))


def adam(master, first, second, grad, rate, decay_on):
    first_new = beta_one * first + (1.0 - beta_one) * grad
    second_new = beta_two * second + (1.0 - beta_two) * grad * grad
    mhat = first_new / (1.0 - beta_one**STEP)
    vhat = second_new / (1.0 - beta_two**STEP)
    new = master - rate * (mhat / (jnp.sqrt(vhat) + epsilon) + decay_on * master)
    return (first_new, second_new, new)


def shards(
    tokens,
    cotangent,
    positions,
    qkv_master,
    qkv_first,
    qkv_second,
    out_master,
    out_first,
    out_second,
    fc1_master,
    fc1_first,
    fc1_second,
    fc2_master,
    fc2_first,
    fc2_second,
    vec_master,
    vec_first,
    vec_second,
):
    n_rep, n_shard = lax.axis_size("rep"), lax.axis_size("shard")
    vec_state = tuple(w.reshape(VEC_ROWS, -1) for w in (vec_master, vec_first, vec_second))
    late, early_grads, rows, part, d_two, act_one, grad_low, vec_early, valid, *tables = mlp(
        (qkv_master, out_master, fc1_master, fc2_master), vec_state[0], tokens, cotangent, positions[None],
        n_rep, n_shard,
    )
    states = (
        (qkv_master, qkv_first, qkv_second),
        (out_master, out_first, out_second),
        (fc1_master, fc1_first, fc1_second),
        (fc2_master, fc2_first, fc2_second),
    )
    output, input_grad, sums, vec_sum = attention(
        early_grads, late, rows, act_one, grad_low, tokens, cotangent, valid, part, d_two, positions[None],
        tables, vec_early, vec_state[0].shape[1], n_rep, n_shard,
    )
    output, input_grad, vec_new, *news = finish(sums, vec_sum, vec_state, output, input_grad, states, n_shard)
    vec_new = (w.reshape(-1) for w in vec_new)
    return (output, input_grad, *(w for new in news for w in new), *vec_new)


def solution(mesh):
    rows, owned, slots = P(("rep", "shard"), None), P("shard", None), P(("rep", "shard"))
    vector = P("shard")
    return jax.shard_map(
        shards,
        mesh=mesh,
        in_specs=(rows, rows, slots) + (owned,) * 12 + (vector,) * 3,
        out_specs=(rows, rows) + (owned,) * 12 + (vector,) * 3,
        check_vma=False,
    )
```

```python
import functools
import math

import jax
import jax.numpy as jnp
import numpy as np
from jax import lax
from jax.experimental import pallas as pl
from jax.experimental.pallas import tpu as pltpu
from jax.sharding import PartitionSpec as P

D = 1024
H = 16
HD = 64
FF = 4096
ROT = 16
STEP = 10

beta_one = 0.9
beta_two = 0.95
epsilon = 1e-08
weight_decay = 0.1
norm_eps = 1e-05
vector_rate = 0.1

MESH = pl.DeviceIdType.MESH
LANES = 128
UNITS = 12
WIDE = 1024
TILE = 256
EARLY = 8
PIECES = 24
STAGES = 4
SLOTS = 4
RING = 4
VEC_ROWS = 13
f32 = jnp.float32
bf16 = jnp.bfloat16


def dot(a, b):
    return jnp.dot(a, b, preferred_element_type=f32)


def dot_nt(a, b):
    return lax.dot_general(a, b, (((1,), (1,)), ((), ())), preferred_element_type=f32)


def dot_tn(a, b):
    return lax.dot_general(a, b, (((0,), (0,)), ((), ())), preferred_element_type=f32)


def run(first, count, width):
    return pl.ds(pl.multiple_of(first * width, LANES), count * width)


class Place:
    def __init__(self, n_rep, n_shard):
        self.n_rep, self.n_shard = n_rep, n_shard
        self.line = n_shard // 2
        self.bits = n_rep.bit_length() - 1
        self.rep = lax.axis_index("rep")
        self.shard = lax.axis_index("shard")
        self.core = lax.rem(self.shard, 2)
        self.spot = lax.div(self.shard, 2)
        digits = [lax.rem(lax.div(self.rep, 1 << p), 2) for p in range(self.bits)]
        turned = sum(digits[p] * (1 << (self.bits - 1 - p)) for p in range(self.bits))
        self.block = (1 - self.core) * self.rep + self.core * turned
        self.line_bits = self.line.bit_length() - 1
        self.line_digits = [lax.rem(lax.div(self.spot, 1 << q), 2) for q in range(self.line_bits)]
        self.twins = []
        for p in range(self.bits):
            q = self.bits - 1 - p
            step_even = (1 - 2 * digits[p]) * (1 << p)
            step_odd = (1 - 2 * digits[q]) * (1 << q)
            self.twins.append(self.rep + (1 - self.core) * step_even + self.core * step_odd)

    def hold(self, p):
        return lax.div(self.block, 1 << p) * (1 << p)

    def other(self, p):
        mine = lax.div(self.block, 1 << p)
        return (mine + 1 - 2 * lax.rem(mine, 2)) * (1 << p)

    def ahead(self, d):
        return lax.rem(self.spot + d, self.line)

    def behind(self, d):
        return lax.rem(self.spot + self.line - d, self.line)

    def along(self, d):
        return (self.rep, 2 * self.ahead(d) + self.core)

    def across(self, q):
        return (self.rep, self.shard + 2 * (1 - 2 * self.line_digits[q]) * (1 << q))

    def sibling(self):
        return (self.rep, self.shard + 1 - 2 * self.core)

    def twin(self, p):
        return (self.twins[p], self.shard)

    def group(self, d):
        return (self.rep, lax.rem(self.shard + d, self.n_shard))

    def replica(self, d):
        return (lax.rem(self.rep + d, self.n_rep), self.shard)

    def greet(self):
        barrier = pltpu.get_barrier_semaphore()
        peers = [self.group(d) for d in range(1, self.n_shard)]
        peers += [self.replica(d) for d in range(1, self.n_rep)]
        for peer in peers:
            pl.semaphore_signal(barrier, inc=1, device_id=peer, device_id_type=MESH)
        pl.semaphore_wait(barrier, len(peers))


class Copies:
    def __init__(self, send, recv):
        self.send, self.recv, self.used, self.sent = send, recv, 0, []

    def take(self, count):
        self.used += count
        return self.used - count

    def make(self, slot, src, dst, peer):
        return pltpu.make_async_remote_copy(
            src_ref=src,
            dst_ref=dst,
            send_sem=self.send.at[slot],
            recv_sem=self.recv.at[slot],
            device_id=peer,
            device_id_type=MESH,
        )

    def start(self, slot, src, dst, peer):
        copy = self.make(slot, src, dst, peer)
        copy.start()
        self.sent.append(copy)

    def arrived(self, slot, dst, peer):
        self.make(slot, dst, dst, peer).wait_recv()

    def drain(self):
        for copy in self.sent:
            copy.wait_send()


class Gather:
    def __init__(self, at, copies, full):
        self.at, self.copies, self.full = at, copies, full
        self.width = WIDE // at.n_rep
        self.half = full.shape[3] // 2
        self.per_piece = (at.line - 1) * (at.bits + 1) + at.line
        self.base = copies.take(self.per_piece * PIECES)

    def slot(self, v, p):
        return self.base + v * self.per_piece + p * (self.at.line - 1)

    def place(self, v, spot, core, cols=slice(None)):
        rows = pl.ds(pl.multiple_of(lax.rem(v, 2) * self.half, self.half), self.half)
        return self.full.at[lax.div(v, 2), spot, core, rows, cols]

    def line_send(self, v, d):
        at = self.at
        piece = self.place(v, at.spot, at.core, run(at.hold(0), 1, self.width))
        return self.copies.make(self.slot(v, 0) + d - 1, piece, piece, at.along(d))

    def twin_send(self, v, p, d):
        at = self.at
        piece = self.place(v, at.behind(d), at.core, run(at.hold(p), 1 << p, self.width))
        return self.copies.make(self.slot(v, p + 1) + d - 1, piece, piece, at.twin(p))

    def sibling_send(self, v, d):
        at = self.at
        piece = self.place(v, at.behind(d), at.core)
        return self.copies.make(self.slot(v, at.bits + 1) + d, piece, piece, at.sibling())

    def begin(self, v):
        for d in range(1, self.at.line):
            self.line_send(v, d).start()

    def stage(self, v, p):
        at = self.at
        if p == at.bits + 1:
            for d in range(at.line):
                self.copies.arrived(self.slot(v, p) + d, self.place(v, at.behind(d), 1 - at.core), at.sibling())
            return
        if p == at.bits:
            self.sibling_send(v, 0).start()
        for d in range(1, at.line):
            got = run(at.other(p - 1), 1 << (p - 1), self.width) if p > 0 else run(at.hold(0), 1, self.width)
            self.copies.arrived(
                self.slot(v, p) + d - 1,
                self.place(v, at.behind(d), at.core, got),
                at.twin(p - 1) if p > 0 else at.along(d),
            )
            if p < at.bits:
                self.twin_send(v, p, d).start()
            else:
                self.sibling_send(v, d).start()

    def step(self, t, first, last):
        if first == 0:
            if isinstance(t, int):
                if t + 3 < PIECES:
                    self.begin(t + 3)
            else:
                pl.when(t + 3 < PIECES)(lambda: self.begin(t + 3))
        for p in range(first, last):
            v = t - p
            if isinstance(t, int):
                if 0 <= v < PIECES:
                    self.stage(v, p)
            else:
                pl.when(v < PIECES)(functools.partial(self.stage, v, p))

    def drain(self, v):
        at = self.at
        for d in range(1, at.line):
            self.line_send(v, d).wait_send()
            for p in range(at.bits):
                self.twin_send(v, p, d).wait_send()
        for d in range(at.line):
            self.sibling_send(v, d).wait_send()


def vector_places(n_shard, lane):
    places = []
    for row in range(VEC_ROWS):
        for q in range(WIDE // lane):
            if 8 <= row < 12:
                start = 8 * WIDE + q * (FF // n_shard) + (row - 8) * lane
            else:
                start = row * WIDE + q * lane
            places.append((row, q * lane, start // lane // VEC_ROWS, start // lane % VEC_ROWS))
    return places


def mlp_kernel(
    n_rep, n_shard, qkv, out, fc1, fc2, vec_in, tokens_in, cot_in, positions, freqs,
    late, grads, rows_out, part_out, d_two_out, act_one_out, grad_low_out, grad_vec, valid, cosine, up, down,
    full, vec_own, vec_full, tokens, cot, part, d_two, act_one, grad_low,
    act_two, act_two_t, act, d_hidden, stage_grads, send, recv, local,
):
    at = Place(n_rep, n_shard)
    line, bits = at.line, at.bits
    shard_rows = full.shape[3]
    tall = TILE // (2 * shard_rows)
    count = tokens.shape[0]
    lane = vec_own.shape[1]

    def stage_block(b):
        return stage_grads.at[b // (2 * line), b % (2 * line) // 2, b % 2]

    sources = [fc1.at[:, k * WIDE : (k + 1) * WIDE] for k in range(4)]
    sources += [fc2.at[k * shard_rows : (k + 1) * shard_rows] for k in range(4)]
    sources += [qkv.at[:, k * WIDE : (k + 1) * WIDE] for k in range(3)] + [out]
    brought = [pltpu.make_async_copy(src, stage_block(b), local.at[b]) for b, src in enumerate(sources)]
    brought += [
        pltpu.make_async_copy(tokens_in, tokens, local.at[UNITS]),
        pltpu.make_async_copy(cot_in, cot, local.at[UNITS + 1]),
    ]
    for copy in brought:
        copy.start()
    vec_own[0:VEC_ROWS] = vec_in[...].astype(bf16).astype(f32)
    vec_own[VEC_ROWS:] = jnp.zeros((16 - VEC_ROWS, lane), f32)
    at.greet()
    copies = Copies(send, recv)
    gather = Gather(at, copies, full)
    vec_slot = copies.take(n_shard)
    for d in range(1, n_shard):
        copies.start(vec_slot + d, vec_own, vec_full.at[at.shard], at.group(d))

    for u in range(UNITS):
        if u == 0:
            for b in range(4):
                brought[b].wait()
        mine = full.at[u, at.spot, at.core]
        if u < 8 and u % 2 == 0:
            for s in range(n_shard):
                from_col = (4 * s + u // 2) * lane
                block = stage_block(from_col // WIDE)
                first = from_col % WIDE
                mine[:, s * lane : (s + 1) * lane] = block[:, first : first + lane].astype(bf16)
        else:
            b = 4 + u // 2 if u < 8 else u
            brought[b].wait()
            mine[...] = stage_block(b)[...].astype(bf16)
        for w in (2 * u, 2 * u + 1):
            if w < 3:
                gather.begin(w)
    vec_full[at.shard] = vec_own[...]

    place = jnp.broadcast_to(positions[...].astype(f32), (LANES, count)).T
    valid[...] = (place >= 0.0).astype(f32)
    angle = jnp.maximum(place, 0.0) * freqs[...]
    in_head = lax.rem(lax.broadcasted_iota(jnp.int32, (1, LANES), 1), HD)
    sine = jnp.sin(angle)
    cosine[...] = jnp.where(in_head < ROT, jnp.cos(angle), 1.0)
    up[...] = jnp.where(in_head < ROT // 2, -sine, 0.0)
    down[...] = jnp.where((in_head >= ROT // 2) & (in_head < ROT), sine, 0.0)

    step = 64
    brought[UNITS].wait()
    brought[UNITS + 1].wait()

    def lower(i, sums):
        rows = pl.ds(pl.multiple_of(i * step, step), step)
        low = (cot[rows] * valid[rows, 0:1]).astype(bf16)
        grad_low[rows] = low
        d_two[rows] = jnp.zeros((step, WIDE), f32)
        return sums + jnp.sum(low.astype(f32), axis=0, keepdims=True)

    grad_vec[4:5] = lax.fori_loop(0, count // step, lower, jnp.zeros((1, WIDE), f32))

    for d in range(1, n_shard):
        copies.arrived(vec_slot + d, vec_full.at[lax.rem(at.shard + n_shard - d, n_shard)], at.group(d))
    for row, first, device, spot in vector_places(n_shard, lane):
        rows_out[row : row + 1, first : first + lane] = vec_full[device, spot : spot + 1, :]

    def norm(i, _):
        rows = pl.ds(pl.multiple_of(i * step, step), step)
        x = tokens[rows].astype(f32)
        centred = x - jnp.mean(x, axis=-1, keepdims=True)
        var = jnp.mean(centred * centred, axis=-1, keepdims=True)
        unit = centred * lax.rsqrt(var + norm_eps)
        act_one[rows] = (unit * rows_out[0:1] + rows_out[1:2]).astype(bf16)
        act_two[rows] = (unit * rows_out[2:3] + rows_out[3:4]).astype(bf16)
        part[rows] = x + rows_out[12:13]
        return 0

    lax.fori_loop(0, count // step, norm, 0)
    act_two_t[...] = act_two[...].T

    def leaving(k):
        src, dst = ((act_one, act_one_out), (grad_low, grad_low_out), (part, part_out), (d_two, d_two_out))[k]
        return pltpu.make_async_copy(src, dst, local.at[UNITS + 2 + k])

    leaving(0).start()
    leaving(1).start()
    ahead = bits + 5
    for t in range(ahead):
        gather.step(t, 0, bits + 2)

    def out_copy(k, u):
        return pltpu.make_async_copy(stage_grads.at[k], grads.at[u], local.at[k])

    def tile(j, _):
        u1, u2 = 2 * j, 2 * j + 1

        def comm(q):
            t = ahead + 4 * j + q // 2
            if q % 2 == 0:
                gather.step(t, 0, bits)
            else:
                gather.step(t, bits, bits + 2)

        for q in range(4):
            comm(q)
            cols = slice(q * TILE, (q + 1) * TILE)
            spots = slice(q * tall, (q + 1) * tall)
            w1 = full[u1, :, :, :, cols].reshape(D, TILE)
            h = dot(act_two[...], w1) + rows_out[pl.ds(8 + j, 1), cols]
            below = 0.5 + 0.5 * lax.erf(h * (0.5**0.5))
            act[:, cols] = (h * below).astype(bf16)
            slope = below + h * (jnp.exp(-0.5 * h * h) * (1.0 / math.sqrt(2.0 * math.pi)))
            w2 = full[u2, spots].reshape(TILE, D)
            dh = (dot_nt(grad_low[...], w2) * slope).astype(bf16)
            d_hidden[:, cols] = dh
            grad_vec[pl.ds(j, 1), cols] = jnp.sum(dh.astype(f32), axis=0, keepdims=True)
        for q in range(4):
            comm(4 + q)
            cols = slice(q * TILE, (q + 1) * TILE)
            spots = slice(q * tall, (q + 1) * tall)
            if q == 0:

                @pl.when(j > 0)
                def _():
                    out_copy(0, 0).wait()
                    out_copy(1, 0).wait()

            part[:, cols] += dot(act[...], full[u2, :, :, :, cols].reshape(D, TILE))
            d_two[:, cols] += dot_nt(d_hidden[...], full[u1, spots].reshape(TILE, WIDE))
            stage_grads[1, spots] = dot_tn(act[:, cols], grad_low[...]).reshape(tall, 2, shard_rows, WIDE)
            stage_grads[0, spots] = dot(act_two_t[cols], d_hidden[...]).reshape(tall, 2, shard_rows, WIDE)
        out_copy(0, u1).start()
        out_copy(1, u2).start()
        return 0

    lax.fori_loop(0, 4, tile, 0)
    leaving(2).start()
    leaving(3).start()

    def late_copy(u):
        return pltpu.make_async_copy(full.at[u], late.at[u - 8], local.at[u])

    late_copy(8).start()
    late_copy(9).start()
    for t in range(ahead + 16, PIECES + bits + 1):
        gather.step(t, 0, bits + 2)
        if (t - bits - 1) % 2 == 1:
            late_copy((t - bits - 1) // 2).start()

    def finish(v, _):
        gather.drain(v)
        return 0

    lax.fori_loop(0, PIECES, finish, 0)
    copies.drain()
    out_copy(0, 0).wait()
    out_copy(1, 0).wait()
    for k in range(4):
        leaving(k).wait()
    for u in range(8, UNITS):
        late_copy(u).wait()


def mlp(masters, vec, tokens, cot, positions, n_rep, n_shard):
    shard_rows, line, bits = masters[1].shape[0], n_shard // 2, n_rep.bit_length() - 1
    slots = PIECES * ((line - 1) * (bits + 1) + line) + n_shard
    count = tokens.shape[0]
    anywhere = pl.BlockSpec(memory_space=pl.ANY)
    vmem = pl.BlockSpec(memory_space=pltpu.VMEM)
    unit = (line, 2, shard_rows, WIDE)
    freqs = 10000.0 ** (-(np.arange(LANES) % (ROT // 2)) * 2.0 / ROT)
    table = jax.ShapeDtypeStruct((count, LANES), f32)
    flat = lambda kind: pltpu.VMEM((count, WIDE), kind)
    return pl.pallas_call(
        functools.partial(mlp_kernel, n_rep, n_shard),
        out_shape=(
            jax.ShapeDtypeStruct((4,) + unit, bf16),
            jax.ShapeDtypeStruct((8,) + unit, f32),
            jax.ShapeDtypeStruct((16, WIDE), f32),
            jax.ShapeDtypeStruct((count, WIDE), f32),
            jax.ShapeDtypeStruct((count, WIDE), f32),
            jax.ShapeDtypeStruct((count, WIDE), bf16),
            jax.ShapeDtypeStruct((count, WIDE), bf16),
            jax.ShapeDtypeStruct((8, WIDE), f32),
            table, table, table, table,
        ),
        in_specs=[anywhere] * 4 + [vmem, anywhere, anywhere, vmem, vmem],
        out_specs=(anywhere, anywhere, vmem) + (anywhere,) * 4 + (vmem,) * 5,
        scratch_shapes=[
            pltpu.VMEM((UNITS,) + unit, bf16),
            pltpu.VMEM((16, vec.shape[1]), f32),
            pltpu.VMEM((n_shard, 16, vec.shape[1]), f32),
            flat(bf16), flat(f32), flat(f32), flat(f32), flat(bf16), flat(bf16),
            flat(bf16),
            pltpu.VMEM((WIDE, count), bf16),
            flat(bf16), flat(bf16),
            pltpu.VMEM((2,) + unit, f32),
            pltpu.SemaphoreType.DMA((slots,)),
            pltpu.SemaphoreType.DMA((slots,)),
            pltpu.SemaphoreType.DMA((UNITS + 6,)),
        ],
        compiler_params=pltpu.CompilerParams(
            collective_id=0, has_side_effects=True, vmem_limit_bytes=60 * 2**20
        ),
        name="gather_and_mlp",
    )(*masters, vec, tokens, cot, positions, jnp.asarray(freqs[None], f32))


def turn(u, tables, sign):
    cosine, up, down = tables
    return u * cosine + sign * (pltpu.roll(u, LANES - ROT // 2, 1) * up + pltpu.roll(u, ROT // 2, 1) * down)


class Reduce:
    def __init__(self, at, copies, early, late, sib, bufs, local):
        self.at, self.copies, self.early, self.late, self.sib, self.local = at, copies, early, late, sib, local
        (self.mine_buf, self.sib_buf, self.keep, self.halves_out, self.halves_in,
         self.line_keep, self.line_early, self.line_late, self.swap_out, self.swap_in, self.total) = bufs
        self.width = WIDE // at.n_rep
        self.half = early.shape[3] // 2
        self.per_piece = 1 + (at.bits - 1) + at.line_bits + 1 + (at.bits - 1)
        self.base = copies.take(self.per_piece * PIECES)
        self.stages = [self.fetch, self.first]
        self.stages += [functools.partial(self.later, p=p) for p in reversed(range(1, at.bits))]
        self.stages += [functools.partial(self.along, q=q) for q in range(1, at.line_bits)]
        self.stages += [self.swap]
        self.stages += [functools.partial(self.spread, p=p) for p in range(1, at.bits + 1)]
        self.lags = [0, 1] + [1 + 2 * (i + 1) for i in range(len(self.stages) - 2)]
        self.depth = self.lags[-1] + 1

    def slot(self, v, k):
        return self.base + v * self.per_piece + k

    def rows(self, v):
        return pl.ds(pl.multiple_of(lax.rem(v, 2) * self.half, self.half), self.half)

    def source(self, v, core):
        if isinstance(v, int) and v >= 2 * EARLY:
            return self.late.at[v // 2 - EARLY, :, core, pl.ds((v % 2) * self.half, self.half)]
        return self.early.at[lax.div(v, 2), :, core, self.rows(v)]

    def sums(self, v, first, count):
        return self.total.at[lax.div(v, 2), self.rows(v), run(first, count, self.width)]

    def sibling_copy(self, v):
        return self.copies.make(self.slot(v, 0), self.source(v, 1 - self.at.core), self.sib.at[v], self.at.sibling())

    def twin_copy(self, v, p):
        ring = lax.rem(v, RING)
        return self.copies.make(
            self.slot(v, self.at.bits - p),
            self.halves_out[p - 1].at[ring],
            self.halves_in[p - 1].at[ring],
            self.at.twin(p),
        )

    def line_bufs(self, v, q):
        late = q > 0 and isinstance(v, int) and v >= 2 * EARLY
        return self.line_late[q - 1] if late else self.line_early[q]

    def line_copy(self, v, q):
        ring = lax.rem(v, RING)
        out, got = self.line_bufs(v, q)
        return self.copies.make(self.slot(v, self.at.bits + q), out.at[ring], got.at[ring], self.at.across(q))

    def swap_copy(self, v):
        ring = lax.rem(v, RING)
        return self.copies.make(
            self.slot(v, self.at.bits + self.at.line_bits), self.swap_out.at[ring], self.swap_in.at[ring], self.at.twin(0)
        )

    def spread_copy(self, v, p):
        piece = self.sums(v, self.at.hold(p), 1 << p)
        return self.copies.make(self.slot(v, self.at.bits + self.at.line_bits + p), piece, piece, self.at.twin(p))

    def loads(self, v):
        return (
            pltpu.make_async_copy(self.source(v, self.at.core), self.mine_buf, self.local.at[0]),
            pltpu.make_async_copy(self.sib.at[v], self.sib_buf, self.local.at[1]),
        )

    def reuse(self, v, copies):
        def wait():
            for copy in copies(v - RING):
                copy.wait_send()

        if isinstance(v, int):
            if v >= RING:
                wait()
        else:
            pl.when(v >= RING)(wait)

    def fetch(self, v):
        self.sibling_copy(v).wait_recv()
        for copy in self.loads(v):
            copy.start()

    def first(self, v):
        at, width = self.at, self.width
        for copy in self.loads(v):
            copy.wait()
        p = at.bits - 1
        self.reuse(v, lambda w: [self.twin_copy(w, p)])
        to, stay = run(at.other(p), 1 << p, width), run(at.hold(p), 1 << p, width)
        ring = lax.rem(v, RING)

        def body(spot, _):
            a, b = self.mine_buf.at[spot], self.sib_buf.at[spot]
            self.halves_out[p - 1][ring, spot] = (a[:, to] + b[:, to]).astype(bf16)
            self.keep[p - 1][ring, spot] = a[:, stay] + b[:, stay]
            return 0

        lax.fori_loop(0, at.line, body, 0)
        self.twin_copy(v, p).start()

    def later(self, v, p):
        at = self.at
        ring = lax.rem(v, RING)
        self.twin_copy(v, p).wait_recv()

        def plane(spot, cols=slice(None)):
            return self.keep[p - 1][ring, spot, :, cols] + self.halves_in[p - 1][ring, spot, :, cols].astype(f32)

        if p > 1:
            self.reuse(v, lambda w: [self.twin_copy(w, p - 1)])
            half = self.width << (p - 1)
            side = lax.rem(lax.div(at.block, 1 << (p - 1)), 2)
            to, stay = run(1 - side, 1, half), run(side, 1, half)

            def body(spot, _):
                self.halves_out[p - 2][ring, spot] = plane(spot, to).astype(bf16)
                self.keep[p - 2][ring, spot] = plane(spot, stay)
                return 0

            lax.fori_loop(0, at.line, body, 0)
            self.twin_copy(v, p - 1).start()
            return
        self.reuse_line(v, 0)
        self.halve(v, 0, plane)

    def reuse_line(self, v, q):
        late = q > 0 and isinstance(v, int) and v >= 2 * EARLY
        if not late or v >= 2 * EARLY + RING:
            self.reuse(v, lambda w: [self.line_copy(w, q)])

    def halve(self, v, q, value):
        at, ring = self.at, lax.rem(v, RING)
        digit = at.line_digits[q]
        out = self.line_bufs(v, q)[0]
        for k in range(at.line >> (q + 1)):
            out[ring, k] = value(2 * k + 1 - digit).astype(out.dtype)
            self.line_keep[q][ring, k] = value(2 * k + digit)
        self.line_copy(v, q).start()

    def line_sum(self, v, q, k):
        ring = lax.rem(v, RING)
        return self.line_keep[q][ring, k] + self.line_bufs(v, q)[1][ring, k].astype(f32)

    def along(self, v, q):
        self.line_copy(v, q - 1).wait_recv()
        self.reuse_line(v, q)
        self.halve(v, q, lambda k: self.line_sum(v, q - 1, k))

    def swap(self, v):
        q = self.at.line_bits - 1
        self.line_copy(v, q).wait_recv()
        self.reuse(v, lambda w: [self.swap_copy(w)])
        self.swap_out[lax.rem(v, RING)] = self.line_sum(v, q, 0)
        self.swap_copy(v).start()

    def spread(self, v, p):
        at = self.at
        if p == 1:
            ring = lax.rem(v, RING)
            self.swap_copy(v).wait_recv()
            self.sums(v, at.hold(1), 2)[...] = self.swap_out[ring] + self.swap_in[ring]
        else:
            got = self.sums(v, at.other(p - 1), 1 << (p - 1))
            self.copies.make(self.slot(v, at.bits + at.line_bits + p - 1), got, got, at.twin(p - 1)).wait_recv()
        if p < at.bits:
            self.spread_copy(v, p).start()

    def jobs(self, t):
        out = []
        if isinstance(t, int):
            if t + 2 < PIECES:
                out.append(lambda: self.sibling_copy(t + 2).start())
        else:
            out.append(lambda: self.sibling_copy(t + 2).start())
        for i in reversed(range(len(self.stages))):
            v = t - self.lags[i]
            if isinstance(t, int):
                if 0 <= v < PIECES:
                    out.append(functools.partial(self.stages[i], v))
            else:
                out.append(functools.partial(lambda i, v: pl.when(v >= 0)(lambda: self.stages[i](v)), i, v))
        return out

    def drain(self):
        at = self.at
        for v in range(PIECES - RING, PIECES):
            for p in range(1, at.bits):
                self.twin_copy(v, p).wait_send()
            for q in range(at.line_bits):
                self.line_copy(v, q).wait_send()
            self.swap_copy(v).wait_send()
        for v in range(2 * EARLY - RING, 2 * EARLY):
            for q in range(1, at.line_bits):
                self.line_copy(v, q).wait_send()

        def body(v, _):
            self.sibling_copy(v).wait_send()
            for p in range(1, at.bits):
                self.spread_copy(v, p).wait_send()
            return 0

        lax.fori_loop(0, 2 * EARLY, body, 0)
        for v in range(2 * EARLY, PIECES):
            body(v, 0)


def attention_kernel(
    n_rep, n_shard, early, late, rows_in, act_one, grad_low, tokens, cot, valid, part_in, d_two_in, positions,
    cosine, up, down, vec_early,
    output, input_grad, sums_out, vec_sum, late_grads, sib,
    weights, part, d_two, query, keys, values, d_mixed, mixed, d_qkv, act_one_t, bias, d_one, stage_grads,
    grad_vec, vec_part, vec_got, vec_all, reduce_bufs, send, recv, local,
):
    at = Place(n_rep, n_shard)
    count = tokens.shape[0]
    line, shard_rows = late.shape[1], late.shape[3]
    tall = TILE // (2 * shard_rows)
    step = 64
    scale = HD**-0.5

    def bring(k, src, dst):
        return pltpu.make_async_copy(src, dst, local.at[2 + k])

    inputs = [(late.at[j], weights.at[j]) for j in range(4)] + [(part_in, part), (d_two_in, d_two)]
    for k, (src, dst) in enumerate(inputs):
        bring(k, src, dst).start()
    at.greet()
    copies = Copies(send, recv)
    reduce = Reduce(at, copies, early, late_grads, sib, reduce_bufs, local)
    vec_slot = copies.take(n_shard)
    vec_slot_rep = copies.take(n_rep)

    def begin(v, _):
        reduce.sibling_copy(v).start()
        return 0

    lax.fori_loop(0, 2, begin, 0)

    tables = (cosine[...], up[...], down[...])

    def weight(j, cols):
        return weights[j, :, :, :, cols].reshape(D, cols.stop - cols.start)

    key_idx = lax.broadcasted_iota(jnp.int32, (count, count), 0)
    query_idx = lax.broadcasted_iota(jnp.int32, (count, count), 1)
    allowed = (key_idx <= query_idx) & (key_idx >= query_idx - jnp.maximum(positions[...], 0))
    bias[...] = jnp.where(allowed, 0.0, -1e30)
    act_one_t[...] = act_one[...].T
    for k in range(4):
        bring(k, *inputs[k]).wait()

    queue = []
    clock = [0]

    def tick(number):
        for _ in range(number):
            while not queue:
                queue.extend(reduce.jobs(clock[0]))
                clock[0] += 1
            queue.pop(0)()

    def flush():
        while queue:
            queue.pop(0)()

    for q in range(4):
        if q % 2 == 0:
            queue.extend(reduce.jobs(clock[0]))
            clock[0] += 1
        flush()
        cols = slice(q * TILE, (q + 1) * TILE)
        spots = slice(q * tall, (q + 1) * tall)
        for j, target in enumerate((query, keys, values)):
            value = dot(act_one[...], weight(j, cols)) + rows_in[4 + j : 5 + j, cols]
            for half in range(TILE // LANES):
                piece = value[:, half * LANES : (half + 1) * LANES]
                if j < 2:
                    piece = turn(piece, tables, 1.0)
                piece = piece.astype(bf16)
                if j == 0:
                    piece = piece * jnp.asarray(scale, bf16)
                target[:, q * TILE + half * LANES : q * TILE + (half + 1) * LANES] = piece
        d_mixed[:, cols] = dot_nt(grad_low[...], weights[3, spots].reshape(TILE, WIDE)).astype(bf16)

    first_head = lax.broadcasted_iota(jnp.int32, (1, LANES), 1) < HD

    def pair(i):
        cols = pl.ds(pl.multiple_of(i * LANES, LANES), LANES)
        q2, k2, v2, o2 = query[:, cols], keys[:, cols], values[:, cols], d_mixed[:, cols]
        nothing = jnp.zeros((), bf16)
        blocks = count // TILE
        mixed_parts, dq_parts = [0.0] * blocks, [0.0] * blocks
        dk_parts, dv_parts = [0.0] * blocks, [0.0] * blocks
        for head in range(2):
            keep = first_head if head == 0 else jnp.logical_not(first_head)
            qm, km, vm, om = (jnp.where(keep, w, nothing) for w in (q2, k2, v2, o2))
            for b in range(blocks):
                span = slice(0, (b + 1) * TILE)
                mine = slice(b * TILE, (b + 1) * TILE)
                scores = dot_nt(k2[span], qm[mine]) + bias[span, mine]
                top = jnp.max(scores, axis=0, keepdims=True)
                expo = jnp.exp(scores - top)
                probs = expo * (1.0 / jnp.sum(expo, axis=0, keepdims=True))
                low = probs.astype(bf16)
                d_probs = dot_nt(v2[span], om[mine])
                inner = jnp.sum(probs * d_probs, axis=0, keepdims=True)
                d_scores = (probs * (d_probs - inner)).astype(bf16)
                mixed_parts[b] += dot_tn(low, vm[span])
                dq_parts[b] += dot_tn(d_scores, km[span])
                dv = dot(low, om[mine])
                dk = dot(d_scores, qm[mine])
                for c in range(b + 1):
                    dk_parts[c] += dk[c * TILE : (c + 1) * TILE]
                    dv_parts[c] += dv[c * TILE : (c + 1) * TILE]
        for b in range(blocks):
            mine = slice(b * TILE, (b + 1) * TILE)
            local_tables = (cosine[mine], up[mine], down[mine])
            mixed[mine, cols] = mixed_parts[b].astype(bf16)
            d_qkv[0, mine, cols] = turn(dq_parts[b] * scale, local_tables, -1.0).astype(bf16)
            d_qkv[1, mine, cols] = turn(dk_parts[b], local_tables, -1.0).astype(bf16)
            d_qkv[2, mine, cols] = dv_parts[b].astype(bf16)

    clock_here = clock[0]

    group, pace = 1, 1

    def some_pairs(i, _):
        jobs = [job for k in range(pace) for job in reduce.jobs(clock_here + pace * i + k)]
        for n in range(group):
            pair(group * i + n)
            for job in jobs[n * len(jobs) // group : (n + 1) * len(jobs) // group]:
                job()
        return 0

    lax.fori_loop(0, H // 2 // group, some_pairs, 0)
    clock[0] += pace * (H // 2 // group)

    def out_copy(k):
        j, q = k // 4, k % 4
        spots = pl.ds(q * tall, tall)
        return pltpu.make_async_copy(
            stage_grads.at[k % STAGES], late_grads.at[j, spots], local.at[2 + len(inputs) + k % STAGES]
        )

    for k in range(16):
        j, q = k // 4, k % 4
        if k >= STAGES:
            out_copy(k - STAGES).wait()
        cols = slice(q * TILE, (q + 1) * TILE)
        if j < 3:
            value = dot(act_one_t[cols], d_qkv[j])
        else:
            value = dot_tn(mixed[:, cols], grad_low[...])
        stage_grads[k % STAGES] = value.reshape(tall, 2, shard_rows, WIDE)
        out_copy(k).start()
        if k % 2 == 1:
            tick(1)
    for k in range(16 - STAGES, 16):
        out_copy(k).wait()
    bring(4, *inputs[4]).wait()
    bring(5, *inputs[5]).wait()
    for q in range(4):
        cols = slice(q * TILE, (q + 1) * TILE)
        spots = slice(q * tall, (q + 1) * tall)
        part[:, cols] += dot(mixed[...], weight(3, cols)) + rows_in[7:8, cols]
        value = dot_nt(d_qkv[0], weights[0, spots].reshape(TILE, WIDE))
        value += dot_nt(d_qkv[1], weights[1, spots].reshape(TILE, WIDE))
        value += dot_nt(d_qkv[2], weights[2, spots].reshape(TILE, WIDE))
        d_one[:, cols] = value
        tick(2)
    pltpu.make_async_copy(part, output, local.at[2]).start()
    for j in range(3):
        grad_vec[4 + j : 5 + j] = jnp.sum(d_qkv[j].astype(f32), axis=0, keepdims=True)

    def norm_back(i, sums):
        mine = pl.ds(pl.multiple_of(i * step, step), step)
        x = tokens[mine].astype(f32)
        centred = x - jnp.mean(x, axis=-1, keepdims=True)
        var = jnp.mean(centred * centred, axis=-1, keepdims=True)
        spread = lax.rsqrt(var + norm_eps)
        unit = centred * spread
        one, two = d_one[mine], d_two[mine]
        d_unit = one * rows_in[0:1] + two * rows_in[2:3]
        flat = jnp.mean(d_unit, axis=-1, keepdims=True)
        tilt = jnp.mean(d_unit * unit, axis=-1, keepdims=True)
        d_two[mine] = cot[mine] * valid[mine, 0:1] + spread * (d_unit - flat - unit * tilt)
        return tuple(
            s + jnp.sum(w, axis=0, keepdims=True) for s, w in zip(sums, (one * unit, one, two * unit, two))
        )

    sums = lax.fori_loop(0, count // step, norm_back, (jnp.zeros((1, WIDE), f32),) * 4)
    for k in range(4):
        grad_vec[k : k + 1] = sums[k]
    pltpu.make_async_copy(d_two, input_grad, local.at[3]).start()
    grad_vec[7:8] = vec_early[4:5]
    grad_vec[8:12] = vec_early[0:4]
    grad_vec[12:13] = vec_early[4:5]
    lane = vec_sum.shape[1]
    for row, start, device, place in vector_places(n_shard, lane):
        vec_part[device, place : place + 1, :] = grad_vec[row : row + 1, start : start + lane]
    for d in range(1, n_shard):
        to = lax.rem(at.shard + d, n_shard)
        copies.start(vec_slot + d, vec_part.at[to], vec_got.at[d], at.group(d))

    def vec_first():
        value = vec_part[at.shard]
        for d in range(1, n_shard):
            copies.arrived(vec_slot + d, vec_got.at[d], at.group(d))
            value = value + vec_got[d]
        vec_all[at.rep] = value
        for d in range(1, n_rep):
            copies.start(vec_slot_rep + d, vec_all.at[at.rep], vec_all.at[at.rep], at.replica(d))

    def vec_last():
        for d in range(1, n_rep):
            copies.arrived(vec_slot_rep + d, vec_all.at[lax.rem(at.rep + n_rep - d, n_rep)], at.replica(d))
        value = vec_all[0]
        for i in range(1, n_rep):
            value = value + vec_all[i]
        vec_sum[...] = value

    def result(u):
        return pltpu.make_async_copy(
            reduce_bufs[-1].at[u], sums_out.at[u], local.at[2 + len(inputs) + STAGES + u]
        )

    done = 0
    while queue or clock[0] < PIECES + reduce.depth - 1:
        tick(len(queue) or 1)
        flush()
        if clock[0] == 2 * EARLY:
            vec_first()
        if clock[0] == 2 * EARLY + 4:
            vec_last()
        while done < min(UNITS, (clock[0] - reduce.depth + 1) // 2):
            result(done).start()
            done += 1
    for u in range(UNITS):
        result(u).wait()
    reduce.drain()
    copies.drain()
    pltpu.make_async_copy(part, output, local.at[2]).wait()
    pltpu.make_async_copy(d_two, input_grad, local.at[3]).wait()


def attention(
    early, late, rows, act_one, grad_low, tokens, cot, valid, part, d_two, positions, tables, vec_early, lane,
    n_rep, n_shard,
):
    count = tokens.shape[0]
    unit = late.shape[1:]
    line, _, shard_rows, _ = unit
    bits, width, half = n_rep.bit_length() - 1, WIDE // n_rep, shard_rows // 2
    line_bits = line.bit_length() - 1
    slots = PIECES * (2 * bits + line_bits) + n_shard + n_rep
    anywhere = pl.BlockSpec(memory_space=pl.ANY)
    vmem = pl.BlockSpec(memory_space=pltpu.VMEM)
    flat = lambda: pltpu.VMEM((count, WIDE), bf16)
    outs = pl.pallas_call(
        functools.partial(attention_kernel, n_rep, n_shard),
        out_shape=(
            jax.ShapeDtypeStruct((count, WIDE), f32),
            jax.ShapeDtypeStruct((count, WIDE), f32),
            jax.ShapeDtypeStruct((UNITS, shard_rows, WIDE), f32),
            jax.ShapeDtypeStruct((16, lane), f32),
            jax.ShapeDtypeStruct((4,) + unit, f32),
            jax.ShapeDtypeStruct((PIECES, line, half, WIDE), f32),
        ),
        in_specs=[anywhere, anywhere] + [vmem] * 6 + [anywhere, anywhere] + [vmem] * 5,
        out_specs=(anywhere, anywhere, anywhere, vmem, anywhere, anywhere),
        scratch_shapes=[
            pltpu.VMEM((4,) + unit, bf16),
            pltpu.VMEM((count, WIDE), f32),
            pltpu.VMEM((count, WIDE), f32),
            flat(), flat(), flat(), flat(), flat(),
            pltpu.VMEM((3, count, WIDE), bf16),
            pltpu.VMEM((WIDE, count), bf16),
            pltpu.VMEM((count, count), f32),
            pltpu.VMEM((count, WIDE), f32),
            pltpu.VMEM((STAGES, TILE // (2 * shard_rows)) + unit[1:], f32),
            pltpu.VMEM((16, WIDE), f32),
            pltpu.VMEM((n_shard, 16, lane), f32),
            pltpu.VMEM((n_shard, 16, lane), f32),
            pltpu.VMEM((n_rep, 16, lane), f32),
            [
                pltpu.VMEM((line, half, WIDE), f32),
                pltpu.VMEM((line, half, WIDE), f32),
                [pltpu.VMEM((RING, line, half, width << p), f32) for p in range(1, bits)],
                [pltpu.VMEM((RING, line, half, width << p), bf16) for p in range(1, bits)],
                [pltpu.VMEM((RING, line, half, width << p), bf16) for p in range(1, bits)],
                [pltpu.VMEM((RING, line >> (q + 1), half, 2 * width), f32) for q in range(line_bits)],
                [[pltpu.VMEM((RING, line >> (q + 1), half, 2 * width), bf16)] * 2 for q in range(line_bits)],
                [[pltpu.VMEM((RING, line >> (q + 1), half, 2 * width), f32)] * 2 for q in range(1, line_bits)],
                pltpu.VMEM((RING, half, 2 * width), f32),
                pltpu.VMEM((RING, half, 2 * width), f32),
                pltpu.VMEM((UNITS, shard_rows, WIDE), f32),
            ],
            pltpu.SemaphoreType.DMA((slots,)),
            pltpu.SemaphoreType.DMA((slots,)),
            pltpu.SemaphoreType.DMA((2 + 6 + STAGES + UNITS,)),
        ],
        compiler_params=pltpu.CompilerParams(
            collective_id=1, has_side_effects=True, vmem_limit_bytes=62 * 2**20
        ),
        name="attention_and_sums",
    )(
        early, late, rows, act_one, grad_low, tokens, cot, valid, part, d_two, positions, *tables, vec_early
    )
    return outs[:4]


class Adam:
    def __init__(self, n_shard, states, results, ins, outs, total, sums, sems):
        self.states, self.results, self.ins, self.outs, self.total, self.sems = states, results, ins, outs, total, sems
        self.sums = sums
        self.rows = total.shape[1]
        lane = FF // n_shard // 4
        self.blocks = []
        share = n_shard // 4
        for k in range(4):
            runs = []
            for s in range(k * share, (k + 1) * share):
                for j in range(4):
                    runs.append((2 * j, s * lane, ((s - k * share) * 4 + j) * lane, lane))
            self.blocks.append((2, slice(0, self.rows), slice(k * WIDE, (k + 1) * WIDE), runs, 0.5 * D ** (-0.5)))
        for j in range(4):
            rows = slice(j * self.rows, (j + 1) * self.rows)
            self.blocks.append((3, rows, slice(0, WIDE), [(2 * j + 1, 0, 0, WIDE)], 0.5 * FF ** (-0.5)))
        for j in range(3):
            cols = slice(j * WIDE, (j + 1) * WIDE)
            runs = [(8 + j, 0, 0, WIDE)]
            self.blocks.append((0, slice(0, self.rows), cols, runs, 0.5 * D ** (-0.5)))
        runs = [(11, 0, 0, WIDE)]
        self.blocks.append((1, slice(0, self.rows), slice(0, WIDE), runs, 0.5 * (32.0 / D) ** 0.5))

    def load(self, i, k):
        kind, rows, cols = self.blocks[i][:3]
        return pltpu.make_async_copy(self.states[kind][k].at[rows, cols], self.ins.at[i % SLOTS, k], self.sems.at[0, i % SLOTS, k])

    def store(self, i, k):
        kind, rows, cols = self.blocks[i][:3]
        return pltpu.make_async_copy(self.outs.at[i % SLOTS, k], self.results[kind][k].at[rows, cols], self.sems.at[1, i % SLOTS, k])

    def grad(self, unit):
        return pltpu.make_async_copy(self.sums.at[unit], self.total.at[unit], self.sems.at[2, 0, unit])

    def begin(self, i):
        for k in range(3):
            self.load(i, k).start()

    def work(self, i):
        runs, rate = self.blocks[i][3:5]
        ring = i % SLOTS
        if i == 0:
            for unit in (0, 2, 4, 6):
                self.grad(unit).wait()
        elif i >= 4:
            self.grad(runs[0][0]).wait()
        for k in range(3):
            self.load(i, k).wait()
            if i >= SLOTS:
                self.store(i - SLOTS, k).wait()
        step = 16

        def body(r, _):
            rows = pl.ds(pl.multiple_of(r * step, step), step)
            for unit, start, to, count in runs:
                cols = slice(to, to + count)
                grad = self.total[unit, rows, start : start + count]
                new = adam(
                    self.ins[ring, 0, rows, cols], self.ins[ring, 1, rows, cols], self.ins[ring, 2, rows, cols],
                    grad, rate, weight_decay,
                )
                for k in range(3):
                    self.outs[ring, k, rows, cols] = new[k]
            return 0

        lax.fori_loop(0, self.rows // step, body, 0)
        for k in range(3):
            self.store(i, k).start()
        if i + SLOTS < len(self.blocks):
            self.begin(i + SLOTS)

    def drain(self):
        for i in range(len(self.blocks) - SLOTS, len(self.blocks)):
            for k in range(3):
                self.store(i, k).wait()


def finish_kernel(
    n_shard, sums, vec_sum, vec_state, out_done, in_done, qkv_state, out_state, fc1_state, fc2_state,
    output, input_grad, vec_new, qkv_new, out_new, fc1_new, fc2_new, ins, outs, total, passing, sems, whole,
):
    pairs = ((out_done, output), (in_done, input_grad))
    arrive = [pltpu.make_async_copy(src, passing.at[k], whole.at[k]) for k, (src, _) in enumerate(pairs)]
    leave = [pltpu.make_async_copy(passing.at[k], dst, whole.at[k]) for k, (_, dst) in enumerate(pairs)]
    optimizer = Adam(
        n_shard, (qkv_state, out_state, fc1_state, fc2_state), (qkv_new, out_new, fc1_new, fc2_new),
        ins, outs, total, sums, sems,
    )
    for unit in (0, 2, 4, 6):
        optimizer.grad(unit).start()
    for i in range(SLOTS):
        optimizer.begin(i)
    for unit in (1, 3, 5, 7, 8, 9, 10, 11):
        optimizer.grad(unit).start()
    for copy in arrive:
        copy.start()
    new = adam(vec_state[0][...], vec_state[1][...], vec_state[2][...], vec_sum[0:VEC_ROWS], vector_rate, 0.0)
    for k in range(3):
        vec_new[k][...] = new[k]
    for i in range(len(optimizer.blocks)):
        optimizer.work(i)
        if i == 3:
            for k in range(2):
                arrive[k].wait()
                leave[k].start()
    optimizer.drain()
    for copy in leave:
        copy.wait()


def finish(sums, vec_sum, vec_state, output, input_grad, states, n_shard):
    anywhere = pl.BlockSpec(memory_space=pl.ANY)
    vmem = pl.BlockSpec(memory_space=pltpu.VMEM)
    rows = sums.shape[1]
    like = lambda a: jax.ShapeDtypeStruct(a.shape, f32)
    return pl.pallas_call(
        functools.partial(finish_kernel, n_shard),
        out_shape=(
            like(output), like(input_grad), (like(vec_state[0]),) * 3, *((like(group[0]),) * 3 for group in states)
        ),
        in_specs=[anywhere, vmem, (vmem,) * 3, anywhere, anywhere] + [(anywhere,) * 3] * 4,
        out_specs=(anywhere, anywhere, (vmem,) * 3) + ((anywhere,) * 3,) * 4,
        scratch_shapes=[
            pltpu.VMEM((SLOTS, 3, rows, WIDE), f32),
            pltpu.VMEM((SLOTS, 3, rows, WIDE), f32),
            pltpu.VMEM(sums.shape, f32),
            pltpu.VMEM((2,) + output.shape, f32),
            pltpu.SemaphoreType.DMA((3, SLOTS, UNITS)),
            pltpu.SemaphoreType.DMA((2,)),
        ],
        compiler_params=pltpu.CompilerParams(vmem_limit_bytes=62 * 2**20),
        name="update",
    )(sums, vec_sum, vec_state, output, input_grad, *states)


def adam(master, first, second, grad, rate, decay_on):
    first_new = beta_one * first + (1.0 - beta_one) * grad
    second_new = beta_two * second + (1.0 - beta_two) * grad * grad
    mhat = first_new / (1.0 - beta_one**STEP)
    vhat = second_new / (1.0 - beta_two**STEP)
    new = master - rate * (mhat / (jnp.sqrt(vhat) + epsilon) + decay_on * master)
    return (first_new, second_new, new)


def shards(
    tokens,
    cotangent,
    positions,
    qkv_master,
    qkv_first,
    qkv_second,
    out_master,
    out_first,
    out_second,
    fc1_master,
    fc1_first,
    fc1_second,
    fc2_master,
    fc2_first,
    fc2_second,
    vec_master,
    vec_first,
    vec_second,
):
    n_rep, n_shard = lax.axis_size("rep"), lax.axis_size("shard")
    vec_state = tuple(w.reshape(VEC_ROWS, -1) for w in (vec_master, vec_first, vec_second))
    late, early_grads, rows, part, d_two, act_one, grad_low, vec_early, valid, *tables = mlp(
        (qkv_master, out_master, fc1_master, fc2_master), vec_state[0], tokens, cotangent, positions[None],
        n_rep, n_shard,
    )
    states = (
        (qkv_master, qkv_first, qkv_second),
        (out_master, out_first, out_second),
        (fc1_master, fc1_first, fc1_second),
        (fc2_master, fc2_first, fc2_second),
    )
    output, input_grad, sums, vec_sum = attention(
        early_grads, late, rows, act_one, grad_low, tokens, cotangent, valid, part, d_two, positions[None],
        tables, vec_early, vec_state[0].shape[1], n_rep, n_shard,
    )
    output, input_grad, vec_new, *news = finish(sums, vec_sum, vec_state, output, input_grad, states, n_shard)
    vec_new = (w.reshape(-1) for w in vec_new)
    return (output, input_grad, *(w for new in news for w in new), *vec_new)


def solution(mesh):
    rows, owned, slots = P(("rep", "shard"), None), P("shard", None), P(("rep", "shard"))
    vector = P("shard")
    return jax.shard_map(
        shards,
        mesh=mesh,
        in_specs=(rows, rows, slots) + (owned,) * 12 + (vector,) * 3,
        out_specs=(rows, rows) + (owned,) * 12 + (vector,) * 3,
        check_vma=False,
    )
```

```python
import functools
import math

import jax
import jax.numpy as jnp
import numpy as np
from jax import lax
from jax.experimental import pallas as pl
from jax.experimental.pallas import tpu as pltpu
from jax.sharding import PartitionSpec as P

D = 1024
H = 16
HD = 64
FF = 4096
ROT = 16
STEP = 10

beta_one = 0.9
beta_two = 0.95
epsilon = 1e-08
weight_decay = 0.1
norm_eps = 1e-05
vector_rate = 0.1

MESH = pl.DeviceIdType.MESH
LANES = 128
UNITS = 12
WIDE = 1024
TILE = 256
EARLY = 8
PIECES = 24
STAGES = 4
SLOTS = 4
RING = 4
LEAD = 2
VEC_ROWS = 13
f32 = jnp.float32
bf16 = jnp.bfloat16


def dot(a, b):
    return jnp.dot(a, b, preferred_element_type=f32)


def dot_nt(a, b):
    return lax.dot_general(a, b, (((1,), (1,)), ((), ())), preferred_element_type=f32)


def dot_tn(a, b):
    return lax.dot_general(a, b, (((0,), (0,)), ((), ())), preferred_element_type=f32)


def run(first, count, width):
    return pl.ds(pl.multiple_of(first * width, LANES), count * width)


class Place:
    def __init__(self, n_rep, n_shard):
        self.n_rep, self.n_shard = n_rep, n_shard
        self.line = n_shard // 2
        self.bits = n_rep.bit_length() - 1
        self.rep = lax.axis_index("rep")
        self.shard = lax.axis_index("shard")
        self.core = lax.rem(self.shard, 2)
        self.spot = lax.div(self.shard, 2)
        digits = [lax.rem(lax.div(self.rep, 1 << p), 2) for p in range(self.bits)]
        turned = sum(digits[p] * (1 << (self.bits - 1 - p)) for p in range(self.bits))
        self.block = (1 - self.core) * self.rep + self.core * turned
        self.line_bits = self.line.bit_length() - 1
        self.line_digits = [lax.rem(lax.div(self.spot, 1 << q), 2) for q in range(self.line_bits)]
        self.twins = []
        for p in range(self.bits):
            q = self.bits - 1 - p
            step_even = (1 - 2 * digits[p]) * (1 << p)
            step_odd = (1 - 2 * digits[q]) * (1 << q)
            self.twins.append(self.rep + (1 - self.core) * step_even + self.core * step_odd)

    def hold(self, p):
        return lax.div(self.block, 1 << p) * (1 << p)

    def other(self, p):
        mine = lax.div(self.block, 1 << p)
        return (mine + 1 - 2 * lax.rem(mine, 2)) * (1 << p)

    def ahead(self, d):
        return lax.rem(self.spot + d, self.line)

    def behind(self, d):
        return lax.rem(self.spot + self.line - d, self.line)

    def along(self, d):
        return (self.rep, 2 * self.ahead(d) + self.core)

    def across(self, q):
        return (self.rep, self.shard + 2 * (1 - 2 * self.line_digits[q]) * (1 << q))

    def mate(self, x):
        return self.spot + sum(
            (1 - 2 * self.line_digits[q]) * (1 << q) for q in range(self.line_bits) if x >> q & 1
        )

    def sibling(self):
        return (self.rep, self.shard + 1 - 2 * self.core)

    def twin(self, p):
        return (self.twins[p], self.shard)

    def group(self, d):
        return (self.rep, lax.rem(self.shard + d, self.n_shard))

    def replica(self, d):
        return (lax.rem(self.rep + d, self.n_rep), self.shard)

    def greet(self):
        barrier = pltpu.get_barrier_semaphore()
        peers = [self.group(d) for d in range(1, self.n_shard)]
        peers += [self.replica(d) for d in range(1, self.n_rep)]
        for peer in peers:
            pl.semaphore_signal(barrier, inc=1, device_id=peer, device_id_type=MESH)
        pl.semaphore_wait(barrier, len(peers))


class Copies:
    def __init__(self, send, recv):
        self.send, self.recv, self.used, self.sent = send, recv, 0, []

    def take(self, count):
        self.used += count
        return self.used - count

    def make(self, slot, src, dst, peer):
        return pltpu.make_async_remote_copy(
            src_ref=src,
            dst_ref=dst,
            send_sem=self.send.at[slot],
            recv_sem=self.recv.at[slot],
            device_id=peer,
            device_id_type=MESH,
        )

    def start(self, slot, src, dst, peer):
        copy = self.make(slot, src, dst, peer)
        copy.start()
        self.sent.append(copy)

    def arrived(self, slot, dst, peer):
        self.make(slot, dst, dst, peer).wait_recv()

    def drain(self):
        for copy in self.sent:
            copy.wait_send()


class Gather:
    def __init__(self, at, copies, full):
        self.at, self.copies, self.full = at, copies, full
        self.width = WIDE // at.n_rep
        self.half = full.shape[3] // 2
        self.per_piece = (at.line - 1) * (at.bits + 1) + at.line
        self.base = copies.take(self.per_piece * PIECES)
        self.last = at.line_bits + at.bits + 1

    def slot(self, v, p):
        return self.base + v * self.per_piece + p * (self.at.line - 1)

    def place(self, v, spot, core, cols=slice(None)):
        rows = pl.ds(pl.multiple_of(lax.rem(v, 2) * self.half, self.half), self.half)
        return self.full.at[lax.div(v, 2), spot, core, rows, cols]

    def line_piece(self, v, x):
        return self.place(v, self.at.mate(x), self.at.core, run(self.at.hold(0), 1, self.width))

    def line_sends(self, v, q):
        at = self.at
        out = []
        for x in range(0, at.line, 2 << q):
            piece = self.line_piece(v, x)
            out.append(self.copies.make(self.slot(v, 0) + x + (1 << q) - 1, piece, piece, at.across(q)))
        return out

    def line_arrived(self, v, q):
        for x in range(1 << q, self.at.line, 2 << q):
            self.copies.arrived(self.slot(v, 0) + x - 1, self.line_piece(v, x), self.at.across(q))

    def twin_send(self, v, p, x):
        at = self.at
        piece = self.place(v, at.mate(x), at.core, run(at.hold(p), 1 << p, self.width))
        return self.copies.make(self.slot(v, p + 1) + x - 1, piece, piece, at.twin(p))

    def sibling_send(self, v, x):
        at = self.at
        piece = self.place(v, at.mate(x), at.core)
        return self.copies.make(self.slot(v, at.bits + 1) + x, piece, piece, at.sibling())

    def stage(self, v, i):
        at = self.at
        top = at.line_bits - 1
        if i <= top:
            if i > 0:
                self.line_arrived(v, top - i + 1)
            for copy in self.line_sends(v, top - i):
                copy.start()
            return
        p = i - at.line_bits
        if p == at.bits + 1:
            for x in range(at.line):
                self.copies.arrived(self.slot(v, p) + x, self.place(v, at.mate(x), 1 - at.core), at.sibling())
            return
        if p == at.bits:
            self.sibling_send(v, 0).start()
        if p == 0:
            self.line_arrived(v, 0)
        for x in range(1, at.line):
            if p > 0:
                got = run(at.other(p - 1), 1 << (p - 1), self.width)
                self.copies.arrived(
                    self.slot(v, p) + x - 1, self.place(v, at.mate(x), at.core, got), at.twin(p - 1)
                )
            if p < at.bits:
                self.twin_send(v, p, x).start()
            else:
                self.sibling_send(v, x).start()

    def do(self, v, i):
        if not isinstance(v, int):
            pl.when(v < PIECES)(lambda: self.stage(v, i))
        elif 0 <= v < PIECES:
            self.stage(v, i)

    def step(self, t, first, last):
        for i in range(first, last):
            self.do(t - self.lags[i], i)

    @property
    def lags(self):
        line = [LEAD + i for i in range(self.at.line_bits)]
        twins = [line[-1] + 2 * (i + 1) for i in range(self.at.bits)]
        return [0] + line + twins + [twins[-1] + 1]

    def drain(self, v):
        at = self.at
        for q in range(at.line_bits):
            for copy in self.line_sends(v, q):
                copy.wait_send()
        for x in range(1, at.line):
            for p in range(at.bits):
                self.twin_send(v, p, x).wait_send()
        for x in range(at.line):
            self.sibling_send(v, x).wait_send()


def vector_places(n_shard, lane):
    places = []
    for row in range(VEC_ROWS):
        for q in range(WIDE // lane):
            if 8 <= row < 12:
                start = 8 * WIDE + q * (FF // n_shard) + (row - 8) * lane
            else:
                start = row * WIDE + q * lane
            places.append((row, q * lane, start // lane // VEC_ROWS, start // lane % VEC_ROWS))
    return places


def mlp_kernel(
    n_rep, n_shard, qkv, out, fc1, fc2, vec_in, tokens_in, cot_in, positions, freqs,
    late, grads, rows_out, part_out, d_two_out, act_one_out, grad_low_out, grad_vec, valid, cosine, up, down,
    full, vec_own, vec_full, tokens, cot, part, d_two, act_one, grad_low,
    act_two, act_two_t, act, d_hidden, stage_grads, send, recv, local,
):
    at = Place(n_rep, n_shard)
    line, bits = at.line, at.bits
    shard_rows = full.shape[3]
    tall = TILE // (2 * shard_rows)
    count = tokens.shape[0]
    lane = vec_own.shape[1]

    def stage_block(b):
        return stage_grads.at[b // (2 * line), b % (2 * line) // 2, b % 2]

    sources = [fc1.at[:, k * WIDE : (k + 1) * WIDE] for k in range(4)]
    sources += [fc2.at[k * shard_rows : (k + 1) * shard_rows] for k in range(4)]
    sources += [qkv.at[:, k * WIDE : (k + 1) * WIDE] for k in range(3)] + [out]
    brought = [pltpu.make_async_copy(src, stage_block(b), local.at[b]) for b, src in enumerate(sources)]
    brought += [
        pltpu.make_async_copy(tokens_in, tokens, local.at[UNITS]),
        pltpu.make_async_copy(cot_in, cot, local.at[UNITS + 1]),
    ]
    for copy in brought:
        copy.start()
    vec_own[0:VEC_ROWS] = vec_in[...].astype(bf16).astype(f32)
    vec_own[VEC_ROWS:] = jnp.zeros((16 - VEC_ROWS, lane), f32)
    at.greet()
    copies = Copies(send, recv)
    gather = Gather(at, copies, full)
    vec_slot = copies.take(n_shard)
    for d in range(1, n_shard):
        copies.start(vec_slot + d, vec_own, vec_full.at[at.shard], at.group(d))

    for u in range(UNITS):
        if u == 0:
            for b in range(4):
                brought[b].wait()
        mine = full.at[u, at.spot, at.core]
        if u < 8 and u % 2 == 0:
            for s in range(n_shard):
                from_col = (4 * s + u // 2) * lane
                block = stage_block(from_col // WIDE)
                first = from_col % WIDE
                mine[:, s * lane : (s + 1) * lane] = block[:, first : first + lane].astype(bf16)
        else:
            b = 4 + u // 2 if u < 8 else u
            brought[b].wait()
            mine[...] = stage_block(b)[...].astype(bf16)
        for w in (2 * u, 2 * u + 1):
            if w < LEAD:
                gather.step(w, 0, 1)
    vec_full[at.shard] = vec_own[...]

    step, part_rows = 64, count // 4
    in_head = lax.rem(lax.broadcasted_iota(jnp.int32, (1, LANES), 1), HD)

    def places():
        place = jnp.broadcast_to(positions[...].astype(f32), (LANES, count)).T
        valid[...] = (place >= 0.0).astype(f32)
        cosine[...] = jnp.maximum(place, 0.0) * freqs[...]

    def rotary(i):
        rows = slice(i * part_rows, (i + 1) * part_rows)
        angle = cosine[rows]
        sine = jnp.sin(angle)
        cosine[rows] = jnp.where(in_head < ROT, jnp.cos(angle), 1.0)
        up[rows] = jnp.where(in_head < ROT // 2, -sine, 0.0)
        down[rows] = jnp.where((in_head >= ROT // 2) & (in_head < ROT), sine, 0.0)

    def lower():
        brought[UNITS].wait()
        brought[UNITS + 1].wait()

        def body(i, sums):
            rows = pl.ds(pl.multiple_of(i * step, step), step)
            low = (cot[rows] * valid[rows, 0:1]).astype(bf16)
            grad_low[rows] = low
            d_two[rows] = jnp.zeros((step, WIDE), f32)
            return sums + jnp.sum(low.astype(f32), axis=0, keepdims=True)

        grad_vec[4:5] = lax.fori_loop(0, count // step, body, jnp.zeros((1, WIDE), f32))
        leaving(1).start()

    def vectors():
        for d in range(1, n_shard):
            copies.arrived(vec_slot + d, vec_full.at[lax.rem(at.shard + n_shard - d, n_shard)], at.group(d))
        for row, first, device, spot in vector_places(n_shard, lane):
            rows_out[row : row + 1, first : first + lane] = vec_full[device, spot : spot + 1, :]

    def norm(half):
        def body(i, _):
            rows = pl.ds(pl.multiple_of(i * step, step), step)
            x = tokens[rows].astype(f32)
            centred = x - jnp.mean(x, axis=-1, keepdims=True)
            var = jnp.mean(centred * centred, axis=-1, keepdims=True)
            unit = centred * lax.rsqrt(var + norm_eps)
            act_one[rows] = (unit * rows_out[0:1] + rows_out[1:2]).astype(bf16)
            act_two[rows] = (unit * rows_out[2:3] + rows_out[3:4]).astype(bf16)
            part[rows] = x + rows_out[12:13]
            return 0

        span = count // step // 2
        lax.fori_loop(half * span, (half + 1) * span, body, 0)

    def turned():
        leaving(0).start()
        act_two_t[...] = act_two[...].T

    def leaving(k):
        src, dst = ((act_one, act_one_out), (grad_low, grad_low_out), (part, part_out), (d_two, d_two_out))[k]
        return pltpu.make_async_copy(src, dst, local.at[UNITS + 2 + k])

    stages = gather.last + 1
    ahead = gather.lags[-1] + 4
    chores = [places, lower, vectors, lambda: norm(0), lambda: norm(1), turned]
    chores += [functools.partial(rotary, i) for i in range(4)]
    for t in range(LEAD, ahead):
        gather.step(t, 0, stages)
        if chores:
            chores.pop(0)()
    for chore in chores:
        chore()

    def out_copy(k, u):
        return pltpu.make_async_copy(stage_grads.at[k], grads.at[u], local.at[k])

    def tile(j, _):
        u1, u2 = 2 * j, 2 * j + 1

        def comm(q):
            t = ahead + 4 * j + q // 2
            if q % 2 == 0:
                gather.step(t, 0, stages - 2)
            else:
                gather.step(t, stages - 2, stages)

        for q in range(4):
            comm(q)
            cols = slice(q * TILE, (q + 1) * TILE)
            spots = slice(q * tall, (q + 1) * tall)
            w1 = full[u1, :, :, :, cols].reshape(D, TILE)
            h = dot(act_two[...], w1) + rows_out[pl.ds(8 + j, 1), cols]
            below = 0.5 + 0.5 * lax.erf(h * (0.5**0.5))
            act[:, cols] = (h * below).astype(bf16)
            slope = below + h * (jnp.exp(-0.5 * h * h) * (1.0 / math.sqrt(2.0 * math.pi)))
            w2 = full[u2, spots].reshape(TILE, D)
            dh = (dot_nt(grad_low[...], w2) * slope).astype(bf16)
            d_hidden[:, cols] = dh
            grad_vec[pl.ds(j, 1), cols] = jnp.sum(dh.astype(f32), axis=0, keepdims=True)
        for q in range(4):
            comm(4 + q)
            cols = slice(q * TILE, (q + 1) * TILE)
            spots = slice(q * tall, (q + 1) * tall)
            if q == 0:

                @pl.when(j > 0)
                def _():
                    out_copy(0, 0).wait()
                    out_copy(1, 0).wait()

            part[:, cols] += dot(act[...], full[u2, :, :, :, cols].reshape(D, TILE))
            d_two[:, cols] += dot_nt(d_hidden[...], full[u1, spots].reshape(TILE, WIDE))
            stage_grads[1, spots] = dot_tn(act[:, cols], grad_low[...]).reshape(tall, 2, shard_rows, WIDE)
            stage_grads[0, spots] = dot(act_two_t[cols], d_hidden[...]).reshape(tall, 2, shard_rows, WIDE)
        out_copy(0, u1).start()
        out_copy(1, u2).start()
        return 0

    lax.fori_loop(0, 4, tile, 0)
    leaving(2).start()
    leaving(3).start()

    def late_copy(u):
        return pltpu.make_async_copy(full.at[u], late.at[u - 8], local.at[u])

    late_copy(8).start()
    late_copy(9).start()
    for t in range(ahead + 16, PIECES + gather.lags[-1]):
        gather.step(t, 0, stages)
        done = t - gather.lags[-1]
        if done % 2 == 1:
            late_copy(done // 2).start()

    def finish(v, _):
        gather.drain(v)
        return 0

    lax.fori_loop(0, PIECES, finish, 0)
    copies.drain()
    out_copy(0, 0).wait()
    out_copy(1, 0).wait()
    for k in range(4):
        leaving(k).wait()
    for u in range(8, UNITS):
        late_copy(u).wait()


def mlp(masters, vec, tokens, cot, positions, n_rep, n_shard):
    shard_rows, line, bits = masters[1].shape[0], n_shard // 2, n_rep.bit_length() - 1
    slots = PIECES * ((line - 1) * (bits + 1) + line) + n_shard
    count = tokens.shape[0]
    anywhere = pl.BlockSpec(memory_space=pl.ANY)
    vmem = pl.BlockSpec(memory_space=pltpu.VMEM)
    unit = (line, 2, shard_rows, WIDE)
    freqs = 10000.0 ** (-(np.arange(LANES) % (ROT // 2)) * 2.0 / ROT)
    table = jax.ShapeDtypeStruct((count, LANES), f32)
    flat = lambda kind: pltpu.VMEM((count, WIDE), kind)
    return pl.pallas_call(
        functools.partial(mlp_kernel, n_rep, n_shard),
        out_shape=(
            jax.ShapeDtypeStruct((4,) + unit, bf16),
            jax.ShapeDtypeStruct((8,) + unit, f32),
            jax.ShapeDtypeStruct((16, WIDE), f32),
            jax.ShapeDtypeStruct((count, WIDE), f32),
            jax.ShapeDtypeStruct((count, WIDE), f32),
            jax.ShapeDtypeStruct((count, WIDE), bf16),
            jax.ShapeDtypeStruct((count, WIDE), bf16),
            jax.ShapeDtypeStruct((8, WIDE), f32),
            table, table, table, table,
        ),
        in_specs=[anywhere] * 4 + [vmem, anywhere, anywhere, vmem, vmem],
        out_specs=(anywhere, anywhere, vmem) + (anywhere,) * 4 + (vmem,) * 5,
        scratch_shapes=[
            pltpu.VMEM((UNITS,) + unit, bf16),
            pltpu.VMEM((16, vec.shape[1]), f32),
            pltpu.VMEM((n_shard, 16, vec.shape[1]), f32),
            flat(bf16), flat(f32), flat(f32), flat(f32), flat(bf16), flat(bf16),
            flat(bf16),
            pltpu.VMEM((WIDE, count), bf16),
            flat(bf16), flat(bf16),
            pltpu.VMEM((2,) + unit, f32),
            pltpu.SemaphoreType.DMA((slots,)),
            pltpu.SemaphoreType.DMA((slots,)),
            pltpu.SemaphoreType.DMA((UNITS + 6,)),
        ],
        compiler_params=pltpu.CompilerParams(
            collective_id=0, has_side_effects=True, vmem_limit_bytes=60 * 2**20
        ),
        name="gather_and_mlp",
    )(*masters, vec, tokens, cot, positions, jnp.asarray(freqs[None], f32))


def turn(u, tables, sign):
    cosine, up, down = tables
    return u * cosine + sign * (pltpu.roll(u, LANES - ROT // 2, 1) * up + pltpu.roll(u, ROT // 2, 1) * down)


class Reduce:
    def __init__(self, at, copies, early, late, sib, bufs, local):
        self.at, self.copies, self.early, self.late, self.sib, self.local = at, copies, early, late, sib, local
        (self.mine_buf, self.sib_buf, self.keep, self.halves_out, self.halves_in,
         self.line_keep, self.line_early, self.line_late, self.swap_out, self.swap_in, self.total) = bufs
        self.width = WIDE // at.n_rep
        self.half = early.shape[3] // 2
        self.per_piece = 1 + (at.bits - 1) + at.line_bits + 1 + (at.bits - 1)
        self.base = copies.take(self.per_piece * PIECES)
        self.stages = [self.fetch, self.first]
        self.stages += [functools.partial(self.later, p=p) for p in reversed(range(1, at.bits))]
        self.stages += [functools.partial(self.along, q=q) for q in range(1, at.line_bits)]
        self.stages += [self.swap]
        self.stages += [functools.partial(self.spread, p=p) for p in range(1, at.bits + 1)]
        self.lags = [0, 1] + [1 + 2 * (i + 1) for i in range(len(self.stages) - 2)]
        self.depth = self.lags[-1] + 1

    def slot(self, v, k):
        return self.base + v * self.per_piece + k

    def rows(self, v):
        return pl.ds(pl.multiple_of(lax.rem(v, 2) * self.half, self.half), self.half)

    def source(self, v, core):
        if isinstance(v, int) and v >= 2 * EARLY:
            return self.late.at[v // 2 - EARLY, :, core, pl.ds((v % 2) * self.half, self.half)]
        return self.early.at[lax.div(v, 2), :, core, self.rows(v)]

    def sums(self, v, first, count):
        return self.total.at[lax.div(v, 2), self.rows(v), run(first, count, self.width)]

    def sibling_copy(self, v):
        return self.copies.make(self.slot(v, 0), self.source(v, 1 - self.at.core), self.sib.at[v], self.at.sibling())

    def twin_copy(self, v, p):
        ring = lax.rem(v, RING)
        return self.copies.make(
            self.slot(v, self.at.bits - p),
            self.halves_out[p - 1].at[ring],
            self.halves_in[p - 1].at[ring],
            self.at.twin(p),
        )

    def line_bufs(self, v, q):
        late = q > 0 and isinstance(v, int) and v >= 2 * EARLY
        return self.line_late[q - 1] if late else self.line_early[q]

    def line_copy(self, v, q):
        ring = lax.rem(v, RING)
        out, got = self.line_bufs(v, q)
        return self.copies.make(self.slot(v, self.at.bits + q), out.at[ring], got.at[ring], self.at.across(q))

    def swap_copy(self, v):
        ring = lax.rem(v, RING)
        return self.copies.make(
            self.slot(v, self.at.bits + self.at.line_bits), self.swap_out.at[ring], self.swap_in.at[ring], self.at.twin(0)
        )

    def spread_copy(self, v, p):
        piece = self.sums(v, self.at.hold(p), 1 << p)
        return self.copies.make(self.slot(v, self.at.bits + self.at.line_bits + p), piece, piece, self.at.twin(p))

    def loads(self, v):
        return (
            pltpu.make_async_copy(self.source(v, self.at.core), self.mine_buf, self.local.at[0]),
            pltpu.make_async_copy(self.sib.at[v], self.sib_buf, self.local.at[1]),
        )

    def reuse(self, v, copies):
        def wait():
            for copy in copies(v - RING):
                copy.wait_send()

        if isinstance(v, int):
            if v >= RING:
                wait()
        else:
            pl.when(v >= RING)(wait)

    def fetch(self, v):
        self.sibling_copy(v).wait_recv()
        for copy in self.loads(v):
            copy.start()

    def first(self, v):
        at, width = self.at, self.width
        for copy in self.loads(v):
            copy.wait()
        p = at.bits - 1
        self.reuse(v, lambda w: [self.twin_copy(w, p)])
        to, stay = run(at.other(p), 1 << p, width), run(at.hold(p), 1 << p, width)
        ring = lax.rem(v, RING)

        def body(spot, _):
            a, b = self.mine_buf.at[spot], self.sib_buf.at[spot]
            self.halves_out[p - 1][ring, spot] = (a[:, to] + b[:, to]).astype(bf16)
            self.keep[p - 1][ring, spot] = a[:, stay] + b[:, stay]
            return 0

        lax.fori_loop(0, at.line, body, 0)
        self.twin_copy(v, p).start()

    def later(self, v, p):
        at = self.at
        ring = lax.rem(v, RING)
        self.twin_copy(v, p).wait_recv()

        def plane(spot, cols=slice(None)):
            return self.keep[p - 1][ring, spot, :, cols] + self.halves_in[p - 1][ring, spot, :, cols].astype(f32)

        if p > 1:
            self.reuse(v, lambda w: [self.twin_copy(w, p - 1)])
            half = self.width << (p - 1)
            side = lax.rem(lax.div(at.block, 1 << (p - 1)), 2)
            to, stay = run(1 - side, 1, half), run(side, 1, half)

            def body(spot, _):
                self.halves_out[p - 2][ring, spot] = plane(spot, to).astype(bf16)
                self.keep[p - 2][ring, spot] = plane(spot, stay)
                return 0

            lax.fori_loop(0, at.line, body, 0)
            self.twin_copy(v, p - 1).start()
            return
        self.reuse_line(v, 0)
        self.halve(v, 0, plane)

    def reuse_line(self, v, q):
        late = q > 0 and isinstance(v, int) and v >= 2 * EARLY
        if not late or v >= 2 * EARLY + RING:
            self.reuse(v, lambda w: [self.line_copy(w, q)])

    def halve(self, v, q, value):
        at, ring = self.at, lax.rem(v, RING)
        digit = at.line_digits[q]
        out = self.line_bufs(v, q)[0]
        for k in range(at.line >> (q + 1)):
            out[ring, k] = value(2 * k + 1 - digit).astype(out.dtype)
            self.line_keep[q][ring, k] = value(2 * k + digit)
        self.line_copy(v, q).start()

    def line_sum(self, v, q, k):
        ring = lax.rem(v, RING)
        return self.line_keep[q][ring, k] + self.line_bufs(v, q)[1][ring, k].astype(f32)

    def along(self, v, q):
        self.line_copy(v, q - 1).wait_recv()
        self.reuse_line(v, q)
        self.halve(v, q, lambda k: self.line_sum(v, q - 1, k))

    def swap(self, v):
        q = self.at.line_bits - 1
        self.line_copy(v, q).wait_recv()
        self.reuse(v, lambda w: [self.swap_copy(w)])
        self.swap_out[lax.rem(v, RING)] = self.line_sum(v, q, 0)
        self.swap_copy(v).start()

    def spread(self, v, p):
        at = self.at
        if p == 1:
            ring = lax.rem(v, RING)
            self.swap_copy(v).wait_recv()
            self.sums(v, at.hold(1), 2)[...] = self.swap_out[ring] + self.swap_in[ring]
        else:
            got = self.sums(v, at.other(p - 1), 1 << (p - 1))
            self.copies.make(self.slot(v, at.bits + at.line_bits + p - 1), got, got, at.twin(p - 1)).wait_recv()
        if p < at.bits:
            self.spread_copy(v, p).start()

    def jobs(self, t):
        out = []
        if isinstance(t, int):
            if t + 2 < PIECES:
                out.append(lambda: self.sibling_copy(t + 2).start())
        else:
            out.append(lambda: self.sibling_copy(t + 2).start())
        for i in reversed(range(len(self.stages))):
            v = t - self.lags[i]
            if isinstance(t, int):
                if 0 <= v < PIECES:
                    out.append(functools.partial(self.stages[i], v))
            else:
                out.append(functools.partial(lambda i, v: pl.when(v >= 0)(lambda: self.stages[i](v)), i, v))
        return out

    def drain(self):
        at = self.at
        for v in range(PIECES - RING, PIECES):
            for p in range(1, at.bits):
                self.twin_copy(v, p).wait_send()
            for q in range(at.line_bits):
                self.line_copy(v, q).wait_send()
            self.swap_copy(v).wait_send()
        for v in range(2 * EARLY - RING, 2 * EARLY):
            for q in range(1, at.line_bits):
                self.line_copy(v, q).wait_send()

        def body(v, _):
            self.sibling_copy(v).wait_send()
            for p in range(1, at.bits):
                self.spread_copy(v, p).wait_send()
            return 0

        lax.fori_loop(0, 2 * EARLY, body, 0)
        for v in range(2 * EARLY, PIECES):
            body(v, 0)


def attention_kernel(
    n_rep, n_shard, early, late, rows_in, act_one_in, grad_low_in, tokens_in, cot_in, valid_in, part_in, d_two_in, positions,
    cosine_in, up_in, down_in, vec_early,
    output, input_grad, sums_out, vec_sum, late_grads, sib,
    act_one, grad_low, tokens, cot, valid, cosine, up, down, weights, part, d_two, query, keys, values, d_mixed, mixed, d_qkv, act_one_t, bias, d_one, stage_grads,
    grad_vec, vec_part, vec_got, vec_all, reduce_bufs, send, recv, local,
):
    at = Place(n_rep, n_shard)
    count = tokens.shape[0]
    line, shard_rows = late.shape[1], late.shape[3]
    tall = TILE // (2 * shard_rows)
    step = 64
    scale = HD**-0.5

    def bring(k, src, dst):
        return pltpu.make_async_copy(src, dst, local.at[2 + k])

    inputs = [(late.at[j], weights.at[j]) for j in range(4)]
    inputs += [(act_one_in, act_one), (grad_low_in, grad_low), (cosine_in, cosine), (up_in, up), (down_in, down)]
    early_inputs = len(inputs)
    inputs += [(tokens_in, tokens), (cot_in, cot), (valid_in, valid), (part_in, part), (d_two_in, d_two)]
    for k, (src, dst) in enumerate(inputs):
        bring(k, src, dst).start()
    key_idx = lax.broadcasted_iota(jnp.int32, (count, count), 0)
    query_idx = lax.broadcasted_iota(jnp.int32, (count, count), 1)
    allowed = (key_idx <= query_idx) & (key_idx >= query_idx - jnp.maximum(positions[...], 0))
    bias[...] = jnp.where(allowed, 0.0, -1e30)
    at.greet()
    copies = Copies(send, recv)
    reduce = Reduce(at, copies, early, late_grads, sib, reduce_bufs, local)
    vec_slot = copies.take(n_shard)
    vec_slot_rep = copies.take(n_rep)

    def begin(v, _):
        reduce.sibling_copy(v).start()
        return 0

    lax.fori_loop(0, 2, begin, 0)

    def weight(j, cols):
        return weights[j, :, :, :, cols].reshape(D, cols.stop - cols.start)

    queue = []
    clock = [0]

    def tick(number):
        for _ in range(number):
            while not queue:
                queue.extend(reduce.jobs(clock[0]))
                clock[0] += 1
            queue.pop(0)()

    def flush():
        while queue:
            queue.pop(0)()

    def whole_step():
        queue.extend(reduce.jobs(clock[0]))
        clock[0] += 1
        flush()

    whole_step()
    whole_step()
    for k in range(early_inputs):
        bring(k, *inputs[k]).wait()
    tables = (cosine[...], up[...], down[...])
    act_one_t[...] = act_one[...].T

    for q in range(4):
        if q > 0:
            whole_step()
        cols = slice(q * TILE, (q + 1) * TILE)
        spots = slice(q * tall, (q + 1) * tall)
        for j, target in enumerate((query, keys, values)):
            value = dot(act_one[...], weight(j, cols)) + rows_in[4 + j : 5 + j, cols]
            for half in range(TILE // LANES):
                piece = value[:, half * LANES : (half + 1) * LANES]
                if j < 2:
                    piece = turn(piece, tables, 1.0)
                piece = piece.astype(bf16)
                if j == 0:
                    piece = piece * jnp.asarray(scale, bf16)
                target[:, q * TILE + half * LANES : q * TILE + (half + 1) * LANES] = piece
        d_mixed[:, cols] = dot_nt(grad_low[...], weights[3, spots].reshape(TILE, WIDE)).astype(bf16)

    first_head = lax.broadcasted_iota(jnp.int32, (1, LANES), 1) < HD

    def pair(i):
        cols = pl.ds(pl.multiple_of(i * LANES, LANES), LANES)
        q2, k2, v2, o2 = query[:, cols], keys[:, cols], values[:, cols], d_mixed[:, cols]
        nothing = jnp.zeros((), bf16)
        blocks = count // TILE
        mixed_parts, dq_parts = [0.0] * blocks, [0.0] * blocks
        dk_parts, dv_parts = [0.0] * blocks, [0.0] * blocks
        for head in range(2):
            keep = first_head if head == 0 else jnp.logical_not(first_head)
            qm, km, vm, om = (jnp.where(keep, w, nothing) for w in (q2, k2, v2, o2))
            for b in range(blocks):
                span = slice(0, (b + 1) * TILE)
                mine = slice(b * TILE, (b + 1) * TILE)
                scores = dot_nt(k2[span], qm[mine]) + bias[span, mine]
                top = jnp.max(scores, axis=0, keepdims=True)
                expo = jnp.exp(scores - top)
                probs = expo * (1.0 / jnp.sum(expo, axis=0, keepdims=True))
                low = probs.astype(bf16)
                d_probs = dot_nt(v2[span], om[mine])
                inner = jnp.sum(probs * d_probs, axis=0, keepdims=True)
                d_scores = (probs * (d_probs - inner)).astype(bf16)
                mixed_parts[b] += dot_tn(low, vm[span])
                dq_parts[b] += dot_tn(d_scores, km[span])
                dv = dot(low, om[mine])
                dk = dot(d_scores, qm[mine])
                for c in range(b + 1):
                    dk_parts[c] += dk[c * TILE : (c + 1) * TILE]
                    dv_parts[c] += dv[c * TILE : (c + 1) * TILE]
        for b in range(blocks):
            mine = slice(b * TILE, (b + 1) * TILE)
            local_tables = (cosine[mine], up[mine], down[mine])
            mixed[mine, cols] = mixed_parts[b].astype(bf16)
            d_qkv[0, mine, cols] = turn(dq_parts[b] * scale, local_tables, -1.0).astype(bf16)
            d_qkv[1, mine, cols] = turn(dk_parts[b], local_tables, -1.0).astype(bf16)
            d_qkv[2, mine, cols] = dv_parts[b].astype(bf16)

    clock_here = clock[0]

    group, pace = 1, 1

    def some_pairs(i, _):
        jobs = [job for k in range(pace) for job in reduce.jobs(clock_here + pace * i + k)]
        for n in range(group):
            pair(group * i + n)
            for job in jobs[n * len(jobs) // group : (n + 1) * len(jobs) // group]:
                job()
        return 0

    lax.fori_loop(0, H // 2 // group, some_pairs, 0)
    clock[0] += pace * (H // 2 // group)

    def out_copy(k):
        j, q = k // 4, k % 4
        spots = pl.ds(q * tall, tall)
        return pltpu.make_async_copy(
            stage_grads.at[k % STAGES], late_grads.at[j, spots], local.at[2 + len(inputs) + k % STAGES]
        )

    for k in range(16):
        j, q = k // 4, k % 4
        if k >= STAGES:
            out_copy(k - STAGES).wait()
        cols = slice(q * TILE, (q + 1) * TILE)
        if j < 3:
            value = dot(act_one_t[cols], d_qkv[j])
        else:
            value = dot_tn(mixed[:, cols], grad_low[...])
        stage_grads[k % STAGES] = value.reshape(tall, 2, shard_rows, WIDE)
        out_copy(k).start()
        if k % 2 == 1:
            tick(1)
    for k in range(16 - STAGES, 16):
        out_copy(k).wait()
    for k in range(early_inputs, len(inputs)):
        bring(k, *inputs[k]).wait()
    for q in range(4):
        cols = slice(q * TILE, (q + 1) * TILE)
        spots = slice(q * tall, (q + 1) * tall)
        part[:, cols] += dot(mixed[...], weight(3, cols)) + rows_in[7:8, cols]
        value = dot_nt(d_qkv[0], weights[0, spots].reshape(TILE, WIDE))
        value += dot_nt(d_qkv[1], weights[1, spots].reshape(TILE, WIDE))
        value += dot_nt(d_qkv[2], weights[2, spots].reshape(TILE, WIDE))
        d_one[:, cols] = value
        tick(2)
    pltpu.make_async_copy(part, output, local.at[2]).start()
    for j in range(3):
        grad_vec[4 + j : 5 + j] = jnp.sum(d_qkv[j].astype(f32), axis=0, keepdims=True)

    def norm_back(i, sums):
        mine = pl.ds(pl.multiple_of(i * step, step), step)
        x = tokens[mine].astype(f32)
        centred = x - jnp.mean(x, axis=-1, keepdims=True)
        var = jnp.mean(centred * centred, axis=-1, keepdims=True)
        spread = lax.rsqrt(var + norm_eps)
        unit = centred * spread
        one, two = d_one[mine], d_two[mine]
        d_unit = one * rows_in[0:1] + two * rows_in[2:3]
        flat = jnp.mean(d_unit, axis=-1, keepdims=True)
        tilt = jnp.mean(d_unit * unit, axis=-1, keepdims=True)
        d_two[mine] = cot[mine] * valid[mine, 0:1] + spread * (d_unit - flat - unit * tilt)
        return tuple(
            s + jnp.sum(w, axis=0, keepdims=True) for s, w in zip(sums, (one * unit, one, two * unit, two))
        )

    sums = lax.fori_loop(0, count // step, norm_back, (jnp.zeros((1, WIDE), f32),) * 4)
    for k in range(4):
        grad_vec[k : k + 1] = sums[k]
    pltpu.make_async_copy(d_two, input_grad, local.at[3]).start()
    grad_vec[7:8] = vec_early[4:5]
    grad_vec[8:12] = vec_early[0:4]
    grad_vec[12:13] = vec_early[4:5]
    lane = vec_sum.shape[1]
    for row, start, device, place in vector_places(n_shard, lane):
        vec_part[device, place : place + 1, :] = grad_vec[row : row + 1, start : start + lane]
    for d in range(1, n_shard):
        to = lax.rem(at.shard + d, n_shard)
        copies.start(vec_slot + d, vec_part.at[to], vec_got.at[d], at.group(d))

    def vec_first():
        value = vec_part[at.shard]
        for d in range(1, n_shard):
            copies.arrived(vec_slot + d, vec_got.at[d], at.group(d))
            value = value + vec_got[d]
        vec_all[at.rep] = value
        for d in range(1, n_rep):
            copies.start(vec_slot_rep + d, vec_all.at[at.rep], vec_all.at[at.rep], at.replica(d))

    def vec_last():
        for d in range(1, n_rep):
            copies.arrived(vec_slot_rep + d, vec_all.at[lax.rem(at.rep + n_rep - d, n_rep)], at.replica(d))
        value = vec_all[0]
        for i in range(1, n_rep):
            value = value + vec_all[i]
        vec_sum[...] = value

    def result(u):
        return pltpu.make_async_copy(
            reduce_bufs[-1].at[u], sums_out.at[u], local.at[2 + len(inputs) + STAGES + u]
        )

    done = 0
    vec_jobs = [vec_first, vec_last]
    while queue or clock[0] < PIECES + reduce.depth - 1:
        tick(len(queue) or 1)
        flush()
        if vec_jobs and clock[0] >= 2 * EARLY + 4 * (2 - len(vec_jobs)):
            vec_jobs.pop(0)()
        while done < min(UNITS, (clock[0] - reduce.depth + 1) // 2):
            result(done).start()
            done += 1
    for u in range(UNITS):
        result(u).wait()
    reduce.drain()
    copies.drain()
    pltpu.make_async_copy(part, output, local.at[2]).wait()
    pltpu.make_async_copy(d_two, input_grad, local.at[3]).wait()


def attention(
    early, late, rows, act_one, grad_low, tokens, cot, valid, part, d_two, positions, tables, vec_early, lane,
    n_rep, n_shard,
):
    count = tokens.shape[0]
    unit = late.shape[1:]
    line, _, shard_rows, _ = unit
    bits, width, half = n_rep.bit_length() - 1, WIDE // n_rep, shard_rows // 2
    line_bits = line.bit_length() - 1
    slots = PIECES * (2 * bits + line_bits) + n_shard + n_rep
    anywhere = pl.BlockSpec(memory_space=pl.ANY)
    vmem = pl.BlockSpec(memory_space=pltpu.VMEM)
    flat = lambda: pltpu.VMEM((count, WIDE), bf16)
    outs = pl.pallas_call(
        functools.partial(attention_kernel, n_rep, n_shard),
        out_shape=(
            jax.ShapeDtypeStruct((count, WIDE), f32),
            jax.ShapeDtypeStruct((count, WIDE), f32),
            jax.ShapeDtypeStruct((UNITS, shard_rows, WIDE), f32),
            jax.ShapeDtypeStruct((16, lane), f32),
            jax.ShapeDtypeStruct((4,) + unit, f32),
            jax.ShapeDtypeStruct((PIECES, line, half, WIDE), f32),
        ),
        in_specs=[anywhere, anywhere, vmem] + [anywhere] * 7 + [vmem] + [anywhere] * 3 + [vmem],
        out_specs=(anywhere, anywhere, anywhere, vmem, anywhere, anywhere),
        scratch_shapes=[
            flat(), flat(), flat(),
            pltpu.VMEM((count, WIDE), f32),
            *(pltpu.VMEM((count, LANES), f32) for _ in range(4)),
            pltpu.VMEM((4,) + unit, bf16),
            pltpu.VMEM((count, WIDE), f32),
            pltpu.VMEM((count, WIDE), f32),
            flat(), flat(), flat(), flat(), flat(),
            pltpu.VMEM((3, count, WIDE), bf16),
            pltpu.VMEM((WIDE, count), bf16),
            pltpu.VMEM((count, count), f32),
            pltpu.VMEM((count, WIDE), f32),
            pltpu.VMEM((STAGES, TILE // (2 * shard_rows)) + unit[1:], f32),
            pltpu.VMEM((16, WIDE), f32),
            pltpu.VMEM((n_shard, 16, lane), f32),
            pltpu.VMEM((n_shard, 16, lane), f32),
            pltpu.VMEM((n_rep, 16, lane), f32),
            [
                pltpu.VMEM((line, half, WIDE), f32),
                pltpu.VMEM((line, half, WIDE), f32),
                [pltpu.VMEM((RING, line, half, width << p), f32) for p in range(1, bits)],
                [pltpu.VMEM((RING, line, half, width << p), bf16) for p in range(1, bits)],
                [pltpu.VMEM((RING, line, half, width << p), bf16) for p in range(1, bits)],
                [pltpu.VMEM((RING, line >> (q + 1), half, 2 * width), f32) for q in range(line_bits)],
                [[pltpu.VMEM((RING, line >> (q + 1), half, 2 * width), bf16)] * 2 for q in range(line_bits)],
                [[pltpu.VMEM((RING, line >> (q + 1), half, 2 * width), f32)] * 2 for q in range(1, line_bits)],
                pltpu.VMEM((RING, half, 2 * width), f32),
                pltpu.VMEM((RING, half, 2 * width), f32),
                pltpu.VMEM((UNITS, shard_rows, WIDE), f32),
            ],
            pltpu.SemaphoreType.DMA((slots,)),
            pltpu.SemaphoreType.DMA((slots,)),
            pltpu.SemaphoreType.DMA((2 + 14 + STAGES + UNITS,)),
        ],
        compiler_params=pltpu.CompilerParams(
            collective_id=1, has_side_effects=True, vmem_limit_bytes=62 * 2**20
        ),
        name="attention_and_sums",
    )(
        early, late, rows, act_one, grad_low, tokens, cot, valid, part, d_two, positions, *tables, vec_early
    )
    return outs[:4]


class Adam:
    def __init__(self, n_shard, states, results, ins, outs, total, sums, sems):
        self.states, self.results, self.ins, self.outs, self.total, self.sems = states, results, ins, outs, total, sems
        self.sums = sums
        self.rows = total.shape[1]
        lane = FF // n_shard // 4
        self.blocks = []
        share = n_shard // 4
        for k in range(4):
            runs = []
            for s in range(k * share, (k + 1) * share):
                for j in range(4):
                    runs.append((2 * j, s * lane, ((s - k * share) * 4 + j) * lane, lane))
            self.blocks.append((2, slice(0, self.rows), slice(k * WIDE, (k + 1) * WIDE), runs, 0.5 * D ** (-0.5)))
        for j in range(4):
            rows = slice(j * self.rows, (j + 1) * self.rows)
            self.blocks.append((3, rows, slice(0, WIDE), [(2 * j + 1, 0, 0, WIDE)], 0.5 * FF ** (-0.5)))
        for j in range(3):
            cols = slice(j * WIDE, (j + 1) * WIDE)
            runs = [(8 + j, 0, 0, WIDE)]
            self.blocks.append((0, slice(0, self.rows), cols, runs, 0.5 * D ** (-0.5)))
        runs = [(11, 0, 0, WIDE)]
        self.blocks.append((1, slice(0, self.rows), slice(0, WIDE), runs, 0.5 * (32.0 / D) ** 0.5))

    def load(self, i, k):
        kind, rows, cols = self.blocks[i][:3]
        return pltpu.make_async_copy(self.states[kind][k].at[rows, cols], self.ins.at[i % SLOTS, k], self.sems.at[0, i % SLOTS, k])

    def store(self, i, k):
        kind, rows, cols = self.blocks[i][:3]
        return pltpu.make_async_copy(self.outs.at[i % SLOTS, k], self.results[kind][k].at[rows, cols], self.sems.at[1, i % SLOTS, k])

    def grad(self, unit):
        return pltpu.make_async_copy(self.sums.at[unit], self.total.at[unit], self.sems.at[2, 0, unit])

    def begin(self, i):
        for k in range(3):
            self.load(i, k).start()

    def work(self, i):
        runs, rate = self.blocks[i][3:5]
        ring = i % SLOTS
        if i == 0:
            for unit in (0, 2, 4, 6):
                self.grad(unit).wait()
        elif i >= 4:
            self.grad(runs[0][0]).wait()
        for k in range(3):
            self.load(i, k).wait()
            if i >= SLOTS:
                self.store(i - SLOTS, k).wait()
        step = 16

        def body(r, _):
            rows = pl.ds(pl.multiple_of(r * step, step), step)
            for unit, start, to, count in runs:
                cols = slice(to, to + count)
                grad = self.total[unit, rows, start : start + count]
                new = adam(
                    self.ins[ring, 0, rows, cols], self.ins[ring, 1, rows, cols], self.ins[ring, 2, rows, cols],
                    grad, rate, weight_decay,
                )
                for k in range(3):
                    self.outs[ring, k, rows, cols] = new[k]
            return 0

        lax.fori_loop(0, self.rows // step, body, 0)
        for k in range(3):
            self.store(i, k).start()
        if i + SLOTS < len(self.blocks):
            self.begin(i + SLOTS)

    def drain(self):
        for i in range(len(self.blocks) - SLOTS, len(self.blocks)):
            for k in range(3):
                self.store(i, k).wait()


def finish_kernel(
    n_shard, sums, vec_sum, vec_state, out_done, in_done, qkv_state, out_state, fc1_state, fc2_state,
    output, input_grad, vec_new, qkv_new, out_new, fc1_new, fc2_new, ins, outs, total, passing, sems, whole,
):
    pairs = ((out_done, output), (in_done, input_grad))
    arrive = [pltpu.make_async_copy(src, passing.at[k], whole.at[k]) for k, (src, _) in enumerate(pairs)]
    leave = [pltpu.make_async_copy(passing.at[k], dst, whole.at[k]) for k, (_, dst) in enumerate(pairs)]
    optimizer = Adam(
        n_shard, (qkv_state, out_state, fc1_state, fc2_state), (qkv_new, out_new, fc1_new, fc2_new),
        ins, outs, total, sums, sems,
    )
    for unit in (0, 2, 4, 6):
        optimizer.grad(unit).start()
    for i in range(SLOTS):
        optimizer.begin(i)
    for unit in (1, 3, 5, 7, 8, 9, 10, 11):
        optimizer.grad(unit).start()
    for copy in arrive:
        copy.start()
    new = adam(vec_state[0][...], vec_state[1][...], vec_state[2][...], vec_sum[0:VEC_ROWS], vector_rate, 0.0)
    for k in range(3):
        vec_new[k][...] = new[k]
    for i in range(len(optimizer.blocks)):
        optimizer.work(i)
        if i == 3:
            for k in range(2):
                arrive[k].wait()
                leave[k].start()
    optimizer.drain()
    for copy in leave:
        copy.wait()


def finish(sums, vec_sum, vec_state, output, input_grad, states, n_shard):
    anywhere = pl.BlockSpec(memory_space=pl.ANY)
    vmem = pl.BlockSpec(memory_space=pltpu.VMEM)
    rows = sums.shape[1]
    like = lambda a: jax.ShapeDtypeStruct(a.shape, f32)
    return pl.pallas_call(
        functools.partial(finish_kernel, n_shard),
        out_shape=(
            like(output), like(input_grad), (like(vec_state[0]),) * 3, *((like(group[0]),) * 3 for group in states)
        ),
        in_specs=[anywhere, vmem, (vmem,) * 3, anywhere, anywhere] + [(anywhere,) * 3] * 4,
        out_specs=(anywhere, anywhere, (vmem,) * 3) + ((anywhere,) * 3,) * 4,
        scratch_shapes=[
            pltpu.VMEM((SLOTS, 3, rows, WIDE), f32),
            pltpu.VMEM((SLOTS, 3, rows, WIDE), f32),
            pltpu.VMEM(sums.shape, f32),
            pltpu.VMEM((2,) + output.shape, f32),
            pltpu.SemaphoreType.DMA((3, SLOTS, UNITS)),
            pltpu.SemaphoreType.DMA((2,)),
        ],
        compiler_params=pltpu.CompilerParams(vmem_limit_bytes=62 * 2**20),
        name="update",
    )(sums, vec_sum, vec_state, output, input_grad, *states)


def adam(master, first, second, grad, rate, decay_on):
    first_new = beta_one * first + (1.0 - beta_one) * grad
    second_new = beta_two * second + (1.0 - beta_two) * grad * grad
    mhat = first_new / (1.0 - beta_one**STEP)
    vhat = second_new / (1.0 - beta_two**STEP)
    new = master - rate * (mhat / (jnp.sqrt(vhat) + epsilon) + decay_on * master)
    return (first_new, second_new, new)


def shards(
    tokens,
    cotangent,
    positions,
    qkv_master,
    qkv_first,
    qkv_second,
    out_master,
    out_first,
    out_second,
    fc1_master,
    fc1_first,
    fc1_second,
    fc2_master,
    fc2_first,
    fc2_second,
    vec_master,
    vec_first,
    vec_second,
):
    n_rep, n_shard = lax.axis_size("rep"), lax.axis_size("shard")
    vec_state = tuple(w.reshape(VEC_ROWS, -1) for w in (vec_master, vec_first, vec_second))
    late, early_grads, rows, part, d_two, act_one, grad_low, vec_early, valid, *tables = mlp(
        (qkv_master, out_master, fc1_master, fc2_master), vec_state[0], tokens, cotangent, positions[None],
        n_rep, n_shard,
    )
    states = (
        (qkv_master, qkv_first, qkv_second),
        (out_master, out_first, out_second),
        (fc1_master, fc1_first, fc1_second),
        (fc2_master, fc2_first, fc2_second),
    )
    output, input_grad, sums, vec_sum = attention(
        early_grads, late, rows, act_one, grad_low, tokens, cotangent, valid, part, d_two, positions[None],
        tables, vec_early, vec_state[0].shape[1], n_rep, n_shard,
    )
    output, input_grad, vec_new, *news = finish(sums, vec_sum, vec_state, output, input_grad, states, n_shard)
    vec_new = (w.reshape(-1) for w in vec_new)
    return (output, input_grad, *(w for new in news for w in new), *vec_new)


def solution(mesh):
    rows, owned, slots = P(("rep", "shard"), None), P("shard", None), P(("rep", "shard"))
    vector = P("shard")
    return jax.shard_map(
        shards,
        mesh=mesh,
        in_specs=(rows, rows, slots) + (owned,) * 12 + (vector,) * 3,
        out_specs=(rows, rows) + (owned,) * 12 + (vector,) * 3,
        check_vma=False,
    )
```

```python
import functools
import math

import jax
import jax.numpy as jnp
import numpy as np
from jax import lax
from jax.experimental import pallas as pl
from jax.experimental.pallas import tpu as pltpu
from jax.sharding import PartitionSpec as P

D = 1024
H = 16
HD = 64
FF = 4096
ROT = 16
STEP = 10

beta_one = 0.9
beta_two = 0.95
epsilon = 1e-08
weight_decay = 0.1
norm_eps = 1e-05
vector_rate = 0.1

MESH = pl.DeviceIdType.MESH
LANES = 128
UNITS = 12
WIDE = 1024
TILE = 256
EARLY = 8
PIECES = 24
STAGES = 4
SLOTS = 4
RING = 6
LEAD = 2
VEC_ROWS = 13
f32 = jnp.float32
bf16 = jnp.bfloat16


def dot(a, b):
    return jnp.dot(a, b, preferred_element_type=f32)


def dot_nt(a, b):
    return lax.dot_general(a, b, (((1,), (1,)), ((), ())), preferred_element_type=f32)


def dot_tn(a, b):
    return lax.dot_general(a, b, (((0,), (0,)), ((), ())), preferred_element_type=f32)


def run(first, count, width):
    return pl.ds(pl.multiple_of(first * width, LANES), count * width)


class Place:
    def __init__(self, n_rep, n_shard):
        self.n_rep, self.n_shard = n_rep, n_shard
        self.line = n_shard // 2
        self.bits = n_rep.bit_length() - 1
        self.rep = lax.axis_index("rep")
        self.shard = lax.axis_index("shard")
        self.core = lax.rem(self.shard, 2)
        self.spot = lax.div(self.shard, 2)
        digits = [lax.rem(lax.div(self.rep, 1 << p), 2) for p in range(self.bits)]
        turned = sum(digits[p] * (1 << (self.bits - 1 - p)) for p in range(self.bits))
        self.block = (1 - self.core) * self.rep + self.core * turned
        self.line_bits = self.line.bit_length() - 1
        self.line_digits = [lax.rem(lax.div(self.spot, 1 << q), 2) for q in range(self.line_bits)]
        self.twins = []
        for p in range(self.bits):
            q = self.bits - 1 - p
            step_even = (1 - 2 * digits[p]) * (1 << p)
            step_odd = (1 - 2 * digits[q]) * (1 << q)
            self.twins.append(self.rep + (1 - self.core) * step_even + self.core * step_odd)

    def hold(self, p):
        return lax.div(self.block, 1 << p) * (1 << p)

    def other(self, p):
        mine = lax.div(self.block, 1 << p)
        return (mine + 1 - 2 * lax.rem(mine, 2)) * (1 << p)

    def ahead(self, d):
        return lax.rem(self.spot + d, self.line)

    def behind(self, d):
        return lax.rem(self.spot + self.line - d, self.line)

    def along(self, d):
        return (self.rep, 2 * self.ahead(d) + self.core)

    def across(self, q):
        return (self.rep, self.shard + 2 * (1 - 2 * self.line_digits[q]) * (1 << q))

    def mate(self, x):
        return self.spot + sum(
            (1 - 2 * self.line_digits[q]) * (1 << q) for q in range(self.line_bits) if x >> q & 1
        )

    def sibling(self):
        return (self.rep, self.shard + 1 - 2 * self.core)

    def twin(self, p):
        return (self.twins[p], self.shard)

    def group(self, d):
        return (self.rep, lax.rem(self.shard + d, self.n_shard))

    def replica(self, d):
        return (lax.rem(self.rep + d, self.n_rep), self.shard)

    def greet(self):
        barrier = pltpu.get_barrier_semaphore()
        peers = [self.group(d) for d in range(1, self.n_shard)]
        peers += [self.replica(d) for d in range(1, self.n_rep)]
        for peer in peers:
            pl.semaphore_signal(barrier, inc=1, device_id=peer, device_id_type=MESH)
        pl.semaphore_wait(barrier, len(peers))


class Copies:
    def __init__(self, send, recv):
        self.send, self.recv, self.used, self.sent = send, recv, 0, []

    def take(self, count):
        self.used += count
        return self.used - count

    def make(self, slot, src, dst, peer):
        return pltpu.make_async_remote_copy(
            src_ref=src,
            dst_ref=dst,
            send_sem=self.send.at[slot],
            recv_sem=self.recv.at[slot],
            device_id=peer,
            device_id_type=MESH,
        )

    def start(self, slot, src, dst, peer):
        copy = self.make(slot, src, dst, peer)
        copy.start()
        self.sent.append(copy)

    def arrived(self, slot, dst, peer):
        self.make(slot, dst, dst, peer).wait_recv()

    def drain(self):
        for copy in self.sent:
            copy.wait_send()


class Gather:
    def __init__(self, at, copies, full):
        self.at, self.copies, self.full = at, copies, full
        self.width = WIDE // at.n_rep
        self.half = full.shape[3] // 2
        self.per_piece = (at.line - 1) * (at.bits + 1) + at.line
        self.base = copies.take(self.per_piece * PIECES)
        self.last = at.line_bits + at.bits + 1

    def slot(self, v, p):
        return self.base + v * self.per_piece + p * (self.at.line - 1)

    def place(self, v, spot, core, cols=slice(None)):
        rows = pl.ds(pl.multiple_of(lax.rem(v, 2) * self.half, self.half), self.half)
        return self.full.at[lax.div(v, 2), spot, core, rows, cols]

    def line_piece(self, v, x):
        return self.place(v, self.at.mate(x), self.at.core, run(self.at.hold(0), 1, self.width))

    def line_sends(self, v, q):
        at = self.at
        out = []
        for x in range(0, at.line, 2 << q):
            piece = self.line_piece(v, x)
            out.append(self.copies.make(self.slot(v, 0) + x + (1 << q) - 1, piece, piece, at.across(q)))
        return out

    def line_arrived(self, v, q):
        for x in range(1 << q, self.at.line, 2 << q):
            self.copies.arrived(self.slot(v, 0) + x - 1, self.line_piece(v, x), self.at.across(q))

    def twin_send(self, v, p, x):
        at = self.at
        piece = self.place(v, at.mate(x), at.core, run(at.hold(p), 1 << p, self.width))
        return self.copies.make(self.slot(v, p + 1) + x - 1, piece, piece, at.twin(p))

    def sibling_send(self, v, x):
        at = self.at
        piece = self.place(v, at.mate(x), at.core)
        return self.copies.make(self.slot(v, at.bits + 1) + x, piece, piece, at.sibling())

    def stage(self, v, i):
        at = self.at
        top = at.line_bits - 1
        if i <= top:
            if i > 0:
                self.line_arrived(v, top - i + 1)
            for copy in self.line_sends(v, top - i):
                copy.start()
            return
        p = i - at.line_bits
        if p == at.bits + 1:
            for x in range(at.line):
                self.copies.arrived(self.slot(v, p) + x, self.place(v, at.mate(x), 1 - at.core), at.sibling())
            return
        if p == at.bits:
            self.sibling_send(v, 0).start()
        if p == 0:
            self.line_arrived(v, 0)
        for x in range(1, at.line):
            if p > 0:
                got = run(at.other(p - 1), 1 << (p - 1), self.width)
                self.copies.arrived(
                    self.slot(v, p) + x - 1, self.place(v, at.mate(x), at.core, got), at.twin(p - 1)
                )
            if p < at.bits:
                self.twin_send(v, p, x).start()
            else:
                self.sibling_send(v, x).start()

    def do(self, v, i):
        if not isinstance(v, int):
            pl.when(v < PIECES)(lambda: self.stage(v, i))
        elif 0 <= v < PIECES:
            self.stage(v, i)

    def step(self, t, first, last):
        for i in range(first, last):
            self.do(t - self.lags[i], i)

    @property
    def lags(self):
        line = [LEAD + i for i in range(self.at.line_bits)]
        twins = [line[-1] + 2 * (i + 1) for i in range(self.at.bits)]
        return [0] + line + twins + [twins[-1] + 1]

    def drain(self, v):
        at = self.at
        for q in range(at.line_bits):
            for copy in self.line_sends(v, q):
                copy.wait_send()
        for x in range(1, at.line):
            for p in range(at.bits):
                self.twin_send(v, p, x).wait_send()
        for x in range(at.line):
            self.sibling_send(v, x).wait_send()


def vector_places(n_shard, lane):
    places = []
    for row in range(VEC_ROWS):
        for q in range(WIDE // lane):
            if 8 <= row < 12:
                start = 8 * WIDE + q * (FF // n_shard) + (row - 8) * lane
            else:
                start = row * WIDE + q * lane
            places.append((row, q * lane, start // lane // VEC_ROWS, start // lane % VEC_ROWS))
    return places


def mlp_kernel(
    n_rep, n_shard, qkv, out, fc1, fc2, vec_in, tokens_in, cot_in, positions, freqs,
    late, grads, rows_out, part_out, d_two_out, act_one_out, grad_low_out, grad_vec, valid, cosine, up, down,
    full, vec_own, vec_full, tokens, cot, part, d_two, act_one, grad_low,
    act_two, act_two_t, act, d_hidden, stage_grads, send, recv, local,
):
    at = Place(n_rep, n_shard)
    line, bits = at.line, at.bits
    shard_rows = full.shape[3]
    tall = TILE // (2 * shard_rows)
    count = tokens.shape[0]
    lane = vec_own.shape[1]

    def stage_block(b):
        return stage_grads.at[b // (2 * line), b % (2 * line) // 2, b % 2]

    sources = [fc1.at[:, k * WIDE : (k + 1) * WIDE] for k in range(4)]
    sources += [fc2.at[k * shard_rows : (k + 1) * shard_rows] for k in range(4)]
    sources += [qkv.at[:, k * WIDE : (k + 1) * WIDE] for k in range(3)] + [out]
    brought = [pltpu.make_async_copy(src, stage_block(b), local.at[b]) for b, src in enumerate(sources)]
    brought += [
        pltpu.make_async_copy(tokens_in, tokens, local.at[UNITS]),
        pltpu.make_async_copy(cot_in, cot, local.at[UNITS + 1]),
    ]
    for copy in brought:
        copy.start()
    vec_own[0:VEC_ROWS] = vec_in[...].astype(bf16).astype(f32)
    vec_own[VEC_ROWS:] = jnp.zeros((16 - VEC_ROWS, lane), f32)
    at.greet()
    copies = Copies(send, recv)
    gather = Gather(at, copies, full)
    vec_slot = copies.take(n_shard)
    for d in range(1, n_shard):
        copies.start(vec_slot + d, vec_own, vec_full.at[at.shard], at.group(d))

    for u in range(UNITS):
        if u == 0:
            for b in range(4):
                brought[b].wait()
        mine = full.at[u, at.spot, at.core]
        if u < 8 and u % 2 == 0:
            for s in range(n_shard):
                from_col = (4 * s + u // 2) * lane
                block = stage_block(from_col // WIDE)
                first = from_col % WIDE
                mine[:, s * lane : (s + 1) * lane] = block[:, first : first + lane].astype(bf16)
        else:
            b = 4 + u // 2 if u < 8 else u
            brought[b].wait()
            mine[...] = stage_block(b)[...].astype(bf16)
        for w in (2 * u, 2 * u + 1):
            if w < LEAD:
                gather.step(w, 0, 1)
    vec_full[at.shard] = vec_own[...]

    step, part_rows = 64, count // 4
    in_head = lax.rem(lax.broadcasted_iota(jnp.int32, (1, LANES), 1), HD)

    def places():
        place = jnp.broadcast_to(positions[...].astype(f32), (LANES, count)).T
        valid[...] = (place >= 0.0).astype(f32)
        cosine[...] = jnp.maximum(place, 0.0) * freqs[...]

    def rotary(i):
        rows = slice(i * part_rows, (i + 1) * part_rows)
        angle = cosine[rows]
        sine = jnp.sin(angle)
        cosine[rows] = jnp.where(in_head < ROT, jnp.cos(angle), 1.0)
        up[rows] = jnp.where(in_head < ROT // 2, -sine, 0.0)
        down[rows] = jnp.where((in_head >= ROT // 2) & (in_head < ROT), sine, 0.0)

    def lower():
        brought[UNITS].wait()
        brought[UNITS + 1].wait()

        def body(i, sums):
            rows = pl.ds(pl.multiple_of(i * step, step), step)
            low = (cot[rows] * valid[rows, 0:1]).astype(bf16)
            grad_low[rows] = low
            d_two[rows] = jnp.zeros((step, WIDE), f32)
            return sums + jnp.sum(low.astype(f32), axis=0, keepdims=True)

        grad_vec[4:5] = lax.fori_loop(0, count // step, body, jnp.zeros((1, WIDE), f32))
        leaving(1).start()

    def vectors():
        for d in range(1, n_shard):
            copies.arrived(vec_slot + d, vec_full.at[lax.rem(at.shard + n_shard - d, n_shard)], at.group(d))
        for row, first, device, spot in vector_places(n_shard, lane):
            rows_out[row : row + 1, first : first + lane] = vec_full[device, spot : spot + 1, :]

    def norm(half):
        def body(i, _):
            rows = pl.ds(pl.multiple_of(i * step, step), step)
            x = tokens[rows].astype(f32)
            centred = x - jnp.mean(x, axis=-1, keepdims=True)
            var = jnp.mean(centred * centred, axis=-1, keepdims=True)
            unit = centred * lax.rsqrt(var + norm_eps)
            act_one[rows] = (unit * rows_out[0:1] + rows_out[1:2]).astype(bf16)
            act_two[rows] = (unit * rows_out[2:3] + rows_out[3:4]).astype(bf16)
            part[rows] = x + rows_out[12:13]
            return 0

        span = count // step // 2
        lax.fori_loop(half * span, (half + 1) * span, body, 0)

    def turned():
        leaving(0).start()
        act_two_t[...] = act_two[...].T

    def leaving(k):
        src, dst = ((act_one, act_one_out), (grad_low, grad_low_out), (part, part_out), (d_two, d_two_out))[k]
        return pltpu.make_async_copy(src, dst, local.at[UNITS + 2 + k])

    stages = gather.last + 1
    ahead = gather.lags[-1] + 4
    chores = [places, lower, vectors, lambda: norm(0), lambda: norm(1), turned]
    chores += [functools.partial(rotary, i) for i in range(4)]
    for t in range(LEAD, ahead):
        gather.step(t, 0, stages)
        if chores:
            chores.pop(0)()
    for chore in chores:
        chore()

    def out_copy(k, u):
        return pltpu.make_async_copy(stage_grads.at[k], grads.at[u], local.at[k])

    def tile(j, _):
        u1, u2 = 2 * j, 2 * j + 1

        def comm(q):
            t = ahead + 4 * j + q // 2
            if q % 2 == 0:
                gather.step(t, 0, stages - 2)
            else:
                gather.step(t, stages - 2, stages)

        for q in range(4):
            comm(q)
            cols = slice(q * TILE, (q + 1) * TILE)
            spots = slice(q * tall, (q + 1) * tall)
            w1 = full[u1, :, :, :, cols].reshape(D, TILE)
            h = dot(act_two[...], w1) + rows_out[pl.ds(8 + j, 1), cols]
            below = 0.5 + 0.5 * lax.erf(h * (0.5**0.5))
            act[:, cols] = (h * below).astype(bf16)
            slope = below + h * (jnp.exp(-0.5 * h * h) * (1.0 / math.sqrt(2.0 * math.pi)))
            w2 = full[u2, spots].reshape(TILE, D)
            dh = (dot_nt(grad_low[...], w2) * slope).astype(bf16)
            d_hidden[:, cols] = dh
            grad_vec[pl.ds(j, 1), cols] = jnp.sum(dh.astype(f32), axis=0, keepdims=True)
        for q in range(4):
            comm(4 + q)
            cols = slice(q * TILE, (q + 1) * TILE)
            spots = slice(q * tall, (q + 1) * tall)
            if q == 0:

                @pl.when(j > 0)
                def _():
                    out_copy(0, 0).wait()
                    out_copy(1, 0).wait()

            part[:, cols] += dot(act[...], full[u2, :, :, :, cols].reshape(D, TILE))
            d_two[:, cols] += dot_nt(d_hidden[...], full[u1, spots].reshape(TILE, WIDE))
            stage_grads[1, spots] = dot_tn(act[:, cols], grad_low[...]).reshape(tall, 2, shard_rows, WIDE)
            stage_grads[0, spots] = dot(act_two_t[cols], d_hidden[...]).reshape(tall, 2, shard_rows, WIDE)
        out_copy(0, u1).start()
        out_copy(1, u2).start()
        return 0

    lax.fori_loop(0, 4, tile, 0)
    leaving(2).start()
    leaving(3).start()

    def late_copy(u):
        return pltpu.make_async_copy(full.at[u], late.at[u - 8], local.at[u])

    late_copy(8).start()
    late_copy(9).start()
    for t in range(ahead + 16, PIECES + gather.lags[-1]):
        gather.step(t, 0, stages)
        done = t - gather.lags[-1]
        if done % 2 == 1:
            late_copy(done // 2).start()

    def finish(v, _):
        gather.drain(v)
        return 0

    lax.fori_loop(0, PIECES, finish, 0)
    copies.drain()
    out_copy(0, 0).wait()
    out_copy(1, 0).wait()
    for k in range(4):
        leaving(k).wait()
    for u in range(8, UNITS):
        late_copy(u).wait()


def mlp(masters, vec, tokens, cot, positions, n_rep, n_shard):
    shard_rows, line, bits = masters[1].shape[0], n_shard // 2, n_rep.bit_length() - 1
    slots = PIECES * ((line - 1) * (bits + 1) + line) + n_shard
    count = tokens.shape[0]
    anywhere = pl.BlockSpec(memory_space=pl.ANY)
    vmem = pl.BlockSpec(memory_space=pltpu.VMEM)
    unit = (line, 2, shard_rows, WIDE)
    freqs = 10000.0 ** (-(np.arange(LANES) % (ROT // 2)) * 2.0 / ROT)
    table = jax.ShapeDtypeStruct((count, LANES), f32)
    flat = lambda kind: pltpu.VMEM((count, WIDE), kind)
    return pl.pallas_call(
        functools.partial(mlp_kernel, n_rep, n_shard),
        out_shape=(
            jax.ShapeDtypeStruct((4,) + unit, bf16),
            jax.ShapeDtypeStruct((8,) + unit, f32),
            jax.ShapeDtypeStruct((16, WIDE), f32),
            jax.ShapeDtypeStruct((count, WIDE), f32),
            jax.ShapeDtypeStruct((count, WIDE), f32),
            jax.ShapeDtypeStruct((count, WIDE), bf16),
            jax.ShapeDtypeStruct((count, WIDE), bf16),
            jax.ShapeDtypeStruct((8, WIDE), f32),
            table, table, table, table,
        ),
        in_specs=[anywhere] * 4 + [vmem, anywhere, anywhere, vmem, vmem],
        out_specs=(anywhere, anywhere, vmem) + (anywhere,) * 4 + (vmem,) * 5,
        scratch_shapes=[
            pltpu.VMEM((UNITS,) + unit, bf16),
            pltpu.VMEM((16, vec.shape[1]), f32),
            pltpu.VMEM((n_shard, 16, vec.shape[1]), f32),
            flat(bf16), flat(f32), flat(f32), flat(f32), flat(bf16), flat(bf16),
            flat(bf16),
            pltpu.VMEM((WIDE, count), bf16),
            flat(bf16), flat(bf16),
            pltpu.VMEM((2,) + unit, f32),
            pltpu.SemaphoreType.DMA((slots,)),
            pltpu.SemaphoreType.DMA((slots,)),
            pltpu.SemaphoreType.DMA((UNITS + 6,)),
        ],
        compiler_params=pltpu.CompilerParams(
            collective_id=0, has_side_effects=True, vmem_limit_bytes=60 * 2**20
        ),
        name="gather_and_mlp",
    )(*masters, vec, tokens, cot, positions, jnp.asarray(freqs[None], f32))


def turn(u, tables, sign):
    cosine, up, down = tables
    return u * cosine + sign * (pltpu.roll(u, LANES - ROT // 2, 1) * up + pltpu.roll(u, ROT // 2, 1) * down)


class Reduce:
    def __init__(self, at, copies, early, late, sib, bufs, local):
        self.at, self.copies, self.early, self.late, self.sib, self.local = at, copies, early, late, sib, local
        (self.mine_buf, self.sib_buf, self.keep, self.halves_out, self.halves_in,
         self.line_keep, self.line_early, self.line_late, self.swap_out, self.swap_in, self.total) = bufs
        self.width = WIDE // at.n_rep
        self.half = early.shape[3] // 2
        self.per_piece = 1 + (at.bits - 1) + at.line_bits + 1 + (at.bits - 1)
        self.base = copies.take(self.per_piece * PIECES)
        self.stages = [self.fetch, self.first]
        self.stages += [functools.partial(self.later, p=p) for p in reversed(range(1, at.bits))]
        self.stages += [functools.partial(self.along, q=q) for q in range(1, at.line_bits)]
        self.stages += [self.swap]
        self.stages += [functools.partial(self.spread, p=p) for p in range(1, at.bits + 1)]
        self.lags = [0, 1] + [1 + 3 * (i + 1) for i in range(len(self.stages) - 2)]
        self.depth = self.lags[-1] + 1

    def slot(self, v, k):
        return self.base + v * self.per_piece + k

    def rows(self, v):
        return pl.ds(pl.multiple_of(lax.rem(v, 2) * self.half, self.half), self.half)

    def source(self, v, core):
        if isinstance(v, int) and v >= 2 * EARLY:
            return self.late.at[v // 2 - EARLY, :, core, pl.ds((v % 2) * self.half, self.half)]
        return self.early.at[lax.div(v, 2), :, core, self.rows(v)]

    def sums(self, v, first, count):
        return self.total.at[lax.div(v, 2), self.rows(v), run(first, count, self.width)]

    def sibling_copy(self, v):
        return self.copies.make(self.slot(v, 0), self.source(v, 1 - self.at.core), self.sib.at[v], self.at.sibling())

    def twin_copy(self, v, p):
        ring = lax.rem(v, RING)
        return self.copies.make(
            self.slot(v, self.at.bits - p),
            self.halves_out[p - 1].at[ring],
            self.halves_in[p - 1].at[ring],
            self.at.twin(p),
        )

    def line_bufs(self, v, q):
        late = q > 0 and isinstance(v, int) and v >= 2 * EARLY
        return self.line_late[q - 1] if late else self.line_early[q]

    def line_copy(self, v, q):
        ring = lax.rem(v, RING)
        out, got = self.line_bufs(v, q)
        return self.copies.make(self.slot(v, self.at.bits + q), out.at[ring], got.at[ring], self.at.across(q))

    def swap_copy(self, v):
        ring = lax.rem(v, RING)
        return self.copies.make(
            self.slot(v, self.at.bits + self.at.line_bits), self.swap_out.at[ring], self.swap_in.at[ring], self.at.twin(0)
        )

    def spread_copy(self, v, p):
        piece = self.sums(v, self.at.hold(p), 1 << p)
        return self.copies.make(self.slot(v, self.at.bits + self.at.line_bits + p), piece, piece, self.at.twin(p))

    def loads(self, v):
        return (
            pltpu.make_async_copy(self.source(v, self.at.core), self.mine_buf, self.local.at[0]),
            pltpu.make_async_copy(self.sib.at[v], self.sib_buf, self.local.at[1]),
        )

    def reuse(self, v, copies):
        def wait():
            for copy in copies(v - RING):
                copy.wait_send()

        if isinstance(v, int):
            if v >= RING:
                wait()
        else:
            pl.when(v >= RING)(wait)

    def fetch(self, v):
        self.sibling_copy(v).wait_recv()
        for copy in self.loads(v):
            copy.start()

    def first(self, v):
        at, width = self.at, self.width
        for copy in self.loads(v):
            copy.wait()
        p = at.bits - 1
        self.reuse(v, lambda w: [self.twin_copy(w, p)])
        to, stay = run(at.other(p), 1 << p, width), run(at.hold(p), 1 << p, width)
        ring = lax.rem(v, RING)

        def body(spot, _):
            a, b = self.mine_buf.at[spot], self.sib_buf.at[spot]
            self.halves_out[p - 1][ring, spot] = (a[:, to] + b[:, to]).astype(bf16)
            self.keep[p - 1][ring, spot] = a[:, stay] + b[:, stay]
            return 0

        lax.fori_loop(0, at.line, body, 0)
        self.twin_copy(v, p).start()

    def later(self, v, p):
        at = self.at
        ring = lax.rem(v, RING)
        self.twin_copy(v, p).wait_recv()

        def plane(spot, cols=slice(None)):
            return self.keep[p - 1][ring, spot, :, cols] + self.halves_in[p - 1][ring, spot, :, cols].astype(f32)

        if p > 1:
            self.reuse(v, lambda w: [self.twin_copy(w, p - 1)])
            half = self.width << (p - 1)
            side = lax.rem(lax.div(at.block, 1 << (p - 1)), 2)
            to, stay = run(1 - side, 1, half), run(side, 1, half)

            def body(spot, _):
                self.halves_out[p - 2][ring, spot] = plane(spot, to).astype(bf16)
                self.keep[p - 2][ring, spot] = plane(spot, stay)
                return 0

            lax.fori_loop(0, at.line, body, 0)
            self.twin_copy(v, p - 1).start()
            return
        self.reuse_line(v, 0)
        self.halve(v, 0, plane)

    def reuse_line(self, v, q):
        late = q > 0 and isinstance(v, int) and v >= 2 * EARLY
        if not late or v >= 2 * EARLY + RING:
            self.reuse(v, lambda w: [self.line_copy(w, q)])

    def halve(self, v, q, value):
        at, ring = self.at, lax.rem(v, RING)
        digit = at.line_digits[q]
        out = self.line_bufs(v, q)[0]
        for k in range(at.line >> (q + 1)):
            out[ring, k] = value(2 * k + 1 - digit).astype(out.dtype)
            self.line_keep[q][ring, k] = value(2 * k + digit)
        self.line_copy(v, q).start()

    def line_sum(self, v, q, k):
        ring = lax.rem(v, RING)
        return self.line_keep[q][ring, k] + self.line_bufs(v, q)[1][ring, k].astype(f32)

    def along(self, v, q):
        self.line_copy(v, q - 1).wait_recv()
        self.reuse_line(v, q)
        self.halve(v, q, lambda k: self.line_sum(v, q - 1, k))

    def swap(self, v):
        q = self.at.line_bits - 1
        self.line_copy(v, q).wait_recv()
        self.reuse(v, lambda w: [self.swap_copy(w)])
        self.swap_out[lax.rem(v, RING)] = self.line_sum(v, q, 0)
        self.swap_copy(v).start()

    def spread(self, v, p):
        at = self.at
        if p == 1:
            ring = lax.rem(v, RING)
            self.swap_copy(v).wait_recv()
            self.sums(v, at.hold(1), 2)[...] = self.swap_out[ring] + self.swap_in[ring]
        else:
            got = self.sums(v, at.other(p - 1), 1 << (p - 1))
            self.copies.make(self.slot(v, at.bits + at.line_bits + p - 1), got, got, at.twin(p - 1)).wait_recv()
        if p < at.bits:
            self.spread_copy(v, p).start()

    def jobs(self, t):
        out = []
        if isinstance(t, int):
            if t + 2 < PIECES:
                out.append(lambda: self.sibling_copy(t + 2).start())
        else:
            out.append(lambda: self.sibling_copy(t + 2).start())
        for i in reversed(range(len(self.stages))):
            v = t - self.lags[i]
            if isinstance(t, int):
                if 0 <= v < PIECES:
                    out.append(functools.partial(self.stages[i], v))
            else:
                out.append(functools.partial(lambda i, v: pl.when(v >= 0)(lambda: self.stages[i](v)), i, v))
        return out

    def drain(self):
        at = self.at
        for v in range(PIECES - RING, PIECES):
            for p in range(1, at.bits):
                self.twin_copy(v, p).wait_send()
            for q in range(at.line_bits):
                self.line_copy(v, q).wait_send()
            self.swap_copy(v).wait_send()
        for v in range(2 * EARLY - RING, 2 * EARLY):
            for q in range(1, at.line_bits):
                self.line_copy(v, q).wait_send()

        def body(v, _):
            self.sibling_copy(v).wait_send()
            for p in range(1, at.bits):
                self.spread_copy(v, p).wait_send()
            return 0

        lax.fori_loop(0, 2 * EARLY, body, 0)
        for v in range(2 * EARLY, PIECES):
            body(v, 0)


def attention_kernel(
    n_rep, n_shard, early, late, rows_in, act_one_in, grad_low_in, tokens_in, cot_in, valid_in, part_in, d_two_in, positions,
    cosine_in, up_in, down_in, vec_early,
    output, input_grad, sums_out, vec_sum, late_grads, sib,
    act_one, grad_low, tokens, cot, valid, cosine, up, down, weights, part, d_two, query, keys, values, d_mixed, mixed, d_qkv, act_one_t, bias, d_one, stage_grads,
    grad_vec, vec_part, vec_got, vec_all, reduce_bufs, send, recv, local,
):
    at = Place(n_rep, n_shard)
    count = tokens.shape[0]
    line, shard_rows = late.shape[1], late.shape[3]
    tall = TILE // (2 * shard_rows)
    step = 64
    scale = HD**-0.5

    def bring(k, src, dst):
        return pltpu.make_async_copy(src, dst, local.at[2 + k])

    inputs = [(late.at[j], weights.at[j]) for j in range(4)]
    inputs += [(act_one_in, act_one), (grad_low_in, grad_low), (cosine_in, cosine), (up_in, up), (down_in, down)]
    early_inputs = len(inputs)
    inputs += [(tokens_in, tokens), (cot_in, cot), (valid_in, valid), (part_in, part), (d_two_in, d_two)]
    for k, (src, dst) in enumerate(inputs):
        bring(k, src, dst).start()
    key_idx = lax.broadcasted_iota(jnp.int32, (count, count), 0)
    query_idx = lax.broadcasted_iota(jnp.int32, (count, count), 1)
    allowed = (key_idx <= query_idx) & (key_idx >= query_idx - jnp.maximum(positions[...], 0))
    bias[...] = jnp.where(allowed, 0.0, -1e30)
    at.greet()
    copies = Copies(send, recv)
    reduce = Reduce(at, copies, early, late_grads, sib, reduce_bufs, local)
    vec_slot = copies.take(n_shard)
    vec_slot_rep = copies.take(n_rep)

    def begin(v, _):
        reduce.sibling_copy(v).start()
        return 0

    lax.fori_loop(0, 2, begin, 0)

    def weight(j, cols):
        return weights[j, :, :, :, cols].reshape(D, cols.stop - cols.start)

    queue = []
    clock = [0]

    def tick(number):
        for _ in range(number):
            while not queue:
                queue.extend(reduce.jobs(clock[0]))
                clock[0] += 1
            queue.pop(0)()

    def flush():
        while queue:
            queue.pop(0)()

    def whole_step():
        queue.extend(reduce.jobs(clock[0]))
        clock[0] += 1
        flush()

    whole_step()
    whole_step()
    for k in range(early_inputs):
        bring(k, *inputs[k]).wait()
    tables = (cosine[...], up[...], down[...])
    act_one_t[...] = act_one[...].T

    for q in range(4):
        if q > 0:
            whole_step()
        cols = slice(q * TILE, (q + 1) * TILE)
        spots = slice(q * tall, (q + 1) * tall)
        for j, target in enumerate((query, keys, values)):
            value = dot(act_one[...], weight(j, cols)) + rows_in[4 + j : 5 + j, cols]
            for half in range(TILE // LANES):
                piece = value[:, half * LANES : (half + 1) * LANES]
                if j < 2:
                    piece = turn(piece, tables, 1.0)
                piece = piece.astype(bf16)
                if j == 0:
                    piece = piece * jnp.asarray(scale, bf16)
                target[:, q * TILE + half * LANES : q * TILE + (half + 1) * LANES] = piece
        d_mixed[:, cols] = dot_nt(grad_low[...], weights[3, spots].reshape(TILE, WIDE)).astype(bf16)

    first_head = lax.broadcasted_iota(jnp.int32, (1, LANES), 1) < HD

    def pair(i):
        cols = pl.ds(pl.multiple_of(i * LANES, LANES), LANES)
        q2, k2, v2, o2 = query[:, cols], keys[:, cols], values[:, cols], d_mixed[:, cols]
        nothing = jnp.zeros((), bf16)
        blocks = count // TILE
        mixed_parts, dq_parts = [0.0] * blocks, [0.0] * blocks
        dk_parts, dv_parts = [0.0] * blocks, [0.0] * blocks
        for head in range(2):
            keep = first_head if head == 0 else jnp.logical_not(first_head)
            qm, km, vm, om = (jnp.where(keep, w, nothing) for w in (q2, k2, v2, o2))
            for b in range(blocks):
                span = slice(0, (b + 1) * TILE)
                mine = slice(b * TILE, (b + 1) * TILE)
                scores = dot_nt(k2[span], qm[mine]) + bias[span, mine]
                top = jnp.max(scores, axis=0, keepdims=True)
                expo = jnp.exp(scores - top)
                probs = expo * (1.0 / jnp.sum(expo, axis=0, keepdims=True))
                low = probs.astype(bf16)
                d_probs = dot_nt(v2[span], om[mine])
                inner = jnp.sum(probs * d_probs, axis=0, keepdims=True)
                d_scores = (probs * (d_probs - inner)).astype(bf16)
                mixed_parts[b] += dot_tn(low, vm[span])
                dq_parts[b] += dot_tn(d_scores, km[span])
                dv = dot(low, om[mine])
                dk = dot(d_scores, qm[mine])
                for c in range(b + 1):
                    dk_parts[c] += dk[c * TILE : (c + 1) * TILE]
                    dv_parts[c] += dv[c * TILE : (c + 1) * TILE]
        for b in range(blocks):
            mine = slice(b * TILE, (b + 1) * TILE)
            local_tables = (cosine[mine], up[mine], down[mine])
            mixed[mine, cols] = mixed_parts[b].astype(bf16)
            d_qkv[0, mine, cols] = turn(dq_parts[b] * scale, local_tables, -1.0).astype(bf16)
            d_qkv[1, mine, cols] = turn(dk_parts[b], local_tables, -1.0).astype(bf16)
            d_qkv[2, mine, cols] = dv_parts[b].astype(bf16)

    clock_here = clock[0]

    group, pace = 1, 1

    def some_pairs(i, _):
        jobs = [job for k in range(pace) for job in reduce.jobs(clock_here + pace * i + k)]
        for n in range(group):
            pair(group * i + n)
            for job in jobs[n * len(jobs) // group : (n + 1) * len(jobs) // group]:
                job()
        return 0

    lax.fori_loop(0, H // 2 // group, some_pairs, 0)
    clock[0] += pace * (H // 2 // group)

    def out_copy(k):
        j, q = k // 4, k % 4
        spots = pl.ds(q * tall, tall)
        return pltpu.make_async_copy(
            stage_grads.at[k % STAGES], late_grads.at[j, spots], local.at[2 + len(inputs) + k % STAGES]
        )

    for k in range(16):
        j, q = k // 4, k % 4
        if k >= STAGES:
            out_copy(k - STAGES).wait()
        cols = slice(q * TILE, (q + 1) * TILE)
        if j < 3:
            value = dot(act_one_t[cols], d_qkv[j])
        else:
            value = dot_tn(mixed[:, cols], grad_low[...])
        stage_grads[k % STAGES] = value.reshape(tall, 2, shard_rows, WIDE)
        out_copy(k).start()
        if k % 2 == 1:
            tick(1)
    for k in range(16 - STAGES, 16):
        out_copy(k).wait()
    for k in range(early_inputs, len(inputs)):
        bring(k, *inputs[k]).wait()
    for q in range(4):
        cols = slice(q * TILE, (q + 1) * TILE)
        spots = slice(q * tall, (q + 1) * tall)
        part[:, cols] += dot(mixed[...], weight(3, cols)) + rows_in[7:8, cols]
        value = dot_nt(d_qkv[0], weights[0, spots].reshape(TILE, WIDE))
        value += dot_nt(d_qkv[1], weights[1, spots].reshape(TILE, WIDE))
        value += dot_nt(d_qkv[2], weights[2, spots].reshape(TILE, WIDE))
        d_one[:, cols] = value
        tick(2)
    pltpu.make_async_copy(part, output, local.at[2]).start()
    for j in range(3):
        grad_vec[4 + j : 5 + j] = jnp.sum(d_qkv[j].astype(f32), axis=0, keepdims=True)

    def norm_back(i, sums):
        mine = pl.ds(pl.multiple_of(i * step, step), step)
        x = tokens[mine].astype(f32)
        centred = x - jnp.mean(x, axis=-1, keepdims=True)
        var = jnp.mean(centred * centred, axis=-1, keepdims=True)
        spread = lax.rsqrt(var + norm_eps)
        unit = centred * spread
        one, two = d_one[mine], d_two[mine]
        d_unit = one * rows_in[0:1] + two * rows_in[2:3]
        flat = jnp.mean(d_unit, axis=-1, keepdims=True)
        tilt = jnp.mean(d_unit * unit, axis=-1, keepdims=True)
        d_two[mine] = cot[mine] * valid[mine, 0:1] + spread * (d_unit - flat - unit * tilt)
        return tuple(
            s + jnp.sum(w, axis=0, keepdims=True) for s, w in zip(sums, (one * unit, one, two * unit, two))
        )

    sums = lax.fori_loop(0, count // step, norm_back, (jnp.zeros((1, WIDE), f32),) * 4)
    for k in range(4):
        grad_vec[k : k + 1] = sums[k]
    pltpu.make_async_copy(d_two, input_grad, local.at[3]).start()
    grad_vec[7:8] = vec_early[4:5]
    grad_vec[8:12] = vec_early[0:4]
    grad_vec[12:13] = vec_early[4:5]
    lane = vec_sum.shape[1]
    for row, start, device, place in vector_places(n_shard, lane):
        vec_part[device, place : place + 1, :] = grad_vec[row : row + 1, start : start + lane]
    for d in range(1, n_shard):
        to = lax.rem(at.shard + d, n_shard)
        copies.start(vec_slot + d, vec_part.at[to], vec_got.at[d], at.group(d))

    def vec_first():
        value = vec_part[at.shard]
        for d in range(1, n_shard):
            copies.arrived(vec_slot + d, vec_got.at[d], at.group(d))
            value = value + vec_got[d]
        vec_all[at.rep] = value
        for d in range(1, n_rep):
            copies.start(vec_slot_rep + d, vec_all.at[at.rep], vec_all.at[at.rep], at.replica(d))

    def vec_last():
        for d in range(1, n_rep):
            copies.arrived(vec_slot_rep + d, vec_all.at[lax.rem(at.rep + n_rep - d, n_rep)], at.replica(d))
        value = vec_all[0]
        for i in range(1, n_rep):
            value = value + vec_all[i]
        vec_sum[...] = value

    def result(u):
        return pltpu.make_async_copy(
            reduce_bufs[-1].at[u], sums_out.at[u], local.at[2 + len(inputs) + STAGES + u]
        )

    done = 0
    vec_jobs = [vec_first, vec_last]
    while queue or clock[0] < PIECES + reduce.depth - 1:
        tick(len(queue) or 1)
        flush()
        if vec_jobs and clock[0] >= 2 * EARLY + 4 * (2 - len(vec_jobs)):
            vec_jobs.pop(0)()
        while done < min(UNITS, (clock[0] - reduce.depth + 1) // 2):
            result(done).start()
            done += 1
    for u in range(UNITS):
        result(u).wait()
    reduce.drain()
    copies.drain()
    pltpu.make_async_copy(part, output, local.at[2]).wait()
    pltpu.make_async_copy(d_two, input_grad, local.at[3]).wait()


def attention(
    early, late, rows, act_one, grad_low, tokens, cot, valid, part, d_two, positions, tables, vec_early, lane,
    n_rep, n_shard,
):
    count = tokens.shape[0]
    unit = late.shape[1:]
    line, _, shard_rows, _ = unit
    bits, width, half = n_rep.bit_length() - 1, WIDE // n_rep, shard_rows // 2
    line_bits = line.bit_length() - 1
    slots = PIECES * (2 * bits + line_bits) + n_shard + n_rep
    anywhere = pl.BlockSpec(memory_space=pl.ANY)
    vmem = pl.BlockSpec(memory_space=pltpu.VMEM)
    flat = lambda: pltpu.VMEM((count, WIDE), bf16)
    outs = pl.pallas_call(
        functools.partial(attention_kernel, n_rep, n_shard),
        out_shape=(
            jax.ShapeDtypeStruct((count, WIDE), f32),
            jax.ShapeDtypeStruct((count, WIDE), f32),
            jax.ShapeDtypeStruct((UNITS, shard_rows, WIDE), f32),
            jax.ShapeDtypeStruct((16, lane), f32),
            jax.ShapeDtypeStruct((4,) + unit, f32),
            jax.ShapeDtypeStruct((PIECES, line, half, WIDE), f32),
        ),
        in_specs=[anywhere, anywhere, vmem] + [anywhere] * 7 + [vmem] + [anywhere] * 3 + [vmem],
        out_specs=(anywhere, anywhere, anywhere, vmem, anywhere, anywhere),
        scratch_shapes=[
            flat(), flat(), flat(),
            pltpu.VMEM((count, WIDE), f32),
            *(pltpu.VMEM((count, LANES), f32) for _ in range(4)),
            pltpu.VMEM((4,) + unit, bf16),
            pltpu.VMEM((count, WIDE), f32),
            pltpu.VMEM((count, WIDE), f32),
            flat(), flat(), flat(), flat(), flat(),
            pltpu.VMEM((3, count, WIDE), bf16),
            pltpu.VMEM((WIDE, count), bf16),
            pltpu.VMEM((count, count), f32),
            pltpu.VMEM((count, WIDE), f32),
            pltpu.VMEM((STAGES, TILE // (2 * shard_rows)) + unit[1:], f32),
            pltpu.VMEM((16, WIDE), f32),
            pltpu.VMEM((n_shard, 16, lane), f32),
            pltpu.VMEM((n_shard, 16, lane), f32),
            pltpu.VMEM((n_rep, 16, lane), f32),
            [
                pltpu.VMEM((line, half, WIDE), f32),
                pltpu.VMEM((line, half, WIDE), f32),
                [pltpu.VMEM((RING, line, half, width << p), f32) for p in range(1, bits)],
                [pltpu.VMEM((RING, line, half, width << p), bf16) for p in range(1, bits)],
                [pltpu.VMEM((RING, line, half, width << p), bf16) for p in range(1, bits)],
                [pltpu.VMEM((RING, line >> (q + 1), half, 2 * width), f32) for q in range(line_bits)],
                [[pltpu.VMEM((RING, line >> (q + 1), half, 2 * width), bf16)] * 2 for q in range(line_bits)],
                [[pltpu.VMEM((RING, line >> (q + 1), half, 2 * width), f32)] * 2 for q in range(1, line_bits)],
                pltpu.VMEM((RING, half, 2 * width), f32),
                pltpu.VMEM((RING, half, 2 * width), f32),
                pltpu.VMEM((UNITS, shard_rows, WIDE), f32),
            ],
            pltpu.SemaphoreType.DMA((slots,)),
            pltpu.SemaphoreType.DMA((slots,)),
            pltpu.SemaphoreType.DMA((2 + 14 + STAGES + UNITS,)),
        ],
        compiler_params=pltpu.CompilerParams(
            collective_id=1, has_side_effects=True, vmem_limit_bytes=62 * 2**20
        ),
        name="attention_and_sums",
    )(
        early, late, rows, act_one, grad_low, tokens, cot, valid, part, d_two, positions, *tables, vec_early
    )
    return outs[:4]


class Adam:
    def __init__(self, n_shard, states, results, ins, outs, total, sums, sems):
        self.states, self.results, self.ins, self.outs, self.total, self.sems = states, results, ins, outs, total, sems
        self.sums = sums
        self.rows = total.shape[1]
        lane = FF // n_shard // 4
        self.blocks = []
        share = n_shard // 4
        for k in range(4):
            runs = []
            for s in range(k * share, (k + 1) * share):
                for j in range(4):
                    runs.append((2 * j, s * lane, ((s - k * share) * 4 + j) * lane, lane))
            self.blocks.append((2, slice(0, self.rows), slice(k * WIDE, (k + 1) * WIDE), runs, 0.5 * D ** (-0.5)))
        for j in range(4):
            rows = slice(j * self.rows, (j + 1) * self.rows)
            self.blocks.append((3, rows, slice(0, WIDE), [(2 * j + 1, 0, 0, WIDE)], 0.5 * FF ** (-0.5)))
        for j in range(3):
            cols = slice(j * WIDE, (j + 1) * WIDE)
            runs = [(8 + j, 0, 0, WIDE)]
            self.blocks.append((0, slice(0, self.rows), cols, runs, 0.5 * D ** (-0.5)))
        runs = [(11, 0, 0, WIDE)]
        self.blocks.append((1, slice(0, self.rows), slice(0, WIDE), runs, 0.5 * (32.0 / D) ** 0.5))

    def load(self, i, k):
        kind, rows, cols = self.blocks[i][:3]
        return pltpu.make_async_copy(self.states[kind][k].at[rows, cols], self.ins.at[i % SLOTS, k], self.sems.at[0, i % SLOTS, k])

    def store(self, i, k):
        kind, rows, cols = self.blocks[i][:3]
        return pltpu.make_async_copy(self.outs.at[i % SLOTS, k], self.results[kind][k].at[rows, cols], self.sems.at[1, i % SLOTS, k])

    def grad(self, unit):
        return pltpu.make_async_copy(self.sums.at[unit], self.total.at[unit], self.sems.at[2, 0, unit])

    def begin(self, i):
        for k in range(3):
            self.load(i, k).start()

    def work(self, i):
        runs, rate = self.blocks[i][3:5]
        ring = i % SLOTS
        if i == 0:
            for unit in (0, 2, 4, 6):
                self.grad(unit).wait()
        elif i >= 4:
            self.grad(runs[0][0]).wait()
        for k in range(3):
            self.load(i, k).wait()
            if i >= SLOTS:
                self.store(i - SLOTS, k).wait()
        step = 16

        def body(r, _):
            rows = pl.ds(pl.multiple_of(r * step, step), step)
            for unit, start, to, count in runs:
                cols = slice(to, to + count)
                grad = self.total[unit, rows, start : start + count]
                new = adam(
                    self.ins[ring, 0, rows, cols], self.ins[ring, 1, rows, cols], self.ins[ring, 2, rows, cols],
                    grad, rate, weight_decay,
                )
                for k in range(3):
                    self.outs[ring, k, rows, cols] = new[k]
            return 0

        lax.fori_loop(0, self.rows // step, body, 0)
        for k in range(3):
            self.store(i, k).start()
        if i + SLOTS < len(self.blocks):
            self.begin(i + SLOTS)

    def drain(self):
        for i in range(len(self.blocks) - SLOTS, len(self.blocks)):
            for k in range(3):
                self.store(i, k).wait()


def finish_kernel(
    n_shard, sums, vec_sum, vec_state, out_done, in_done, qkv_state, out_state, fc1_state, fc2_state,
    output, input_grad, vec_new, qkv_new, out_new, fc1_new, fc2_new, ins, outs, total, passing, sems, whole,
):
    pairs = ((out_done, output), (in_done, input_grad))
    arrive = [pltpu.make_async_copy(src, passing.at[k], whole.at[k]) for k, (src, _) in enumerate(pairs)]
    leave = [pltpu.make_async_copy(passing.at[k], dst, whole.at[k]) for k, (_, dst) in enumerate(pairs)]
    optimizer = Adam(
        n_shard, (qkv_state, out_state, fc1_state, fc2_state), (qkv_new, out_new, fc1_new, fc2_new),
        ins, outs, total, sums, sems,
    )
    for unit in (0, 2, 4, 6):
        optimizer.grad(unit).start()
    for i in range(SLOTS):
        optimizer.begin(i)
    for unit in (1, 3, 5, 7, 8, 9, 10, 11):
        optimizer.grad(unit).start()
    for copy in arrive:
        copy.start()
    new = adam(vec_state[0][...], vec_state[1][...], vec_state[2][...], vec_sum[0:VEC_ROWS], vector_rate, 0.0)
    for k in range(3):
        vec_new[k][...] = new[k]
    for i in range(len(optimizer.blocks)):
        optimizer.work(i)
        if i == 3:
            for k in range(2):
                arrive[k].wait()
                leave[k].start()
    optimizer.drain()
    for copy in leave:
        copy.wait()


def finish(sums, vec_sum, vec_state, output, input_grad, states, n_shard):
    anywhere = pl.BlockSpec(memory_space=pl.ANY)
    vmem = pl.BlockSpec(memory_space=pltpu.VMEM)
    rows = sums.shape[1]
    like = lambda a: jax.ShapeDtypeStruct(a.shape, f32)
    return pl.pallas_call(
        functools.partial(finish_kernel, n_shard),
        out_shape=(
            like(output), like(input_grad), (like(vec_state[0]),) * 3, *((like(group[0]),) * 3 for group in states)
        ),
        in_specs=[anywhere, vmem, (vmem,) * 3, anywhere, anywhere] + [(anywhere,) * 3] * 4,
        out_specs=(anywhere, anywhere, (vmem,) * 3) + ((anywhere,) * 3,) * 4,
        scratch_shapes=[
            pltpu.VMEM((SLOTS, 3, rows, WIDE), f32),
            pltpu.VMEM((SLOTS, 3, rows, WIDE), f32),
            pltpu.VMEM(sums.shape, f32),
            pltpu.VMEM((2,) + output.shape, f32),
            pltpu.SemaphoreType.DMA((3, SLOTS, UNITS)),
            pltpu.SemaphoreType.DMA((2,)),
        ],
        compiler_params=pltpu.CompilerParams(vmem_limit_bytes=62 * 2**20),
        name="update",
    )(sums, vec_sum, vec_state, output, input_grad, *states)


def adam(master, first, second, grad, rate, decay_on):
    first_new = beta_one * first + (1.0 - beta_one) * grad
    second_new = beta_two * second + (1.0 - beta_two) * grad * grad
    mhat = first_new / (1.0 - beta_one**STEP)
    vhat = second_new / (1.0 - beta_two**STEP)
    new = master - rate * (mhat / (jnp.sqrt(vhat) + epsilon) + decay_on * master)
    return (first_new, second_new, new)


def shards(
    tokens,
    cotangent,
    positions,
    qkv_master,
    qkv_first,
    qkv_second,
    out_master,
    out_first,
    out_second,
    fc1_master,
    fc1_first,
    fc1_second,
    fc2_master,
    fc2_first,
    fc2_second,
    vec_master,
    vec_first,
    vec_second,
):
    n_rep, n_shard = lax.axis_size("rep"), lax.axis_size("shard")
    vec_state = tuple(w.reshape(VEC_ROWS, -1) for w in (vec_master, vec_first, vec_second))
    late, early_grads, rows, part, d_two, act_one, grad_low, vec_early, valid, *tables = mlp(
        (qkv_master, out_master, fc1_master, fc2_master), vec_state[0], tokens, cotangent, positions[None],
        n_rep, n_shard,
    )
    states = (
        (qkv_master, qkv_first, qkv_second),
        (out_master, out_first, out_second),
        (fc1_master, fc1_first, fc1_second),
        (fc2_master, fc2_first, fc2_second),
    )
    output, input_grad, sums, vec_sum = attention(
        early_grads, late, rows, act_one, grad_low, tokens, cotangent, valid, part, d_two, positions[None],
        tables, vec_early, vec_state[0].shape[1], n_rep, n_shard,
    )
    output, input_grad, vec_new, *news = finish(sums, vec_sum, vec_state, output, input_grad, states, n_shard)
    vec_new = (w.reshape(-1) for w in vec_new)
    return (output, input_grad, *(w for new in news for w in new), *vec_new)


def solution(mesh):
    rows, owned, slots = P(("rep", "shard"), None), P("shard", None), P(("rep", "shard"))
    vector = P("shard")
    return jax.shard_map(
        shards,
        mesh=mesh,
        in_specs=(rows, rows, slots) + (owned,) * 12 + (vector,) * 3,
        out_specs=(rows, rows) + (owned,) * 12 + (vector,) * 3,
        check_vma=False,
    )
```
